256 devices in a mesh: dp: 8 (over y, z_hi), expert: 32 (over x, z_lo, core).
Axes of the slice: x: 4, y: 4, z: 8 (z_hi: 2, z_lo: 4; z = z_hi * 4 + z_lo), core: 2. Of those that a mesh axis runs over, the one named last changes fastest.
Arguments:
- tokens: bfloat16 [32768, 2560], P(('dp', 'expert')), may hold values from -6 to 6
- expert_ids: int32 [32768, 6], P(('dp', 'expert')), may hold values from 0 to 31, all different within a row; in each aligned block of 128 rows (0 to 127, 128 to 255, ...) at most 28 rows name the same one
- route_weight: float32 [32768, 6], P(('dp', 'expert')), may hold values from 0.03 to 0.5
- placement: int32 [32], replicated, may hold values from 0 to 31, each once
- swap_mask: int32 [1], replicated, may hold values from 1 to 15
- gate_weight: bfloat16 [32, 2560, 768], P('expert'), may hold values from -0.125 to 0.125
- up_weight: bfloat16 [32, 2560, 768], P('expert'), may hold values from -0.125 to 0.125
- down_weight: bfloat16 [32, 768, 2560], P('expert', 'dp'), may hold values from -0.21875 to 0.21875
- first_moment: bfloat16 [32, 768, 2560], P('expert', 'dp'), may hold values from -6 to 6
- second_moment: bfloat16 [32, 768, 2560], P('expert', 'dp'), may hold values from 1 to 30
- out_grad: bfloat16 [32768, 2560], P(('dp', 'expert')), may hold values from -6 to 6
Outputs:
- layer_out: bfloat16 [32768, 2560], P(('dp', 'expert'))
- new_down: bfloat16 [32, 768, 2560], P('expert', 'dp')
- new_first: bfloat16 [32, 768, 2560], P('expert', 'dp')
- new_second: bfloat16 [32, 768, 2560], P('expert', 'dp')
The draws below stay inside these ranges and needn't reach their ends.
Inputs may be any that keep to these rules, and one draw needn't show every extreme that they name: `expert_ids`: each row names 6 different experts; among the rows of one device no expert is named more than 28 times, and in every draw some expert is named exactly 28 times by the rows of some device. `placement`: each expert appears once.
All inputs are finite; a program needn't handle non-finite values.
Results may differ from the reference program's by a relative error of at most 0.025.
Values may be sent and summed in bfloat16 or wider, within the bound.
No kernel may reach another device: no remote copies, remote signals or barrier semaphores. Data moves between devices by JAX's collectives and lax.ppermute only.
A program may use at most 128 MiB of HBM per device.

```python
import math
import jax
import jax.numpy as jnp
import numpy as np
from jax import lax

D = 2560
FFN = 768
TOP = 6
SWAP_BITS = 4
TOK_DEV = 128
EXPERTS = 32
CAP = 28
TOKEN_TOTAL = 32768
N_DP = 8
N_EXPERT = 32


def level_of(key, extent, pieces, least, largest):
    loudness, own = 1.0, jax.random.fold_in(key, 6)
    for dim, parts in pieces:
        draws = jnp.exp(jax.random.uniform(jax.random.fold_in(own, dim), (parts,), jnp.float32, least / len(pieces), largest / len(pieces)))
        loudness = loudness * jnp.repeat(draws, extent[dim] // parts).reshape([-1 if axis == dim else 1 for axis in range(len(extent))])
    return loudness


def assign_block(rng, own, number, rows, number_of, top, most, lean):
    ranking = jax.random.permutation(rng, number_of)
    crowded, common = load_shares(number_of, rows * top, most, lean, True), load_shares(number_of, rows * top, most, lean, False)
    places = jnp.arange(number_of)

    def named(tallies, turn):
        used = int((tallies > 0).sum())
        fixed = max(1, used // 4)
        passed = fixed + (places - fixed + turn * (used - fixed)) % max(1, number_of - fixed)
        return jnp.zeros((number_of,), jnp.int32).at[ranking[jnp.where(places < fixed, places, passed)]].set(jnp.asarray(tallies, jnp.int32))

    tallies = jnp.where(number % 4 == 0, named(crowded, number // 4), named(common, number - number // 4 - 1))
    mixed = jax.random.permutation(jax.random.fold_in(own, 3), number_of)
    giver, sink = mixed[0:number_of // 2 * 2:2], mixed[1:number_of // 2 * 2:2]
    slack = jnp.minimum(tallies[giver] - 1, most - tallies[sink]) // 2
    slack = jnp.where((giver == ranking[0]) | (sink == ranking[0]) | (tallies[sink] == 0), 0, jnp.maximum(slack, 0))
    passed = jax.random.randint(jax.random.fold_in(own, 4), (number_of // 2,), 0, 1 << 20) % (slack + 1)
    tallies = tallies.at[giver].add(-passed).at[sink].add(passed)
    members = jnp.searchsorted(jnp.cumsum(tallies), jnp.arange(rows * top), side="right").astype(jnp.int32)
    table = members.reshape(top, rows).T
    table = table[jax.random.permutation(jax.random.fold_in(own, 1), rows)]
    turn = jax.random.randint(jax.random.fold_in(own, 2), (rows, 1), 0, top)
    return jnp.take_along_axis(table, (jnp.arange(top)[None, :] + turn) % top, axis=1)


def load_shares(number_of, total, most, skew, full):
    loads = [(1 << 20) // math.isqrt(standing ** skew) + 1 for standing in range(1, number_of + 1)]
    largest = most if full else min(most, max(-(-total // number_of), total * loads[0] // sum(loads)))
    least = 1 if total - largest >= number_of - 1 else 0
    counts, surplus = [largest] + [least] * (number_of - 1), total - largest - least * (number_of - 1)
    while surplus > 0:
        candidates = [i for i in range(1, number_of) if counts[i] < largest] or [i for i in range(1, number_of) if counts[i] < most]
        pool, budget = sum([loads[i] for i in candidates]), surplus
        for i in candidates:
            addition = min(most - counts[i], max(1, budget * loads[i] // pool), surplus)
            counts[i] = counts[i] + addition
            surplus = surplus - addition
    return np.array(counts)


def noise(own_key, shape, deviation, bound, split=(), held_as=jnp.bfloat16):
    result = jax.random.normal(own_key, shape, jnp.float32) * deviation
    if len(split) > 0:
        result = level_of(own_key, shape, split, -0.22, 0.18) * result
    return jnp.clip(result, min=-bound, max=bound).astype(held_as)


def setup_inputs(seed: int = 0) -> dict:
    splits = jax.random.split(jax.random.key(seed), 12)
    tokens = noise(splits[0], (TOKEN_TOTAL, D), 1.0, 6.0, ((0, 256),))
    expert_ids_keys = jax.random.split(jax.random.fold_in(splits[1], 1), TOKEN_TOTAL // TOK_DEV)
    expert_ids_turns = jax.random.permutation(jax.random.fold_in(splits[1], 3), TOKEN_TOTAL // TOK_DEV)
    expert_ids = jax.vmap(lambda own, number: assign_block(jax.random.fold_in(splits[1], 2), own, number, TOK_DEV, EXPERTS, TOP, CAP, 1))(expert_ids_keys, expert_ids_turns).reshape((TOKEN_TOTAL, TOP))
    route_weight = jnp.clip(jnp.exp(math.log(0.5) - 2.8134107 * jax.random.uniform(splits[2], (TOKEN_TOTAL, TOP), jnp.float32) ** level_of(splits[2], (TOKEN_TOTAL, TOP), ((0, 256),), -0.2, 0.2)), 0.03, 0.5)
    placement = jax.random.permutation(splits[3], EXPERTS).astype(jnp.int32)
    swap_mask = jax.random.randint(splits[4], (1,), 1, 2 ** SWAP_BITS).astype(jnp.int32)
    gate_weight = noise(splits[5], (EXPERTS, D, FFN), D ** -0.5, 0.125, ((0, 32),))
    up_weight = noise(splits[6], (EXPERTS, D, FFN), D ** -0.5, 0.125, ((0, 32),))
    down_weight = noise(splits[7], (EXPERTS, FFN, D), FFN ** -0.5, 0.21875, ((0, 32), (1, 8)))
    first_moment = noise(splits[8], (EXPERTS, FFN, D), 1.0, 6.0, ((0, 32), (1, 8)))
    second_moment = jnp.clip(jnp.exp(math.log(30.0) - 3.4011974 * jax.random.uniform(splits[9], (EXPERTS, FFN, D), jnp.float32) ** level_of(splits[9], (EXPERTS, FFN, D), ((0, 32), (1, 8)), -0.2, 0.2)), 1.0, 30.0).astype(jnp.bfloat16)
    out_grad = noise(splits[10], (TOKEN_TOTAL, D), 1.0, 6.0, ((0, 256),))
    return {"tokens": tokens, "expert_ids": expert_ids, "route_weight": route_weight, "placement": placement, "swap_mask": swap_mask, "gate_weight": gate_weight, "up_weight": up_weight, "down_weight": down_weight, "first_moment": first_moment, "second_moment": second_moment, "out_grad": out_grad}


first_decay_rate = 0.9
beta_two = 0.95
learn_rate = 0.003
adam_eps = 1e-08

def reference(tokens, expert_ids, route_weight, placement, swap_mask, gate_weight, up_weight, down_weight, first_moment, second_moment, out_grad):
    devices_all = N_DP * N_EXPERT
    dest_slot = placement[expert_ids]
    dest_flat = dest_slot.reshape(devices_all, TOK_DEV * TOP)
    onehot = (dest_flat[:, :, None] == jnp.arange(N_EXPERT, dtype=jnp.int32)[None, None, :]).astype(jnp.int32)
    before = jnp.cumsum(onehot, axis=1) - onehot
    rank_in = lax.optimization_barrier(jnp.sum(before * onehot, axis=2))
    slot_pos = (dest_flat * CAP + rank_in).astype(jnp.int32)
    device_rows = jnp.arange(devices_all, dtype=jnp.int32)[:, None]
    owner_row = device_rows * TOK_DEV + jnp.arange(TOK_DEV * TOP, dtype=jnp.int32)[None, :] // TOP
    row_table = jnp.full((devices_all, N_EXPERT * CAP), TOKEN_TOTAL, jnp.int32).at[device_rows, slot_pos].set(owner_row)
    weight_table = jnp.zeros((devices_all, N_EXPERT * CAP), jnp.float32).at[device_rows, slot_pos].set(route_weight.reshape(devices_all, TOK_DEV * TOP))
    row_table = row_table.reshape(N_DP, N_EXPERT, N_EXPERT, CAP)
    weight_table = weight_table.reshape(N_DP, N_EXPERT, N_EXPERT, CAP)
    empty_row_filler = jnp.zeros((1, D), tokens.dtype)
    padded_x = jnp.concatenate([tokens, empty_row_filler], axis=0)
    padded_dy = jnp.concatenate([out_grad, empty_row_filler], axis=0)

    def per_slot(y_acc, slot_index):
        rows_idx = lax.dynamic_index_in_dim(row_table, slot_index, 2, keepdims=False).reshape(N_DP, N_EXPERT * CAP)
        weights_in = lax.dynamic_index_in_dim(weight_table, slot_index, 2, keepdims=False).reshape(N_DP, N_EXPERT * CAP)
        token_rows = padded_x[rows_idx].astype(jnp.float32)
        gate_mat = gate_weight[slot_index].astype(jnp.float32)
        up_projection_weight = up_weight[slot_index].astype(jnp.float32)
        down_mat = down_weight[slot_index].astype(jnp.float32)
        gate_act = jnp.einsum('prc,cf->prf', token_rows, gate_mat)
        up_act = jnp.einsum('prc,cf->prf', token_rows, up_projection_weight)
        hidden_state = (jax.nn.silu(gate_act) * up_act).astype(jnp.bfloat16)
        expert_rows = jnp.einsum('prf,fc->prc', hidden_state.astype(jnp.float32), down_mat).astype(jnp.bfloat16)
        contrib = weights_in[:, :, None] * expert_rows.astype(jnp.float32)
        y_acc = y_acc.at[rows_idx.reshape(-1)].add(contrib.reshape(-1, D))
        gradient_weighted = (weights_in[:, :, None] * padded_dy[rows_idx].astype(jnp.float32)).astype(jnp.bfloat16)
        value_portion = jnp.einsum('mjt,mjy->mty', hidden_state.astype(jnp.float32), gradient_weighted.astype(jnp.float32))
        grad = lax.optimization_barrier(jnp.sum(value_portion.astype(jnp.bfloat16).astype(jnp.float32), axis=0))
        weight_old = down_weight[slot_index].astype(jnp.float32)
        moment_one = first_decay_rate * first_moment[slot_index].astype(jnp.float32) + (1.0 - first_decay_rate) * grad
        moment_two = beta_two * second_moment[slot_index].astype(jnp.float32) + (1.0 - beta_two) * grad * grad
        updated = weight_old - learn_rate * moment_one / (jnp.sqrt(moment_two) + adam_eps)
        return (y_acc, (updated.astype(jnp.bfloat16), moment_one.astype(jnp.bfloat16), moment_two.astype(jnp.bfloat16)))
    y_start = jnp.zeros((TOKEN_TOTAL + 1, D), jnp.float32)
    y_acc, (updated_all, first_all, second_all) = lax.scan(per_slot, y_start, jnp.arange(N_EXPERT, dtype=jnp.int32))
    layer_out = y_acc[:TOKEN_TOTAL].astype(jnp.bfloat16)
    source_index = jnp.bitwise_xor(jnp.arange(N_EXPERT, dtype=jnp.int32), swap_mask[0])
    return (layer_out, updated_all[source_index], first_all[source_index], second_all[source_index])
```

```python
import jax
import jax.numpy as jnp
from jax import lax
from jax.experimental import pallas as pl
from jax.experimental.pallas import tpu as pltpu
from jax.sharding import Mesh, PartitionSpec as P

SWAP_BITS = 4
N_Y, N_ZH, N_X, N_ZL, N_C = 4, 2, 4, 4, 2
AXES = ("y", "zh", "x", "zl", "c")
MIB = 1024 * 1024

first_decay_rate = 0.9
beta_two = 0.95
learn_rate = 0.003
adam_eps = 1e-08

X_CHUNKS = 1
G_CHUNKS = 2
R_CHUNKS = 2


def flat_index(y, z, x, c):
    z = z % 8
    return ((((y % 4) * N_ZH + z // N_ZL) * N_X + x % 4) * N_ZL + z % N_ZL) * N_C + c % 2


def permute(array, move):
    pairs = []
    for y in range(N_Y):
        for z in range(8):
            for x in range(N_X):
                for c in range(N_C):
                    pairs.append((flat_index(y, z, x, c), flat_index(*move(y, z, x, c))))
    return lax.ppermute(array, AXES, pairs)


def along(c):
    return 1 if c == 0 else -1


def z_up(array):
    return permute(array, lambda y, z, x, c: (y, z + along(c), x, c))


def z_down(array):
    return permute(array, lambda y, z, x, c: (y, z - along(c), x, c))


def z_gather(array):
    near = z_up(array)
    other = z_down(array)
    far = z_up(near)
    return array, near, other, far


def relocate(array, mask, flip_zh=False):
    def move(y, z, x, c):
        zl = (z % 4) ^ (mask >> 1 & 3)
        zh = z // 4 ^ (1 if flip_zh else 0)
        return y, zh * 4 + zl, x ^ (mask >> 3), c ^ (mask & 1)

    return permute(array, move)


def params(mib, *semantics):
    return pltpu.CompilerParams(
        dimension_semantics=semantics or None, vmem_limit_bytes=mib * MIB
    )


def plan_kernel(cap, top, ids_here, m0, m1, m2, m3, slot_ref, weight_ref):
    rows = m0.shape[1]
    before = lax.broadcasted_iota(jnp.int32, (rows, rows), 0)
    after = lax.broadcasted_iota(jnp.int32, (rows, rows), 1)
    earlier = (before < after).astype(jnp.float32).astype(jnp.bfloat16)
    wanted = ids_here[...]
    for s, meta in enumerate((m0, m1, m2, m3)):
        named = jnp.zeros(wanted.shape, jnp.float32)
        weight = jnp.zeros(wanted.shape, jnp.float32)
        for k in range(top):
            same = (meta[k : k + 1, :] == wanted).astype(jnp.float32)
            named = named + same
            weight = weight + same * meta[8 + k : 9 + k, :]
        rank = jnp.dot(named.astype(jnp.bfloat16), earlier, preferred_element_type=jnp.float32)
        slot = jnp.where(named > 0.5, rank + float(s * cap), -1.0)
        slot_ref[:, s * rows : (s + 1) * rows] = slot
        weight_ref[:, s * rows : (s + 1) * rows] = weight


def make_plan(cap, top, ids_here, metas):
    rows = metas[0].shape[1]
    out = jax.ShapeDtypeStruct((8, 4 * rows), jnp.float32)
    return pl.pallas_call(
        lambda *refs: plan_kernel(cap, top, *refs),
        out_shape=(out, out),
        compiler_params=params(16),
        name="plan",
    )(ids_here, *metas)


def select_kernel(scaled, slots, weights, t0, t1, t2, t3, out, pick, scale):
    dests, block, width = out.shape
    tokens = slots.shape[1]

    @pl.when(pl.program_id(0) == 0)
    def _():
        place = lax.broadcasted_iota(jnp.int32, (block, tokens), 0).astype(jnp.float32)
        for d in range(dests):
            hit = (slots[d : d + 1, :] == place).astype(jnp.float32)
            pick[d * block : (d + 1) * block, :] = hit.astype(jnp.bfloat16)
            if scaled:
                row = jnp.sum(hit * weights[d : d + 1, :], axis=1, keepdims=True)
                scale[d * block : (d + 1) * block, :] = jnp.broadcast_to(row, (block, 128))

    source = jnp.concatenate([t0[...], t1[...], t2[...], t3[...]], axis=0)
    rows = jnp.dot(pick[...], source, preferred_element_type=jnp.float32)
    if scaled:
        rows = rows * scale[:, 0:1]
    out[...] = rows.astype(jnp.bfloat16).reshape(dests, block, width)


def select_rows(scaled, cap, plan, parts, first, width):
    slots, weights = plan
    rows = parts[0].shape[0]
    block = 4 * cap
    tile = 256 if width % 512 else 512
    offset = first // tile
    whole = pl.BlockSpec(slots.shape, lambda j: (0, 0))
    return pl.pallas_call(
        lambda *refs: select_kernel(scaled, *refs),
        grid=(width // tile,),
        in_specs=[whole, whole]
        + [pl.BlockSpec((rows, tile), lambda j: (0, j + offset)) for _ in range(4)],
        out_specs=pl.BlockSpec((8, block, tile), lambda j: (0, 0, j)),
        out_shape=jax.ShapeDtypeStruct((8, block, width), jnp.bfloat16),
        scratch_shapes=[
            pltpu.VMEM((8 * block, 4 * rows), jnp.bfloat16),
            pltpu.VMEM((8 * block, 128), jnp.float32),
        ],
        compiler_params=params(40, "arbitrary"),
        name="select_scaled" if scaled else "select",
    )(slots, weights, *parts)


def hidden_kernel(count, where, *refs):
    xs, (gate_w, up_w, out, held) = refs[:count], refs[count:]
    step, tile = pl.program_id(0), gate_w.shape[1]
    steps, features = held.shape[0], out.shape[1]
    gate, up, first = None, None, 0
    for x in xs:
        rows = x[...].reshape(-1, x.shape[2])
        part = slice(first, first + x.shape[2])
        first += x.shape[2]
        g = jnp.dot(rows, gate_w[part, :], preferred_element_type=jnp.float32)
        u = jnp.dot(rows, up_w[part, :], preferred_element_type=jnp.float32)
        gate, up = (g, u) if gate is None else (gate + g, up + u)
    held[step] = (gate / (1.0 + jnp.exp(-gate)) * up).astype(jnp.bfloat16)

    @pl.when(step == steps - 1)
    def _():
        shard = features // (N_Y * N_ZH)
        column = lax.broadcasted_iota(jnp.int32, (tile, features), 1)
        row = lax.broadcasted_iota(jnp.int32, (tile, features), 0)
        number = column // shard
        y = (where[0] + number // 2) % N_Y
        zh = (where[1] + number % 2) % N_ZH
        origin = (y * N_ZH + zh) * shard + (column - number * shard)
        total = None
        for s in range(steps):
            move = (row + s * tile == origin).astype(jnp.float32).astype(jnp.bfloat16)
            part = jnp.dot(held[s], move, preferred_element_type=jnp.float32)
            total = part if total is None else total + part
        out[...] = total.astype(jnp.bfloat16)


def hidden_rows(where, xs, gate_weight, up_weight):
    depth, features = gate_weight.shape
    count = xs[0].shape[0] * xs[0].shape[1]
    tile = 256
    steps = features // tile
    return pl.pallas_call(
        lambda *refs: hidden_kernel(len(xs), *refs),
        grid=(steps,),
        in_specs=[pl.BlockSpec(memory_space=pltpu.SMEM)]
        + [pl.BlockSpec(x.shape, lambda j: (0, 0, 0)) for x in xs]
        + [pl.BlockSpec((depth, tile), lambda j: (0, j)) for _ in range(2)],
        out_specs=pl.BlockSpec((count, features), lambda j: (0, 0)),
        out_shape=jax.ShapeDtypeStruct((count, features), jnp.bfloat16),
        scratch_shapes=[pltpu.VMEM((steps, count, tile), jnp.bfloat16)],
        compiler_params=params(52, "arbitrary"),
        name="hidden",
    )(where, *xs, gate_weight, up_weight)


def down_kernel(hidden, d0, d1, d2, d3, d4, out):
    weight = jnp.concatenate([d0[...], d1[...], d2[...], d3[...], d4[...]], axis=0)
    rows = jnp.dot(hidden[...], weight, preferred_element_type=jnp.float32)
    out[...] = rows.astype(jnp.bfloat16).reshape(out.shape)


def down_rows(hidden, downs, cap, first, width):
    tile = 256 if width % 512 else 512
    offset = first // tile
    block = 4 * cap
    return pl.pallas_call(
        down_kernel,
        grid=(width // tile,),
        in_specs=[pl.BlockSpec(hidden.shape, lambda j: (0, 0))]
        + [pl.BlockSpec((d.shape[0], tile), lambda j: (0, j + offset)) for d in downs],
        out_specs=pl.BlockSpec((8, block, tile), lambda j: (0, 0, j)),
        out_shape=jax.ShapeDtypeStruct((8, block, width), jnp.bfloat16),
        compiler_params=params(40, "arbitrary"),
        name="down",
    )(hidden, *downs)


def grad_kernel(hidden, rows, o0, o1, o2, o3, turned):
    @pl.when(pl.program_id(0) == 0)
    def _():
        turned[...] = hidden[...].T

    value = rows[...].reshape(-1, rows.shape[2])
    grad = jnp.dot(turned[...], value, preferred_element_type=jnp.float32).astype(jnp.bfloat16)
    quarter = o0.shape[0]
    for k, out in enumerate((o0, o1, o2, o3)):
        out[...] = grad[k * quarter : (k + 1) * quarter, :]


def grad_blocks(hidden, rows):
    width = rows.shape[2]
    tile = 256 if width % 512 else 512
    quarter = hidden.shape[1] // N_Y
    spec = pl.BlockSpec((quarter, tile), lambda j: (0, j))
    out = jax.ShapeDtypeStruct((quarter, width), jnp.bfloat16)
    return pl.pallas_call(
        grad_kernel,
        grid=(width // tile,),
        in_specs=[
            pl.BlockSpec(hidden.shape, lambda j: (0, 0)),
            pl.BlockSpec((*rows.shape[:2], tile), lambda j: (0, 0, j)),
        ],
        out_specs=(spec,) * 4,
        out_shape=(out,) * 4,
        scratch_shapes=[pltpu.VMEM(hidden.shape[::-1], jnp.bfloat16)],
        compiler_params=params(40, "arbitrary"),
        name="grad",
    )(hidden, rows)


def combine_kernel(slots, weights, rows, o0, o1, o2, o3, high, low):
    dests, block, width = rows.shape
    tokens = slots.shape[1]

    @pl.when(pl.program_id(0) == 0)
    def _():
        place = lax.broadcasted_iota(jnp.int32, (block, tokens), 0).astype(jnp.float32)
        picked = []
        for d in range(dests):
            hit = (slots[d : d + 1, :] == place).astype(jnp.float32)
            picked.append(hit * weights[d : d + 1, :])
        pick = jnp.concatenate(picked, axis=0).T
        coarse = pick.astype(jnp.bfloat16)
        high[...] = coarse
        low[...] = (pick - coarse.astype(jnp.float32)).astype(jnp.bfloat16)

    value = rows[...].reshape(-1, width)
    total = jnp.dot(high[...], value, preferred_element_type=jnp.float32)
    total = total + jnp.dot(low[...], value, preferred_element_type=jnp.float32)
    count = o0.shape[0]
    for s, out in enumerate((o0, o1, o2, o3)):
        out[...] = total[s * count : (s + 1) * count, :].astype(out.dtype)


def combine_rows(plan, rows):
    slots, weights = plan
    width = rows.shape[2]
    tile = 256 if width % 512 else 512
    count = slots.shape[1] // 4
    whole = pl.BlockSpec(slots.shape, lambda j: (0, 0))
    spec = pl.BlockSpec((count, tile), lambda j: (0, j))
    return pl.pallas_call(
        combine_kernel,
        grid=(width // tile,),
        in_specs=[whole, whole, pl.BlockSpec((*rows.shape[:2], tile), lambda j: (0, 0, j))],
        out_specs=(spec,) * 4,
        out_shape=tuple(
            jax.ShapeDtypeStruct((count, width), t)
            for t in (jnp.float32, jnp.bfloat16, jnp.bfloat16, jnp.bfloat16)
        ),
        scratch_shapes=[
            pltpu.VMEM((slots.shape[1], rows.shape[0] * rows.shape[1]), jnp.bfloat16)
            for _ in range(2)
        ],
        compiler_params=params(40, "arbitrary"),
        name="combine",
    )(slots, weights, rows)


def plane_exchange(rows):
    return lax.all_to_all(rows, ("x", "c"), split_axis=0, concat_axis=0, tiled=True)


def z_return(own, near, other, far):
    step = z_down(far).astype(jnp.float32) + near.astype(jnp.float32)
    from_near = z_down(step.astype(jnp.bfloat16))
    from_other = z_up(other)
    total = own + from_near.astype(jnp.float32) + from_other.astype(jnp.float32)
    return total.astype(jnp.bfloat16)


def y_move(array, k):
    return permute(array, lambda y, z, x, c: (y + k, z, x, c))


def adam(grad, weight, first, second):
    weight_old = weight.astype(jnp.float32)
    moment_one = first_decay_rate * first.astype(jnp.float32) + (1.0 - first_decay_rate) * grad
    moment_two = beta_two * second.astype(jnp.float32) + (1.0 - beta_two) * grad * grad
    updated = weight_old - learn_rate * moment_one / (jnp.sqrt(moment_two) + adam_eps)
    return tuple(v.astype(jnp.bfloat16)[None] for v in (updated, moment_one, moment_two))


def local(
    tokens,
    expert_ids,
    route_weight,
    placement,
    swap_mask,
    gate_weight,
    up_weight,
    down_weight,
    first_moment,
    second_moment,
    out_grad,
):
    tok_rows, top = expert_ids.shape
    width = tokens.shape[1]
    experts = placement.shape[0]
    cap = tok_rows * top * 7 // (6 * experts)
    branch = jnp.clip(swap_mask[0] - 1, 0, 2**SWAP_BITS - 2)
    masks = range(1, 2**SWAP_BITS)

    dest = jnp.arange(8, dtype=jnp.int32)
    held_at = (dest // 2) * 8 + lax.axis_index("zl") * 2 + dest % 2
    ids = jnp.arange(experts, dtype=jnp.int32)
    here = jnp.sum(jnp.where(placement[None, :] == held_at[:, None], ids[None, :], 0), axis=1)
    here = jnp.broadcast_to(here.astype(jnp.float32)[:, None], (8, tok_rows))
    pad = jnp.zeros((8 - top, tok_rows), jnp.float32)
    meta = jnp.concatenate([expert_ids.T.astype(jnp.float32), pad, route_weight.T, pad], axis=0)

    plan = make_plan(cap, top, here, z_gather(meta))
    x_parts = z_gather(tokens)
    g_parts = z_gather(out_grad)

    chunk = width // X_CHUNKS
    xs = [
        plane_exchange(select_rows(False, cap, plan, x_parts, i * chunk, chunk))
        for i in range(X_CHUNKS)
    ]

    chunk = width // G_CHUNKS
    gs = [
        plane_exchange(select_rows(True, cap, plan, g_parts, i * chunk, chunk))
        for i in range(G_CHUNKS)
    ]

    down = down_weight[0]
    state = (down, first_moment[0], second_moment[0])
    state = lax.switch(
        branch, [lambda s, m=m: tuple(relocate(v, m) for v in s) for m in masks], state
    )

    partner = permute(down, lambda y, z, x, c: (y, z + 4, x, c))
    pair = jnp.concatenate([down, partner], axis=0)
    downs = (down, partner, y_move(pair, -1), y_move(pair, -2), y_move(pair, 1))

    where = jnp.stack([lax.axis_index("y"), lax.axis_index("zh")]).astype(jnp.int32)
    hidden = hidden_rows(where, xs, gate_weight[0], up_weight[0])

    chunk = width // R_CHUNKS
    returned = [
        plane_exchange(down_rows(hidden, downs, cap, i * chunk, chunk)) for i in range(R_CHUNKS)
    ]

    halves = []
    for g in gs:
        blocks = grad_blocks(hidden, g)
        total = blocks[0].astype(jnp.float32)
        for k in (1, 2, 3):
            total = total + y_move(blocks[k], k).astype(jnp.float32)
        halves.append(total.astype(jnp.bfloat16))
    total = jnp.concatenate(halves, axis=1)
    rows = total.shape[0] // 2
    mine, theirs = lax.switch(
        branch,
        [lambda a, b, m=m: (relocate(a, m), relocate(b, m, True)) for m in masks],
        total[:rows],
        total[rows:],
    )
    grad = mine.astype(jnp.float32) + theirs.astype(jnp.float32)
    new_state = adam(grad, *state)

    layer_out = jnp.concatenate([z_return(*combine_rows(plan, r)) for r in returned], axis=1)
    return (layer_out, *new_state)


def solution(mesh):
    fine = Mesh(mesh.devices.reshape(N_Y, N_ZH, N_X, N_ZL, N_C), AXES)
    dp, expert = ("y", "zh"), ("x", "zl", "c")
    batch, weight, state = P(dp + expert, None), P(expert, None, None), P(expert, dp, None)
    return jax.shard_map(
        local,
        mesh=fine,
        in_specs=(batch,) * 3 + (P(), P()) + (weight,) * 2 + (state,) * 3 + (batch,),
        out_specs=(batch, state, state, state),
        check_vma=False,
    )
```

```python
import jax
import jax.numpy as jnp
from jax import lax
from jax.experimental import pallas as pl
from jax.experimental.pallas import tpu as pltpu
from jax.sharding import Mesh, PartitionSpec as P

SWAP_BITS = 4
N_Y, N_ZH, N_X, N_ZL, N_C = 4, 2, 4, 4, 2
AXES = ("y", "zh", "x", "zl", "c")
MIB = 1024 * 1024

first_decay_rate = 0.9
beta_two = 0.95
learn_rate = 0.003
adam_eps = 1e-08

G_CHUNKS = 1
R_CHUNKS = 1


def flat_index(y, z, x, c):
    z = z % 8
    return ((((y % 4) * N_ZH + z // N_ZL) * N_X + x % 4) * N_ZL + z % N_ZL) * N_C + c % 2


def permute(array, move):
    pairs = []
    for y in range(N_Y):
        for z in range(8):
            for x in range(N_X):
                for c in range(N_C):
                    pairs.append((flat_index(y, z, x, c), flat_index(*move(y, z, x, c))))
    return lax.ppermute(array, AXES, pairs)


def along(c):
    return 1 if c == 0 else -1


def z_up(array):
    return permute(array, lambda y, z, x, c: (y, z + along(c), x, c))


def z_down(array):
    return permute(array, lambda y, z, x, c: (y, z - along(c), x, c))


def z_gather(array):
    near = z_up(array)
    other = z_down(array)
    far = z_up(near)
    return array, near, other, far


def swap(array, zl=0, x=0, c=0):
    return permute(array, lambda y, z, i, j: (y, z ^ zl, i ^ x, j ^ c))


def relocate(array, jump, flip_zh=False):
    if jump == 0 and not flip_zh:
        return array

    def move(y, z, x, c):
        zl = (z % 4) ^ (jump & 3)
        zh = z // 4 ^ (1 if flip_zh else 0)
        return y, zh * 4 + zl, x ^ (jump >> 2), c

    return permute(array, move)


LIGHT = pl.CostEstimate(flops=1, bytes_accessed=1, transcendentals=0)


def params(mib, *semantics):
    return pltpu.CompilerParams(
        dimension_semantics=semantics or None, vmem_limit_bytes=mib * MIB
    )


def hold_kernel(count, start, *refs):
    out, first = refs[-1], 0
    for array in refs[:count]:
        rows = array.shape[0] - start
        out[first : first + rows, :] = array[start:, :]
        first += rows


def hold(arrays, *earlier, start=0):
    rows, width = sum(a.shape[0] - start for a in arrays), arrays[0].shape[1]
    return pl.pallas_call(
        lambda *refs: hold_kernel(len(arrays), start, *refs),
        in_specs=[pl.BlockSpec(memory_space=pltpu.VMEM) for _ in arrays]
        + [pl.BlockSpec(memory_space=pl.ANY) for _ in earlier],
        out_specs=pl.BlockSpec(memory_space=pltpu.VMEM),
        out_shape=jax.ShapeDtypeStruct((rows, width), arrays[0].dtype),
        compiler_params=params(60),
        cost_estimate=LIGHT,
        name="hold",
    )(*arrays, *earlier)


def choose_kernel(wanted, other, own, *refs):
    @pl.when(wanted[0] == 1)
    def _():
        refs[-1][...] = other[...]

    @pl.when(wanted[0] != 1)
    def _():
        refs[-1][...] = own[...]


def choose(wanted, other, own, *earlier):
    return pl.pallas_call(
        choose_kernel,
        in_specs=[pl.BlockSpec(memory_space=pltpu.SMEM)]
        + [pl.BlockSpec(memory_space=pltpu.VMEM) for _ in range(2)]
        + [pl.BlockSpec(memory_space=pl.ANY) for _ in earlier],
        out_specs=pl.BlockSpec(memory_space=pltpu.VMEM),
        out_shape=jax.ShapeDtypeStruct(own.shape, own.dtype),
        compiler_params=params(60),
        cost_estimate=LIGHT,
        name="choose",
    )(wanted, other, own, *earlier)


def sum_kernel(a, b, c, d, *refs):
    total = a[...].astype(jnp.float32) + b[...].astype(jnp.float32)
    total = total + c[...].astype(jnp.float32) + d[...].astype(jnp.float32)
    refs[-1][...] = total.astype(jnp.bfloat16)


def sum_blocks(blocks, *earlier):
    return pl.pallas_call(
        sum_kernel,
        in_specs=[pl.BlockSpec(memory_space=pltpu.VMEM) for _ in blocks]
        + [pl.BlockSpec(memory_space=pl.ANY) for _ in earlier],
        out_specs=pl.BlockSpec(memory_space=pltpu.VMEM),
        out_shape=jax.ShapeDtypeStruct(blocks[0].shape, jnp.bfloat16),
        compiler_params=params(60),
        cost_estimate=LIGHT,
        name="sum",
    )(*blocks, *earlier)


def plan_kernel(cap, top, ids_here, m0, m1, m2, m3, slot_ref, weight_ref):
    rows = m0.shape[1]
    before = lax.broadcasted_iota(jnp.int32, (rows, rows), 0)
    after = lax.broadcasted_iota(jnp.int32, (rows, rows), 1)
    earlier = (before < after).astype(jnp.float32).astype(jnp.bfloat16)
    wanted = ids_here[...]
    for s, meta in enumerate((m0, m1, m2, m3)):
        named = jnp.zeros(wanted.shape, jnp.float32)
        weight = jnp.zeros(wanted.shape, jnp.float32)
        for k in range(top):
            same = (meta[k : k + 1, :] == wanted).astype(jnp.float32)
            named = named + same
            weight = weight + same * meta[8 + k : 9 + k, :]
        rank = jnp.dot(named.astype(jnp.bfloat16), earlier, preferred_element_type=jnp.float32)
        slot = jnp.where(named > 0.5, rank + float(s * cap), -1.0)
        slot_ref[:, s * rows : (s + 1) * rows] = slot
        weight_ref[:, s * rows : (s + 1) * rows] = weight


def make_plan(cap, top, ids_here, metas):
    rows = metas[0].shape[1]
    out = jax.ShapeDtypeStruct((ids_here.shape[0], 4 * rows), jnp.float32)
    return pl.pallas_call(
        lambda *refs: plan_kernel(cap, top, *refs),
        out_shape=(out, out),
        compiler_params=params(16),
        name="plan",
    )(ids_here, *metas)


def select_kernel(scaled, slots, weights, t0, t1, t2, t3, *refs):
    *outs, pick, scale = refs
    tokens = slots.shape[1]
    block = pick.shape[0] // 8
    base = 8 if scaled else 0

    @pl.when(pl.program_id(0) == 0)
    def _():
        place = lax.broadcasted_iota(jnp.int32, (block, tokens), 0).astype(jnp.float32)
        for d in range(8):
            hit = (slots[base + d : base + d + 1, :] == place).astype(jnp.float32)
            pick[d * block : (d + 1) * block, :] = hit.astype(jnp.bfloat16)
            if scaled:
                row = jnp.sum(hit * weights[base + d : base + d + 1, :], axis=1, keepdims=True)
                scale[d * block : (d + 1) * block, :] = jnp.broadcast_to(row, (block, 128))

    source = jnp.concatenate([t0[...], t1[...], t2[...], t3[...]], axis=0)
    rows = jnp.dot(pick[...], source, preferred_element_type=jnp.float32)
    if scaled:
        rows = (rows * scale[:, 0:1]).astype(jnp.bfloat16)
        for k, out in enumerate(outs[-4:]):
            out[...] = rows[2 * k * block : 2 * (k + 1) * block, :]
    else:
        outs[-1][...] = rows.astype(jnp.bfloat16).reshape(8, block, -1)


def select_rows(scaled, cap, plan, parts, *earlier):
    slots, weights = plan
    rows, width = parts[0].shape
    block = 4 * cap
    tile = 512
    whole = pl.BlockSpec(slots.shape, lambda j: (0, 0))
    if scaled:
        out_spec = (pl.BlockSpec((2 * block, tile), lambda j: (0, j)),) * 4
        out_shape = (jax.ShapeDtypeStruct((2 * block, width), jnp.bfloat16),) * 4
    else:
        out_spec = pl.BlockSpec((8, block, tile), lambda j: (0, 0, j))
        out_shape = jax.ShapeDtypeStruct((8, block, width), jnp.bfloat16)
    return pl.pallas_call(
        lambda *refs: select_kernel(scaled, *refs),
        grid=(width // tile,),
        in_specs=[whole, whole]
        + [pl.BlockSpec((rows, tile), lambda j: (0, j)) for _ in range(4)]
        + [pl.BlockSpec(memory_space=pl.ANY) for _ in earlier],
        out_specs=out_spec,
        out_shape=out_shape,
        scratch_shapes=[
            pltpu.VMEM((8 * block, 4 * rows), jnp.bfloat16),
            pltpu.VMEM((8 * block, 128), jnp.float32),
        ],
        compiler_params=params(60, "arbitrary"),
        cost_estimate=LIGHT,
        name="select_scaled" if scaled else "select",
    )(slots, weights, *parts, *earlier)


def hidden_kernel(count, where, *refs):
    xs, (gate_w, up_w, _, fixed, turned, held) = refs[:count], refs[count:]
    step, tile = pl.program_id(0), gate_w.shape[1]
    steps, features = held.shape[0], fixed.shape[1]
    gate, up, first = None, None, 0
    for x in xs:
        rows = x[...].reshape(-1, x.shape[2])
        part = slice(first, first + x.shape[2])
        first += x.shape[2]
        g = jnp.dot(rows, gate_w[part, :], preferred_element_type=jnp.float32)
        u = jnp.dot(rows, up_w[part, :], preferred_element_type=jnp.float32)
        gate, up = (g, u) if gate is None else (gate + g, up + u)
    held[step] = (gate / (1.0 + jnp.exp(-gate)) * up).astype(jnp.bfloat16)

    @pl.when(step == steps - 1)
    def _():
        shard = features // (N_Y * N_ZH)
        column = lax.broadcasted_iota(jnp.int32, (tile, features), 1)
        row = lax.broadcasted_iota(jnp.int32, (tile, features), 0)
        number = column // shard
        zh = (where[1] + number % 2) % N_ZH
        y = (where[0] + number // 2) % N_Y
        origin = (y * N_ZH + zh) * shard + (column - number * shard)
        total = None
        for s in range(steps):
            fixed[:, s * tile : (s + 1) * tile] = held[s]
            move = (row + s * tile == origin).astype(jnp.float32).astype(jnp.bfloat16)
            part = jnp.dot(held[s], move, preferred_element_type=jnp.float32)
            total = part if total is None else total + part
        turned[...] = total.astype(jnp.bfloat16)


def hidden_rows(where, xs, gate_weight, up_weight, earlier):
    depth, features = gate_weight.shape
    count = xs[0].shape[0] * xs[0].shape[1]
    tile = 256
    steps = features // tile
    return pl.pallas_call(
        lambda *refs: hidden_kernel(len(xs), *refs),
        grid=(steps,),
        in_specs=[pl.BlockSpec(memory_space=pltpu.SMEM)]
        + [pl.BlockSpec(x.shape, lambda j: (0, 0, 0)) for x in xs]
        + [pl.BlockSpec((depth, tile), lambda j: (0, j)) for _ in range(2)]
        + [pl.BlockSpec(memory_space=pl.ANY)],
        out_specs=(pl.BlockSpec((count, features), lambda j: (0, 0)),) * 2,
        out_shape=(jax.ShapeDtypeStruct((count, features), jnp.bfloat16),) * 2,
        scratch_shapes=[pltpu.VMEM((steps, count, tile), jnp.bfloat16)],
        compiler_params=params(60, "arbitrary"),
        name="hidden",
    )(where, *xs, gate_weight, up_weight, earlier)


def down_kernel(hidden, down, out):
    rows = jnp.dot(hidden[...], down[...], preferred_element_type=jnp.float32)
    out[...] = rows.astype(jnp.bfloat16).reshape(out.shape)


def down_rows(hidden, down, cap, first, width):
    tile = 256 if width % 512 else 512
    offset = first // tile
    block = 4 * cap
    return pl.pallas_call(
        down_kernel,
        grid=(width // tile,),
        in_specs=[pl.BlockSpec(hidden.shape, lambda j: (0, 0))]
        + [pl.BlockSpec((down.shape[0], tile), lambda j: (0, j + offset))],
        out_specs=pl.BlockSpec((8, block, tile), lambda j: (0, 0, j)),
        out_shape=jax.ShapeDtypeStruct((8, block, width), jnp.bfloat16),
        compiler_params=params(60, "arbitrary"),
        name="down",
    )(hidden, down)


def grad_kernel(where, hidden, *refs):
    rows, outs, turned = refs[:5], refs[5:9], refs[9]
    block = rows[0].shape[0]

    @pl.when(pl.program_id(0) == 0)
    def _():
        parts = []
        for k in range(8):
            source = (where[2] + N_X - k % 4) % N_X * 2 + (where[3] + k // 4) % 2
            parts.append(hidden[pl.ds(pl.multiple_of(source * block, 16), block), :])
        turned[...] = jnp.concatenate(parts, axis=0).T

    value = jnp.concatenate([r[...] for r in rows], axis=0)
    grad = jnp.dot(turned[...], value, preferred_element_type=jnp.float32).astype(jnp.bfloat16)
    quarter = outs[0].shape[0]
    for k, out in enumerate(outs):
        out[...] = grad[k * quarter : (k + 1) * quarter, :]


def grad_blocks(where, hidden, rows, first, width):
    block = rows[0].shape[0] // 2
    tile = 256 if width % 512 else 512
    offset = first // tile
    quarter = hidden.shape[1] // N_Y
    spec = pl.BlockSpec((quarter, tile), lambda j: (0, j))
    out = jax.ShapeDtypeStruct((quarter, width), jnp.bfloat16)
    return pl.pallas_call(
        grad_kernel,
        grid=(width // tile,),
        in_specs=[
            pl.BlockSpec(memory_space=pltpu.SMEM),
            pl.BlockSpec(hidden.shape, lambda j: (0, 0)),
        ]
        + [pl.BlockSpec((block, tile), lambda j: (0, j + offset)) for _ in range(4)]
        + [pl.BlockSpec((4 * block, tile), lambda j: (0, j + offset))],
        out_specs=(spec,) * 4,
        out_shape=(out,) * 4,
        scratch_shapes=[pltpu.VMEM(hidden.shape[::-1], jnp.bfloat16)],
        compiler_params=params(60, "arbitrary"),
        name="grad",
    )(where, hidden, *rows)


def combine_kernel(slots, weights, rows, o0, o1, o2, o3, high, low):
    dests, block, width = rows.shape
    tokens = slots.shape[1]

    @pl.when(pl.program_id(0) == 0)
    def _():
        place = lax.broadcasted_iota(jnp.int32, (block, tokens), 0).astype(jnp.float32)
        picked = []
        for d in range(dests):
            hit = (slots[d : d + 1, :] == place).astype(jnp.float32)
            picked.append(hit * weights[d : d + 1, :])
        pick = jnp.concatenate(picked, axis=0).T
        coarse = pick.astype(jnp.bfloat16)
        high[...] = coarse
        low[...] = (pick - coarse.astype(jnp.float32)).astype(jnp.bfloat16)

    value = rows[...].reshape(-1, width)
    total = jnp.dot(high[...], value, preferred_element_type=jnp.float32)
    total = total + jnp.dot(low[...], value, preferred_element_type=jnp.float32)
    count = o0.shape[0]
    for s, out in enumerate((o0, o1, o2, o3)):
        out[...] = total[s * count : (s + 1) * count, :].astype(out.dtype)


def combine_rows(plan, rows):
    slots, weights = plan
    width = rows.shape[2]
    tile = 256 if width % 512 else 512
    count = slots.shape[1] // 4
    whole = pl.BlockSpec((8, slots.shape[1]), lambda j: (0, 0))
    spec = pl.BlockSpec((count, tile), lambda j: (0, j))
    return pl.pallas_call(
        combine_kernel,
        grid=(width // tile,),
        in_specs=[whole, whole, pl.BlockSpec((*rows.shape[:2], tile), lambda j: (0, 0, j))],
        out_specs=(spec,) * 4,
        out_shape=tuple(
            jax.ShapeDtypeStruct((count, width), t)
            for t in (jnp.float32, jnp.bfloat16, jnp.bfloat16, jnp.bfloat16)
        ),
        scratch_shapes=[
            pltpu.VMEM((slots.shape[1], rows.shape[0] * rows.shape[1]), jnp.bfloat16)
            for _ in range(2)
        ],
        compiler_params=params(60, "arbitrary"),
        name="combine",
    )(slots, weights, rows)


def plane_permute(blocks):
    out = [blocks[0]]
    for k in range(1, N_X):
        out.append(permute(blocks[k], lambda y, z, x, c, k=k: (y, z, x + k, c)))
    return out


def core_permute(blocks, *earlier):
    passed = hold(blocks, *earlier, start=blocks[0].shape[0] // 2)
    return permute(passed, lambda y, z, x, c: (y, z, x, c + 1))


def plane_exchange(rows):
    return lax.all_to_all(rows, ("x", "c"), split_axis=0, concat_axis=0, tiled=True)


def z_return(own, near, other, far):
    step = z_down(far).astype(jnp.float32) + near.astype(jnp.float32)
    from_near = z_down(step.astype(jnp.bfloat16))
    from_other = z_up(other)
    total = own + from_near.astype(jnp.float32) + from_other.astype(jnp.float32)
    return total.astype(jnp.bfloat16)


def y_move(array, k):
    return permute(array, lambda y, z, x, c: (y + k, z, x, c))


def adam(grad, weight, first, second):
    weight_old = weight.astype(jnp.float32)
    moment_one = first_decay_rate * first.astype(jnp.float32) + (1.0 - first_decay_rate) * grad
    moment_two = beta_two * second.astype(jnp.float32) + (1.0 - beta_two) * grad * grad
    updated = weight_old - learn_rate * moment_one / (jnp.sqrt(moment_two) + adam_eps)
    return tuple(v.astype(jnp.bfloat16)[None] for v in (updated, moment_one, moment_two))


def local(
    tokens,
    expert_ids,
    route_weight,
    placement,
    swap_mask,
    gate_weight,
    up_weight,
    down_weight,
    first_moment,
    second_moment,
    out_grad,
):
    tok_rows, top = expert_ids.shape
    width = tokens.shape[1]
    experts = placement.shape[0]
    cap = tok_rows * top * 7 // (6 * experts)
    jumps = range(2 ** (SWAP_BITS - 1))
    jump = jnp.clip(swap_mask[0] // 2, 0, len(jumps) - 1)
    bits = [swap_mask // 2**bit % 2 for bit in range(SWAP_BITS)]

    where = [lax.axis_index(a) for a in ("y", "zh", "x", "c")]
    where = jnp.stack(where).astype(jnp.int32)

    dest = jnp.arange(8, dtype=jnp.int32)
    ring = (where[2] + dest // 2) % N_X * 2 + (where[3] + dest) % 2
    dest = jnp.concatenate([dest, ring])
    held_at = (dest // 2) * 8 + lax.axis_index("zl") * 2 + dest % 2
    ids = jnp.arange(experts, dtype=jnp.int32)
    here = jnp.sum(jnp.where(placement[None, :] == held_at[:, None], ids[None, :], 0), axis=1)
    here = jnp.broadcast_to(here.astype(jnp.float32)[:, None], (16, tok_rows))
    pad = jnp.zeros((8 - top, tok_rows), jnp.float32)
    meta = jnp.concatenate([expert_ids.T.astype(jnp.float32), pad, route_weight.T, pad], axis=0)

    plan = make_plan(cap, top, here, z_gather(meta))
    x_parts = z_gather(tokens)
    state = hold((down_weight[0], first_moment[0], second_moment[0]))
    far_state = swap(state, x=1)
    x_send = select_rows(False, cap, plan, x_parts, far_state)
    x_rows = plane_exchange(x_send)
    g_parts = z_gather(hold((out_grad,), x_send))
    state = choose(bits[3], far_state, state, x_send)
    state_cores = choose(bits[0], swap(state, c=1), state, g_parts[1], g_parts[2])
    state = choose(bits[1], swap(state_cores, zl=1), state_cores)
    state_far = swap(state, zl=2)

    g_send = select_rows(True, cap, plan, g_parts, x_rows, state_cores)
    g_rows = plane_permute(g_send)

    down_full = lax.all_gather(down_weight[0], ("y", "zh"), axis=0, tiled=True)

    hidden, turned = hidden_rows(where, [x_rows], gate_weight[0], up_weight[0], g_send[3])

    chunk = width // R_CHUNKS
    r_sends = [down_rows(hidden, down_full, cap, i * chunk, chunk) for i in range(R_CHUNKS)]
    returned = [plane_exchange(r) for r in r_sends]

    g_rows = (*g_rows, core_permute(g_rows, r_sends[0], state))
    state = jnp.split(choose(bits[2], state_far, state, r_sends[0]), 3, axis=0)

    halves = []
    chunk = width // G_CHUNKS
    for i in range(G_CHUNKS):
        blocks = grad_blocks(where, turned, g_rows, i * chunk, chunk)
        blocks = [blocks[0]] + [y_move(blocks[k], k) for k in (1, 2, 3)]
        halves.append(sum_blocks(blocks, returned[0]))
    total = jnp.concatenate(halves, axis=1)
    total = jnp.where(bits[0][0] == 1, swap(total, c=1), total)
    rows = total.shape[0] // 2
    mine, theirs = lax.switch(
        jump,
        [lambda a, b, m=m: (relocate(a, m), relocate(b, m, True)) for m in jumps],
        total[:rows],
        total[rows:],
    )
    grad = mine.astype(jnp.float32) + theirs.astype(jnp.float32)
    new_state = adam(grad, *state)

    layer_out = jnp.concatenate([z_return(*combine_rows(plan, r)) for r in returned], axis=1)
    return (layer_out, *new_state)


def solution(mesh):
    fine = Mesh(mesh.devices.reshape(N_Y, N_ZH, N_X, N_ZL, N_C), AXES)
    dp, expert = ("y", "zh"), ("x", "zl", "c")
    batch, weight, state = P(dp + expert, None), P(expert, None, None), P(expert, dp, None)
    return jax.shard_map(
        local,
        mesh=fine,
        in_specs=(batch,) * 3 + (P(), P()) + (weight,) * 2 + (state,) * 3 + (batch,),
        out_specs=(batch, state, state, state),
        check_vma=False,
    )
```

```python
import jax
import jax.numpy as jnp
from jax import lax
from jax.experimental import pallas as pl
from jax.experimental.pallas import tpu as pltpu
from jax.sharding import Mesh, PartitionSpec as P

SWAP_BITS = 4
N_Y, N_ZH, N_X, N_ZL, N_C = 4, 2, 4, 4, 2
AXES = ("y", "zh", "x", "zl", "c")
MIB = 1024 * 1024

first_decay_rate = 0.9
beta_two = 0.95
learn_rate = 0.003
adam_eps = 1e-08

G_CHUNKS = 2
R_CHUNKS = 2


def flat_index(y, z, x, c):
    z = z % 8
    return ((((y % 4) * N_ZH + z // N_ZL) * N_X + x % 4) * N_ZL + z % N_ZL) * N_C + c % 2


def permute(array, move):
    pairs = []
    for y in range(N_Y):
        for z in range(8):
            for x in range(N_X):
                for c in range(N_C):
                    pairs.append((flat_index(y, z, x, c), flat_index(*move(y, z, x, c))))
    return lax.ppermute(array, AXES, pairs)


def along(c):
    return 1 if c == 0 else -1


def z_up(array):
    return permute(array, lambda y, z, x, c: (y, z + along(c), x, c))


def z_down(array):
    return permute(array, lambda y, z, x, c: (y, z - along(c), x, c))


def z_gather(array):
    near = z_up(array)
    other = z_down(array)
    far = z_up(near)
    return array, near, other, far


def swap(array, zl=0, x=0, c=0):
    return permute(array, lambda y, z, i, j: (y, z ^ zl, i ^ x, j ^ c))


def relocate(array, jump, flip_zh=False):
    if jump == 0 and not flip_zh:
        return array

    def move(y, z, x, c):
        zl = (z % 4) ^ (jump & 3)
        zh = z // 4 ^ (1 if flip_zh else 0)
        return y, zh * 4 + zl, x ^ (jump >> 2), c

    return permute(array, move)


LIGHT = pl.CostEstimate(flops=1, bytes_accessed=1, transcendentals=0)


def params(mib, *semantics):
    return pltpu.CompilerParams(
        dimension_semantics=semantics or None, vmem_limit_bytes=mib * MIB
    )


def hold_kernel(count, start, *refs):
    out, first = refs[-1], 0
    for array in refs[:count]:
        rows = array.shape[0] - start
        out[first : first + rows, :] = array[start:, :]
        first += rows


def hold(arrays, *earlier, start=0):
    rows, width = sum(a.shape[0] - start for a in arrays), arrays[0].shape[1]
    return pl.pallas_call(
        lambda *refs: hold_kernel(len(arrays), start, *refs),
        in_specs=[pl.BlockSpec(memory_space=pltpu.VMEM) for _ in arrays]
        + [pl.BlockSpec(memory_space=pl.ANY) for _ in earlier],
        out_specs=pl.BlockSpec(memory_space=pltpu.VMEM),
        out_shape=jax.ShapeDtypeStruct((rows, width), arrays[0].dtype),
        compiler_params=params(60),
        cost_estimate=LIGHT,
        name="hold",
    )(*arrays, *earlier)


def mark_kernel(tokens, meta, out):
    width = tokens.shape[1]
    out[:, :width] = tokens[...]
    left = meta[...]
    total = None
    for turn in range(3):
        part = left.astype(jnp.bfloat16).astype(jnp.float32)
        left = left - part
        part = pltpu.roll(part, 16 * turn, 1) if turn else part
        total = part if total is None else total + part
    out[:, width:] = total.astype(jnp.bfloat16)


def mark(tokens, meta):
    rows, width = tokens.shape
    return pl.pallas_call(
        mark_kernel,
        in_specs=[pl.BlockSpec(memory_space=pltpu.VMEM)] * 2,
        out_specs=pl.BlockSpec(memory_space=pltpu.VMEM),
        out_shape=jax.ShapeDtypeStruct((rows, width + 128), jnp.bfloat16),
        compiler_params=params(60),
        cost_estimate=LIGHT,
        name="mark",
    )(tokens, meta)


def choose_kernel(wanted, other, own, *refs):
    @pl.when(wanted[0] == 1)
    def _():
        refs[-1][...] = other[...]

    @pl.when(wanted[0] != 1)
    def _():
        refs[-1][...] = own[...]


def choose(wanted, other, own, *earlier):
    return pl.pallas_call(
        choose_kernel,
        in_specs=[pl.BlockSpec(memory_space=pltpu.SMEM)]
        + [pl.BlockSpec(memory_space=pltpu.VMEM) for _ in range(2)]
        + [pl.BlockSpec(memory_space=pl.ANY) for _ in earlier],
        out_specs=pl.BlockSpec(memory_space=pltpu.VMEM),
        out_shape=jax.ShapeDtypeStruct(own.shape, own.dtype),
        compiler_params=params(60),
        cost_estimate=LIGHT,
        name="choose",
    )(wanted, other, own, *earlier)


def plan_kernel(cap, top, ids_here, m0, m1, m2, m3, slot_ref, weight_ref):
    rows = m0.shape[0]
    before = lax.broadcasted_iota(jnp.int32, (rows, rows), 0)
    after = lax.broadcasted_iota(jnp.int32, (rows, rows), 1)
    earlier = (before < after).astype(jnp.float32).astype(jnp.bfloat16)
    wanted = ids_here[...]
    for s, block in enumerate((m0, m1, m2, m3)):
        meta = block[...].astype(jnp.float32).T
        scale = meta[8:16, :] + meta[24:32, :] + meta[40:48, :]
        named = jnp.zeros(wanted.shape, jnp.float32)
        weight = jnp.zeros(wanted.shape, jnp.float32)
        for k in range(top):
            same = (meta[k : k + 1, :] == wanted).astype(jnp.float32)
            named = named + same
            weight = weight + same * scale[k : k + 1, :]
        rank = jnp.dot(named.astype(jnp.bfloat16), earlier, preferred_element_type=jnp.float32)
        slot = jnp.where(named > 0.5, rank + float(s * cap), -1.0)
        slot_ref[:, s * rows : (s + 1) * rows] = slot
        weight_ref[:, s * rows : (s + 1) * rows] = weight


def make_plan(cap, top, ids_here, parts):
    rows, width = parts[0].shape
    last = width // 128 - 1
    out = jax.ShapeDtypeStruct((ids_here.shape[0], 4 * rows), jnp.float32)
    whole = pl.BlockSpec(out.shape, lambda i: (0, 0))
    return pl.pallas_call(
        lambda *refs: plan_kernel(cap, top, *refs),
        grid=(1,),
        in_specs=[pl.BlockSpec(ids_here.shape, lambda i: (0, 0))]
        + [pl.BlockSpec((rows, 128), lambda i: (0, last)) for _ in parts],
        out_specs=(whole, whole),
        out_shape=(out, out),
        compiler_params=params(60, "arbitrary"),
        cost_estimate=LIGHT,
        name="plan",
    )(ids_here, *parts)


def select_kernel(scaled, slots, weights, t0, t1, t2, t3, *refs):
    *outs, pick, scale = refs
    tokens = slots.shape[1]
    block = pick.shape[0] // 8
    base = 8 if scaled else 0

    @pl.when(pl.program_id(0) == 0)
    def _():
        place = lax.broadcasted_iota(jnp.int32, (block, tokens), 0).astype(jnp.float32)
        for d in range(8):
            hit = (slots[base + d : base + d + 1, :] == place).astype(jnp.float32)
            pick[d * block : (d + 1) * block, :] = hit.astype(jnp.bfloat16)
            if scaled:
                row = jnp.sum(hit * weights[base + d : base + d + 1, :], axis=1, keepdims=True)
                scale[d * block : (d + 1) * block, :] = jnp.broadcast_to(row, (block, 128))

    source = jnp.concatenate([t0[...], t1[...], t2[...], t3[...]], axis=0)
    rows = jnp.dot(pick[...], source, preferred_element_type=jnp.float32)
    if scaled:
        rows = (rows * scale[:, 0:1]).astype(jnp.bfloat16)
        for k, out in enumerate(outs[-4:]):
            out[...] = rows[2 * k * block : 2 * (k + 1) * block, :]
    else:
        outs[-1][...] = rows.astype(jnp.bfloat16).reshape(8, block, -1)


def select_rows(scaled, cap, plan, parts, first, width, *earlier):
    slots, weights = plan
    rows = parts[0].shape[0]
    block = 4 * cap
    tile = 256 if width % 512 else 512
    offset = first // tile
    whole = pl.BlockSpec(slots.shape, lambda j: (0, 0))
    if scaled:
        out_spec = (pl.BlockSpec((2 * block, tile), lambda j: (0, j)),) * 4
        out_shape = (jax.ShapeDtypeStruct((2 * block, width), jnp.bfloat16),) * 4
    else:
        out_spec = pl.BlockSpec((8, block, tile), lambda j: (0, 0, j))
        out_shape = jax.ShapeDtypeStruct((8, block, width), jnp.bfloat16)
    return pl.pallas_call(
        lambda *refs: select_kernel(scaled, *refs),
        grid=(width // tile,),
        in_specs=[whole, whole]
        + [pl.BlockSpec((rows, tile), lambda j: (0, j + offset)) for _ in range(4)]
        + [pl.BlockSpec(memory_space=pl.ANY) for _ in earlier],
        out_specs=out_spec,
        out_shape=out_shape,
        scratch_shapes=[
            pltpu.VMEM((8 * block, 4 * rows), jnp.bfloat16),
            pltpu.VMEM((8 * block, 128), jnp.float32),
        ],
        compiler_params=params(60, "arbitrary"),
        cost_estimate=LIGHT,
        name="select_scaled" if scaled else "select",
    )(slots, weights, *parts, *earlier)


def hidden_kernel(count, *refs):
    xs, (gate_w, up_w), out = refs[:count], refs[count : count + 2], refs[-1]
    gate, up, first = None, None, 0
    for x in xs:
        rows = x[...].reshape(-1, x.shape[2])
        part = slice(first, first + x.shape[2])
        first += x.shape[2]
        g = jnp.dot(rows, gate_w[part, :], preferred_element_type=jnp.float32)
        u = jnp.dot(rows, up_w[part, :], preferred_element_type=jnp.float32)
        gate, up = (g, u) if gate is None else (gate + g, up + u)
    out[...] = (gate / (1.0 + jnp.exp(-gate)) * up).astype(jnp.bfloat16)


def hidden_rows(xs, gate_weight, up_weight, earlier):
    depth, features = gate_weight.shape
    count = xs[0].shape[0] * xs[0].shape[1]
    tile = 256
    return pl.pallas_call(
        lambda *refs: hidden_kernel(len(xs), *refs),
        grid=(features // tile,),
        in_specs=[pl.BlockSpec(x.shape, lambda j: (0, 0, 0)) for x in xs]
        + [pl.BlockSpec((depth, tile), lambda j: (0, j)) for _ in range(2)]
        + [pl.BlockSpec(memory_space=pl.ANY) for _ in earlier],
        out_specs=pl.BlockSpec((count, tile), lambda j: (0, j)),
        out_shape=jax.ShapeDtypeStruct((count, features), jnp.bfloat16),
        compiler_params=params(60, "arbitrary"),
        cost_estimate=LIGHT,
        name="hidden",
    )(*xs, gate_weight, up_weight, *earlier)


def down_kernel(hidden, down, *refs):
    out = refs[-1]
    rows = jnp.dot(hidden[...], down[...], preferred_element_type=jnp.float32)
    out[...] = rows.astype(jnp.bfloat16).reshape(out.shape)


def down_rows(hidden, down, cap, first, width, *earlier):
    tile = 256 if width % 512 else 512
    offset = first // tile
    block = 4 * cap
    return pl.pallas_call(
        down_kernel,
        grid=(width // tile,),
        in_specs=[pl.BlockSpec(hidden.shape, lambda j: (0, 0))]
        + [pl.BlockSpec((down.shape[0], tile), lambda j: (0, j + offset))]
        + [pl.BlockSpec(memory_space=pl.ANY) for _ in earlier],
        out_specs=pl.BlockSpec((8, block, tile), lambda j: (0, 0, j)),
        out_shape=jax.ShapeDtypeStruct((8, block, width), jnp.bfloat16),
        compiler_params=params(60, "arbitrary"),
        cost_estimate=LIGHT,
        name="down",
    )(hidden, down, *earlier)


def grad_kernel(where, hidden, *refs):
    rows, out, turned = refs[:5], refs[5], refs[6]
    block = rows[0].shape[0]

    @pl.when(pl.program_id(0) == 0)
    def _():
        parts = []
        for k in range(8):
            source = (where[0] + N_X - k % 4) % N_X * 2 + (where[1] + k // 4) % 2
            parts.append(hidden[pl.ds(pl.multiple_of(source * block, 16), block), :])
        turned[...] = jnp.concatenate(parts, axis=0).T

    value = jnp.concatenate([r[...] for r in rows], axis=0)
    grad = jnp.dot(turned[...], value, preferred_element_type=jnp.float32)
    out[...] = grad.astype(jnp.bfloat16)


def grad_partial(where, hidden, rows):
    width = rows[0].shape[1]
    block = rows[0].shape[0] // 2
    tile = 256 if width % 512 else 512
    features = hidden.shape[1]
    return pl.pallas_call(
        grad_kernel,
        grid=(width // tile,),
        in_specs=[
            pl.BlockSpec(memory_space=pltpu.SMEM),
            pl.BlockSpec(hidden.shape, lambda j: (0, 0)),
        ]
        + [pl.BlockSpec((block, tile), lambda j: (0, j)) for _ in range(4)]
        + [pl.BlockSpec((4 * block, tile), lambda j: (0, j))],
        out_specs=pl.BlockSpec((features, tile), lambda j: (0, j)),
        out_shape=jax.ShapeDtypeStruct((features, width), jnp.bfloat16),
        scratch_shapes=[pltpu.VMEM(hidden.shape[::-1], jnp.bfloat16)],
        compiler_params=params(60, "arbitrary"),
        cost_estimate=LIGHT,
        name="grad",
    )(where, hidden, *rows)


def combine_kernel(slots, weights, rows, *refs):
    *outs, high, low = refs[-6:]
    dests, block, width = rows.shape
    tokens = slots.shape[1]

    @pl.when(pl.program_id(0) == 0)
    def _():
        place = lax.broadcasted_iota(jnp.int32, (block, tokens), 0).astype(jnp.float32)
        picked = []
        for d in range(dests):
            hit = (slots[d : d + 1, :] == place).astype(jnp.float32)
            picked.append(hit * weights[d : d + 1, :])
        pick = jnp.concatenate(picked, axis=0).T
        coarse = pick.astype(jnp.bfloat16)
        high[...] = coarse
        low[...] = (pick - coarse.astype(jnp.float32)).astype(jnp.bfloat16)

    value = rows[...].reshape(-1, width)
    total = jnp.dot(high[...], value, preferred_element_type=jnp.float32)
    total = total + jnp.dot(low[...], value, preferred_element_type=jnp.float32)
    count = outs[0].shape[0]
    for s, out in enumerate(outs):
        out[...] = total[s * count : (s + 1) * count, :].astype(out.dtype)


def combine_rows(plan, rows, *earlier):
    slots, weights = plan
    width = rows.shape[2]
    tile = 256 if width % 512 else 512
    count = slots.shape[1] // 4
    whole = pl.BlockSpec((8, slots.shape[1]), lambda j: (0, 0))
    spec = pl.BlockSpec((count, tile), lambda j: (0, j))
    return pl.pallas_call(
        combine_kernel,
        grid=(width // tile,),
        in_specs=[whole, whole, pl.BlockSpec((*rows.shape[:2], tile), lambda j: (0, 0, j))]
        + [pl.BlockSpec(memory_space=pl.ANY) for _ in earlier],
        out_specs=(spec,) * 4,
        out_shape=tuple(
            jax.ShapeDtypeStruct((count, width), t)
            for t in (jnp.float32, jnp.bfloat16, jnp.bfloat16, jnp.bfloat16)
        ),
        scratch_shapes=[
            pltpu.VMEM((slots.shape[1], rows.shape[0] * rows.shape[1]), jnp.bfloat16)
            for _ in range(2)
        ],
        compiler_params=params(60, "arbitrary"),
        cost_estimate=LIGHT,
        name="combine",
    )(slots, weights, rows, *earlier)


def plane_permute(blocks):
    out = [blocks[0]]
    for k in range(1, N_X):
        out.append(permute(blocks[k], lambda y, z, x, c, k=k: (y, z, x + k, c)))
    return out


def core_permute(blocks, *earlier):
    passed = hold(blocks, *earlier, start=blocks[0].shape[0] // 2)
    return permute(passed, lambda y, z, x, c: (y, z, x, c + 1))


def plane_exchange(rows):
    return lax.all_to_all(rows, ("x", "c"), split_axis=0, concat_axis=0, tiled=True)


def z_return(own, near, other, far):
    step = z_down(far).astype(jnp.float32) + near.astype(jnp.float32)
    from_near = z_down(step.astype(jnp.bfloat16))
    from_other = z_up(other)
    total = own + from_near.astype(jnp.float32) + from_other.astype(jnp.float32)
    return total.astype(jnp.bfloat16)


def adam(grad, weight, first, second):
    weight_old = weight.astype(jnp.float32)
    moment_one = first_decay_rate * first.astype(jnp.float32) + (1.0 - first_decay_rate) * grad
    moment_two = beta_two * second.astype(jnp.float32) + (1.0 - beta_two) * grad * grad
    updated = weight_old - learn_rate * moment_one / (jnp.sqrt(moment_two) + adam_eps)
    return tuple(v.astype(jnp.bfloat16)[None] for v in (updated, moment_one, moment_two))


def local(
    tokens,
    expert_ids,
    route_weight,
    placement,
    swap_mask,
    gate_weight,
    up_weight,
    down_weight,
    first_moment,
    second_moment,
    out_grad,
):
    tok_rows, top = expert_ids.shape
    width = tokens.shape[1]
    experts = placement.shape[0]
    cap = tok_rows * top * 7 // (6 * experts)
    jumps = range(2 ** (SWAP_BITS - 1))
    jump = jnp.clip(swap_mask[0] // 2, 0, len(jumps) - 1)
    bits = [swap_mask // 2**bit % 2 for bit in range(SWAP_BITS)]

    where = [lax.axis_index(a) for a in ("x", "c")]
    where = jnp.stack(where).astype(jnp.int32)

    dest = jnp.arange(8, dtype=jnp.int32)
    ring = (where[0] + dest // 2) % N_X * 2 + (where[1] + dest) % 2
    dest = jnp.concatenate([dest, ring])
    held_at = (dest // 2) * 8 + lax.axis_index("zl") * 2 + dest % 2
    ids = jnp.arange(experts, dtype=jnp.int32)
    here = jnp.sum(jnp.where(placement[None, :] == held_at[:, None], ids[None, :], 0), axis=1)
    here = jnp.broadcast_to(here.astype(jnp.float32)[:, None], (16, tok_rows))
    numbers = jnp.pad(expert_ids.astype(jnp.float32), ((0, 0), (0, 128 - top)))
    meta = numbers + jnp.pad(route_weight, ((0, 0), (8, 120 - top)))

    x_parts = z_gather(mark(tokens, meta))
    plan = make_plan(cap, top, here, x_parts)
    state = hold((down_weight[0], first_moment[0], second_moment[0]))
    far_state = swap(state, x=1)
    x_send = select_rows(False, cap, plan, x_parts, 0, width, far_state)
    x_rows = plane_exchange(x_send)
    g_parts = z_gather(hold((out_grad,), x_parts[3]))
    state = choose(bits[3], far_state, state, x_send)
    state_cores = choose(bits[0], swap(state, c=1), state, g_parts[1], g_parts[2])
    state = choose(bits[1], swap(state_cores, zl=1), state_cores)
    state_far = swap(state, zl=2)

    chunk = width // G_CHUNKS
    g_sends = []
    for i in range(G_CHUNKS):
        earlier = [x_rows, state_cores] + [g[3] for g in g_sends]
        g_sends.append(select_rows(True, cap, plan, g_parts, i * chunk, chunk, *earlier))
    g_rows = [plane_permute(g) for g in g_sends]

    down_full = lax.all_gather(down_weight[0], ("y", "zh"), axis=0, tiled=True)

    hidden = hidden_rows([x_rows], gate_weight[0], up_weight[0], [g[3] for g in g_sends] + [state])

    chunk = width // R_CHUNKS
    r_sends = []
    for i in range(R_CHUNKS):
        earlier = g_rows[i % G_CHUNKS][1:] if i else ()
        r_sends.append(down_rows(hidden, down_full, cap, i * chunk, chunk, *earlier))
    returned = [plane_exchange(r) for r in r_sends]

    near_state = state
    state = choose(bits[2], state_far, state, r_sends[0])

    grads, partial, zh = [], None, lax.axis_index("zh")
    for i, g in enumerate(g_rows):
        earlier = (near_state,) if partial is None else (partial, *returned[:i])
        passed = core_permute(g, r_sends[i % R_CHUNKS], *earlier)
        partial = grad_partial(where, hidden, (*g, passed))
        total = lax.psum_scatter(partial, "y", scatter_dimension=0, tiled=True)
        total = choose(bits[0], swap(total, c=1), total, *returned[1 : i + 1])
        rows = total.shape[0] // 2
        mine, theirs = lax.switch(
            jump,
            [lambda a, b, m=m: (relocate(a, m), relocate(b, m, True)) for m in jumps],
            lax.dynamic_slice_in_dim(total, zh * rows, rows),
            lax.dynamic_slice_in_dim(total, (1 - zh) * rows, rows),
        )
        grads.append(mine.astype(jnp.float32) + theirs.astype(jnp.float32))
    new_state = adam(jnp.concatenate(grads, axis=1), *jnp.split(state, 3, axis=0))

    sums = [combine_rows(plan, r, *grads[:i]) for i, r in enumerate(returned)]
    layer_out = jnp.concatenate([z_return(*s) for s in sums], axis=1)
    return (layer_out, *new_state)


def solution(mesh):
    fine = Mesh(mesh.devices.reshape(N_Y, N_ZH, N_X, N_ZL, N_C), AXES)
    dp, expert = ("y", "zh"), ("x", "zl", "c")
    batch, weight, state = P(dp + expert, None), P(expert, None, None), P(expert, dp, None)
    return jax.shard_map(
        local,
        mesh=fine,
        in_specs=(batch,) * 3 + (P(), P()) + (weight,) * 2 + (state,) * 3 + (batch,),
        out_specs=(batch, state, state, state),
        check_vma=False,
    )
```

```python
import jax
import jax.numpy as jnp
from jax import lax
from jax.experimental import pallas as pl
from jax.experimental.pallas import tpu as pltpu
from jax.sharding import Mesh, PartitionSpec as P

SWAP_BITS = 4
N_Y, N_ZH, N_X, N_ZL, N_C = 4, 2, 4, 4, 2
AXES = ("y", "zh", "x", "zl", "c")
MIB = 1024 * 1024

first_decay_rate = 0.9
beta_two = 0.95
learn_rate = 0.003
adam_eps = 1e-08

G_CHUNKS = 2


def flat_index(y, z, x, c):
    z = z % 8
    return ((((y % 4) * N_ZH + z // N_ZL) * N_X + x % 4) * N_ZL + z % N_ZL) * N_C + c % 2


def permute(array, move):
    pairs = []
    for y in range(N_Y):
        for z in range(8):
            for x in range(N_X):
                for c in range(N_C):
                    pairs.append((flat_index(y, z, x, c), flat_index(*move(y, z, x, c))))
    return lax.ppermute(array, AXES, pairs)


def along(c):
    return 1 if c == 0 else -1


def z_up(array):
    return permute(array, lambda y, z, x, c: (y, z + along(c), x, c))


def z_down(array):
    return permute(array, lambda y, z, x, c: (y, z - along(c), x, c))


def z_gather(array):
    near = z_up(array)
    other = z_down(array)
    far = z_up(near)
    return array, near, other, far


def swap(array, zl=0, x=0, c=0):
    return permute(array, lambda y, z, i, j: (y, z ^ zl, i ^ x, j ^ c))


def relocate(array, jump, flip_zh=False):
    if jump == 0 and not flip_zh:
        return array

    def move(y, z, x, c):
        zl = (z % 4) ^ (jump & 3)
        zh = z // 4 ^ (1 if flip_zh else 0)
        return y, zh * 4 + zl, x ^ (jump >> 2), c

    return permute(array, move)


LIGHT = pl.CostEstimate(flops=1, bytes_accessed=1, transcendentals=0)


def params(mib, *semantics):
    return pltpu.CompilerParams(
        dimension_semantics=semantics or None, vmem_limit_bytes=mib * MIB
    )


def hold_kernel(count, start, *refs):
    out, first = refs[-1], 0
    for array in refs[:count]:
        rows = array.shape[0] - start
        out[first : first + rows, :] = array[start:, :]
        first += rows


def hold(arrays, *earlier, start=0):
    rows, width = sum(a.shape[0] - start for a in arrays), arrays[0].shape[1]
    return pl.pallas_call(
        lambda *refs: hold_kernel(len(arrays), start, *refs),
        in_specs=[pl.BlockSpec(memory_space=pltpu.VMEM) for _ in arrays]
        + [pl.BlockSpec(memory_space=pl.ANY) for _ in earlier],
        out_specs=pl.BlockSpec(memory_space=pltpu.VMEM),
        out_shape=jax.ShapeDtypeStruct((rows, width), arrays[0].dtype),
        compiler_params=params(60),
        cost_estimate=LIGHT,
        name="hold",
    )(*arrays, *earlier)


def mark_kernel(tokens, meta, out):
    width = tokens.shape[1]
    out[:, :width] = tokens[...]
    left = meta[...]
    total = None
    for turn in range(3):
        part = left.astype(jnp.bfloat16).astype(jnp.float32)
        left = left - part
        part = pltpu.roll(part, 16 * turn, 1) if turn else part
        total = part if total is None else total + part
    out[:, width:] = total.astype(jnp.bfloat16)


def mark(tokens, meta):
    rows, width = tokens.shape
    return pl.pallas_call(
        mark_kernel,
        in_specs=[pl.BlockSpec(memory_space=pltpu.VMEM)] * 2,
        out_specs=pl.BlockSpec(memory_space=pltpu.VMEM),
        out_shape=jax.ShapeDtypeStruct((rows, width + 128), jnp.bfloat16),
        compiler_params=params(60),
        cost_estimate=LIGHT,
        name="mark",
    )(tokens, meta)


def choose_kernel(wanted, other, own, *refs):
    @pl.when(wanted[0] == 1)
    def _():
        refs[-1][...] = other[...]

    @pl.when(wanted[0] != 1)
    def _():
        refs[-1][...] = own[...]


def choose(wanted, other, own, *earlier):
    return pl.pallas_call(
        choose_kernel,
        in_specs=[pl.BlockSpec(memory_space=pltpu.SMEM)]
        + [pl.BlockSpec(memory_space=pltpu.VMEM) for _ in range(2)]
        + [pl.BlockSpec(memory_space=pl.ANY) for _ in earlier],
        out_specs=pl.BlockSpec(memory_space=pltpu.VMEM),
        out_shape=jax.ShapeDtypeStruct(own.shape, own.dtype),
        compiler_params=params(60),
        cost_estimate=LIGHT,
        name="choose",
    )(wanted, other, own, *earlier)


def sum_kernel(a, b, c, d, *refs):
    total = a[...].astype(jnp.float32) + b[...].astype(jnp.float32)
    total = total + c[...].astype(jnp.float32) + d[...].astype(jnp.float32)
    refs[-1][...] = total.astype(jnp.bfloat16)


def sum_blocks(blocks, *earlier):
    return pl.pallas_call(
        sum_kernel,
        in_specs=[pl.BlockSpec(memory_space=pltpu.VMEM) for _ in blocks]
        + [pl.BlockSpec(memory_space=pl.ANY) for _ in earlier],
        out_specs=pl.BlockSpec(memory_space=pltpu.VMEM),
        out_shape=jax.ShapeDtypeStruct(blocks[0].shape, jnp.bfloat16),
        compiler_params=params(60),
        cost_estimate=LIGHT,
        name="sum",
    )(*blocks, *earlier)


def plan_kernel(cap, top, ids_here, m0, m1, m2, m3, *refs):
    slot_ref, weight_ref = refs[-2:]
    rows = m0.shape[0]
    before = lax.broadcasted_iota(jnp.int32, (rows, rows), 0)
    after = lax.broadcasted_iota(jnp.int32, (rows, rows), 1)
    earlier = (before < after).astype(jnp.float32).astype(jnp.bfloat16)
    wanted = ids_here[...]
    for s, block in enumerate((m0, m1, m2, m3)):
        meta = block[...].astype(jnp.float32).T
        scale = meta[8:16, :] + meta[24:32, :] + meta[40:48, :]
        named = jnp.zeros(wanted.shape, jnp.float32)
        weight = jnp.zeros(wanted.shape, jnp.float32)
        for k in range(top):
            same = (meta[k : k + 1, :] == wanted).astype(jnp.float32)
            named = named + same
            weight = weight + same * scale[k : k + 1, :]
        rank = jnp.dot(named.astype(jnp.bfloat16), earlier, preferred_element_type=jnp.float32)
        slot = jnp.where(named > 0.5, rank + float(s * cap), -1.0)
        slot_ref[:, s * rows : (s + 1) * rows] = slot
        weight_ref[:, s * rows : (s + 1) * rows] = weight


def make_plan(cap, top, ids_here, parts, *earlier):
    rows, width = parts[0].shape
    last = width // 128 - 1
    out = jax.ShapeDtypeStruct((ids_here.shape[0], 4 * rows), jnp.float32)
    whole = pl.BlockSpec(out.shape, lambda i: (0, 0))
    return pl.pallas_call(
        lambda *refs: plan_kernel(cap, top, *refs),
        grid=(1,),
        in_specs=[pl.BlockSpec(ids_here.shape, lambda i: (0, 0))]
        + [pl.BlockSpec((rows, 128), lambda i: (0, last)) for _ in parts]
        + [pl.BlockSpec(memory_space=pl.ANY) for _ in earlier],
        out_specs=(whole, whole),
        out_shape=(out, out),
        compiler_params=params(60, "arbitrary"),
        cost_estimate=LIGHT,
        name="plan",
    )(ids_here, *parts, *earlier)


def select_kernel(scaled, slots, weights, t0, t1, t2, t3, *refs):
    *outs, pick, scale = refs
    tokens = slots.shape[1]
    block = pick.shape[0] // 8
    base = 8 if scaled else 0

    @pl.when(pl.program_id(0) == 0)
    def _():
        place = lax.broadcasted_iota(jnp.int32, (block, tokens), 0).astype(jnp.float32)
        for d in range(8):
            hit = (slots[base + d : base + d + 1, :] == place).astype(jnp.float32)
            pick[d * block : (d + 1) * block, :] = hit.astype(jnp.bfloat16)
            if scaled:
                row = jnp.sum(hit * weights[base + d : base + d + 1, :], axis=1, keepdims=True)
                scale[d * block : (d + 1) * block, :] = jnp.broadcast_to(row, (block, 128))

    source = jnp.concatenate([t0[...], t1[...], t2[...], t3[...]], axis=0)
    rows = jnp.dot(pick[...], source, preferred_element_type=jnp.float32)
    if scaled:
        rows = (rows * scale[:, 0:1]).astype(jnp.bfloat16)
        for k, out in enumerate(outs[-4:]):
            out[...] = rows[2 * k * block : 2 * (k + 1) * block, :]
    else:
        outs[-1][...] = rows.astype(jnp.bfloat16).reshape(8, block, -1)


def select_rows(scaled, cap, plan, parts, first, width, *earlier):
    slots, weights = plan
    rows = parts[0].shape[0]
    block = 4 * cap
    tile = 256 if width % 512 else 512
    offset = first // tile
    whole = pl.BlockSpec(slots.shape, lambda j: (0, 0))
    if scaled:
        out_spec = (pl.BlockSpec((2 * block, tile), lambda j: (0, j)),) * 4
        out_shape = (jax.ShapeDtypeStruct((2 * block, width), jnp.bfloat16),) * 4
    else:
        out_spec = pl.BlockSpec((8, block, tile), lambda j: (0, 0, j))
        out_shape = jax.ShapeDtypeStruct((8, block, width), jnp.bfloat16)
    return pl.pallas_call(
        lambda *refs: select_kernel(scaled, *refs),
        grid=(width // tile,),
        in_specs=[whole, whole]
        + [pl.BlockSpec((rows, tile), lambda j: (0, j + offset)) for _ in range(4)]
        + [pl.BlockSpec(memory_space=pl.ANY) for _ in earlier],
        out_specs=out_spec,
        out_shape=out_shape,
        scratch_shapes=[
            pltpu.VMEM((8 * block, 4 * rows), jnp.bfloat16),
            pltpu.VMEM((8 * block, 128), jnp.float32),
        ],
        compiler_params=params(60, "arbitrary"),
        cost_estimate=LIGHT,
        name="select_scaled" if scaled else "select",
    )(slots, weights, *parts, *earlier)


def hidden_kernel(count, where, *refs):
    xs, (gate_w, up_w), (fixed, turned, held) = refs[:count], refs[count : count + 2], refs[-3:]
    step, tile = pl.program_id(0), gate_w.shape[1]
    steps, features = held.shape[0], fixed.shape[1]
    gate, up, first = None, None, 0
    for x in xs:
        rows = x[...].reshape(-1, x.shape[2])
        part = slice(first, first + x.shape[2])
        first += x.shape[2]
        g = jnp.dot(rows, gate_w[part, :], preferred_element_type=jnp.float32)
        u = jnp.dot(rows, up_w[part, :], preferred_element_type=jnp.float32)
        gate, up = (g, u) if gate is None else (gate + g, up + u)
    held[step] = (gate / (1.0 + jnp.exp(-gate)) * up).astype(jnp.bfloat16)

    @pl.when(step == steps - 1)
    def _():
        shard = features // (N_Y * N_ZH)
        column = lax.broadcasted_iota(jnp.int32, (tile, features), 1)
        row = lax.broadcasted_iota(jnp.int32, (tile, features), 0)
        number = column // shard
        zh = (where[1] + number % 2) % N_ZH
        y = (where[0] + number // 2) % N_Y
        origin = (y * N_ZH + zh) * shard + (column - number * shard)
        total = None
        for s in range(steps):
            fixed[:, s * tile : (s + 1) * tile] = held[s]
            move = (row + s * tile == origin).astype(jnp.float32).astype(jnp.bfloat16)
            part = jnp.dot(held[s], move, preferred_element_type=jnp.float32)
            total = part if total is None else total + part
        turned[...] = total.astype(jnp.bfloat16)


def hidden_rows(where, xs, gate_weight, up_weight, earlier):
    depth, features = gate_weight.shape
    count = xs[0].shape[0] * xs[0].shape[1]
    tile = 256
    steps = features // tile
    return pl.pallas_call(
        lambda *refs: hidden_kernel(len(xs), *refs),
        grid=(steps,),
        in_specs=[pl.BlockSpec(memory_space=pltpu.SMEM)]
        + [pl.BlockSpec(x.shape, lambda j: (0, 0, 0)) for x in xs]
        + [pl.BlockSpec((depth, tile), lambda j: (0, j)) for _ in range(2)]
        + [pl.BlockSpec(memory_space=pl.ANY) for _ in earlier],
        out_specs=(pl.BlockSpec((count, features), lambda j: (0, 0)),) * 2,
        out_shape=(jax.ShapeDtypeStruct((count, features), jnp.bfloat16),) * 2,
        scratch_shapes=[pltpu.VMEM((steps, count, tile), jnp.bfloat16)],
        compiler_params=params(60, "arbitrary"),
        name="hidden",
    )(where, *xs, gate_weight, up_weight, *earlier)


def down_kernel(hidden, down, *refs):
    out = refs[-1]
    rows = jnp.dot(hidden[...], down[...], preferred_element_type=jnp.float32)
    out[...] = rows.astype(jnp.bfloat16).reshape(out.shape)


def down_rows(hidden, down, cap, first, width, *earlier):
    tile = 256 if width % 512 else 512
    offset = first // tile
    block = 4 * cap
    return pl.pallas_call(
        down_kernel,
        grid=(width // tile,),
        in_specs=[pl.BlockSpec(hidden.shape, lambda j: (0, 0))]
        + [pl.BlockSpec((down.shape[0], tile), lambda j: (0, j + offset))]
        + [pl.BlockSpec(memory_space=pl.ANY) for _ in earlier],
        out_specs=pl.BlockSpec((8, block, tile), lambda j: (0, 0, j)),
        out_shape=jax.ShapeDtypeStruct((8, block, width), jnp.bfloat16),
        compiler_params=params(60, "arbitrary"),
        name="down",
    )(hidden, down, *earlier)


def grad_kernel(where, hidden, *refs):
    rows, outs, turned = refs[:5], refs[-5:-1], refs[-1]
    block = rows[0].shape[0]

    @pl.when(pl.program_id(0) == 0)
    def _():
        parts = []
        for k in range(8):
            source = (where[2] + N_X - k % 4) % N_X * 2 + (where[3] + k // 4) % 2
            parts.append(hidden[pl.ds(pl.multiple_of(source * block, 16), block), :])
        turned[...] = jnp.concatenate(parts, axis=0).T

    value = jnp.concatenate([r[...] for r in rows], axis=0)
    grad = jnp.dot(turned[...], value, preferred_element_type=jnp.float32).astype(jnp.bfloat16)
    quarter = outs[0].shape[0]
    for k, out in enumerate(outs):
        out[...] = grad[k * quarter : (k + 1) * quarter, :]


def grad_blocks(where, hidden, rows, first, width, *earlier):
    block = rows[0].shape[0] // 2
    tile = 256 if width % 512 else 512
    offset = first // tile
    quarter = hidden.shape[1] // N_Y
    spec = pl.BlockSpec((quarter, tile), lambda j: (0, j))
    out = jax.ShapeDtypeStruct((quarter, width), jnp.bfloat16)
    return pl.pallas_call(
        grad_kernel,
        grid=(width // tile,),
        in_specs=[
            pl.BlockSpec(memory_space=pltpu.SMEM),
            pl.BlockSpec(hidden.shape, lambda j: (0, 0)),
        ]
        + [pl.BlockSpec((block, tile), lambda j: (0, j + offset)) for _ in range(4)]
        + [pl.BlockSpec((4 * block, tile), lambda j: (0, j + offset))]
        + [pl.BlockSpec(memory_space=pl.ANY) for _ in earlier],
        out_specs=(spec,) * 4,
        out_shape=(out,) * 4,
        scratch_shapes=[pltpu.VMEM(hidden.shape[::-1], jnp.bfloat16)],
        compiler_params=params(60, "arbitrary"),
        name="grad",
    )(where, hidden, *rows, *earlier)


def combine_kernel(slots, weights, rows, o0, o1, o2, o3, high, low):
    dests, block, width = rows.shape
    tokens = slots.shape[1]

    @pl.when(pl.program_id(0) == 0)
    def _():
        place = lax.broadcasted_iota(jnp.int32, (block, tokens), 0).astype(jnp.float32)
        picked = []
        for d in range(dests):
            hit = (slots[d : d + 1, :] == place).astype(jnp.float32)
            picked.append(hit * weights[d : d + 1, :])
        pick = jnp.concatenate(picked, axis=0).T
        coarse = pick.astype(jnp.bfloat16)
        high[...] = coarse
        low[...] = (pick - coarse.astype(jnp.float32)).astype(jnp.bfloat16)

    value = rows[...].reshape(-1, width)
    total = jnp.dot(high[...], value, preferred_element_type=jnp.float32)
    total = total + jnp.dot(low[...], value, preferred_element_type=jnp.float32)
    count = o0.shape[0]
    for s, out in enumerate((o0, o1, o2, o3)):
        out[...] = total[s * count : (s + 1) * count, :].astype(out.dtype)


def combine_rows(plan, rows):
    slots, weights = plan
    width = rows.shape[2]
    tile = 256 if width % 512 else 512
    count = slots.shape[1] // 4
    whole = pl.BlockSpec((8, slots.shape[1]), lambda j: (0, 0))
    spec = pl.BlockSpec((count, tile), lambda j: (0, j))
    return pl.pallas_call(
        combine_kernel,
        grid=(width // tile,),
        in_specs=[whole, whole, pl.BlockSpec((*rows.shape[:2], tile), lambda j: (0, 0, j))],
        out_specs=(spec,) * 4,
        out_shape=tuple(
            jax.ShapeDtypeStruct((count, width), t)
            for t in (jnp.float32, jnp.bfloat16, jnp.bfloat16, jnp.bfloat16)
        ),
        scratch_shapes=[
            pltpu.VMEM((slots.shape[1], rows.shape[0] * rows.shape[1]), jnp.bfloat16)
            for _ in range(2)
        ],
        compiler_params=params(60, "arbitrary"),
        name="combine",
    )(slots, weights, rows)


def plane_permute(blocks):
    out = [blocks[0]]
    for k in range(1, N_X):
        out.append(permute(blocks[k], lambda y, z, x, c, k=k: (y, z, x + k, c)))
    return out


def core_permute(blocks, *earlier):
    passed = hold(blocks, *earlier, start=blocks[0].shape[0] // 2)
    return permute(passed, lambda y, z, x, c: (y, z, x, c + 1))


def plane_exchange(rows):
    return lax.all_to_all(rows, ("x", "c"), split_axis=0, concat_axis=0, tiled=True)


def z_return(own, near, other, far):
    step = z_down(far).astype(jnp.float32) + near.astype(jnp.float32)
    from_near = z_down(step.astype(jnp.bfloat16))
    from_other = z_up(other)
    total = own + from_near.astype(jnp.float32) + from_other.astype(jnp.float32)
    return total.astype(jnp.bfloat16)


def y_move(array, k):
    return permute(array, lambda y, z, x, c: (y + k, z, x, c))


def adam(grad, weight, first, second):
    weight_old = weight.astype(jnp.float32)
    moment_one = first_decay_rate * first.astype(jnp.float32) + (1.0 - first_decay_rate) * grad
    moment_two = beta_two * second.astype(jnp.float32) + (1.0 - beta_two) * grad * grad
    updated = weight_old - learn_rate * moment_one / (jnp.sqrt(moment_two) + adam_eps)
    return tuple(v.astype(jnp.bfloat16)[None] for v in (updated, moment_one, moment_two))


def local(
    tokens,
    expert_ids,
    route_weight,
    placement,
    swap_mask,
    gate_weight,
    up_weight,
    down_weight,
    first_moment,
    second_moment,
    out_grad,
):
    tok_rows, top = expert_ids.shape
    width = tokens.shape[1]
    experts = placement.shape[0]
    cap = tok_rows * top * 7 // (6 * experts)
    jumps = range(2 ** (SWAP_BITS - 1))
    jump = jnp.clip(swap_mask[0] // 2, 0, len(jumps) - 1)
    bits = [swap_mask // 2**bit % 2 for bit in range(SWAP_BITS)]

    where = [lax.axis_index(a) for a in ("y", "zh", "x", "c")]
    where = jnp.stack(where).astype(jnp.int32)

    dest = jnp.arange(8, dtype=jnp.int32)
    ring = (where[2] + dest // 2) % N_X * 2 + (where[3] + dest) % 2
    dest = jnp.concatenate([dest, ring])
    held_at = (dest // 2) * 8 + lax.axis_index("zl") * 2 + dest % 2
    ids = jnp.arange(experts, dtype=jnp.int32)
    here = jnp.sum(jnp.where(placement[None, :] == held_at[:, None], ids[None, :], 0), axis=1)
    here = jnp.broadcast_to(here.astype(jnp.float32)[:, None], (16, tok_rows))
    numbers = jnp.pad(expert_ids.astype(jnp.float32), ((0, 0), (0, 128 - top)))
    meta = numbers + jnp.pad(route_weight, ((0, 0), (8, 120 - top)))

    x_parts = z_gather(mark(tokens, meta))
    state = hold((down_weight[0], first_moment[0], second_moment[0]))
    far_state = swap(state, x=1)
    plan = make_plan(cap, top, here, x_parts, far_state)
    x_send = select_rows(False, cap, plan, x_parts, 0, width)
    x_rows = plane_exchange(x_send)
    g_parts = z_gather(hold((out_grad,), plan[0]))
    state = choose(bits[3], far_state, state, x_send)
    state_cores = choose(bits[0], swap(state, c=1), state, *g_parts[2:])
    state_far = swap(state_cores, zl=2)

    g_send = select_rows(True, cap, plan, g_parts, 0, width, x_rows, state_cores)
    g_rows = plane_permute(g_send)

    down_full = lax.all_gather(hold((down_weight[0],), plan[0]), ("y", "zh"), axis=0, tiled=True)

    hidden, turned = hidden_rows(where, [x_rows], gate_weight[0], up_weight[0], g_send[3:])
    r_send = down_rows(hidden, down_full, cap, 0, width)
    returned = plane_exchange(r_send)
    state_far = choose(bits[2], state_far, state_cores, r_send)
    state = choose(bits[1], swap(state_far, zl=1), state_far)

    g_rows = (*g_rows, core_permute(g_rows, state_far))
    grads, blocks, chunk = [], (r_send,), width // G_CHUNKS
    for i in range(G_CHUNKS):
        blocks = grad_blocks(where, turned, g_rows, i * chunk, chunk, blocks[0])
        blocks = [blocks[0]] + [y_move(blocks[k], k) for k in (1, 2, 3)]
        total = sum_blocks(blocks, state, *((grads[-1], returned) if grads else ()))
        total = choose(bits[0], swap(total, c=1), total)
        rows = total.shape[0] // 2
        mine, theirs = lax.switch(
            jump,
            [lambda a, b, m=m: (relocate(a, m), relocate(b, m, True)) for m in jumps],
            total[:rows],
            total[rows:],
        )
        grads.append(mine.astype(jnp.float32) + theirs.astype(jnp.float32))
    new_state = adam(jnp.concatenate(grads, axis=1), *jnp.split(state, 3, axis=0))

    layer_out = z_return(*combine_rows(plan, returned))
    return (layer_out, *new_state)


def solution(mesh):
    fine = Mesh(mesh.devices.reshape(N_Y, N_ZH, N_X, N_ZL, N_C), AXES)
    dp, expert = ("y", "zh"), ("x", "zl", "c")
    batch, weight, state = P(dp + expert, None), P(expert, None, None), P(expert, dp, None)
    return jax.shard_map(
        local,
        mesh=fine,
        in_specs=(batch,) * 3 + (P(), P()) + (weight,) * 2 + (state,) * 3 + (batch,),
        out_specs=(batch, state, state, state),
        check_vma=False,
    )
```

```python
import jax
import jax.numpy as jnp
from jax import lax
from jax.experimental import pallas as pl
from jax.experimental.pallas import tpu as pltpu
from jax.sharding import Mesh, PartitionSpec as P

SWAP_BITS = 4
N_Y, N_ZH, N_X, N_ZL, N_C = 4, 2, 4, 4, 2
AXES = ("y", "zh", "x", "zl", "c")
MIB = 1024 * 1024

first_decay_rate = 0.9
beta_two = 0.95
learn_rate = 0.003
adam_eps = 1e-08

G_CHUNKS = 2


def flat_index(y, z, x, c):
    z = z % 8
    return ((((y % 4) * N_ZH + z // N_ZL) * N_X + x % 4) * N_ZL + z % N_ZL) * N_C + c % 2


def permute(array, move):
    pairs = []
    for y in range(N_Y):
        for z in range(8):
            for x in range(N_X):
                for c in range(N_C):
                    pairs.append((flat_index(y, z, x, c), flat_index(*move(y, z, x, c))))
    return lax.ppermute(array, AXES, pairs)


def along(c):
    return 1 if c == 0 else -1


def z_up(array):
    return permute(array, lambda y, z, x, c: (y, z + along(c), x, c))


def z_down(array):
    return permute(array, lambda y, z, x, c: (y, z - along(c), x, c))


def z_gather(array):
    near = z_up(array)
    other = z_down(array)
    far = z_up(near)
    return array, near, other, far


def swap(array, zl=0, x=0, c=0):
    return permute(array, lambda y, z, i, j: (y, z ^ zl, i ^ x, j ^ c))


def relocate(array, jump, flip_zh=False):
    if jump == 0 and not flip_zh:
        return array

    def move(y, z, x, c):
        zl = (z % 4) ^ (jump & 3)
        zh = z // 4 ^ (1 if flip_zh else 0)
        return y, zh * 4 + zl, x ^ (jump >> 2), c

    return permute(array, move)


LIGHT = pl.CostEstimate(flops=1, bytes_accessed=1, transcendentals=0)


def params(mib, *semantics):
    return pltpu.CompilerParams(
        dimension_semantics=semantics or None, vmem_limit_bytes=mib * MIB
    )


def hold_kernel(count, start, *refs):
    out, first = refs[-1], 0
    for array in refs[:count]:
        rows = array.shape[0] - start
        out[first : first + rows, :] = array[start:, :]
        first += rows


def hold(arrays, *earlier, start=0):
    rows, width = sum(a.shape[0] - start for a in arrays), arrays[0].shape[1]
    return pl.pallas_call(
        lambda *refs: hold_kernel(len(arrays), start, *refs),
        in_specs=[pl.BlockSpec(memory_space=pltpu.VMEM) for _ in arrays]
        + [pl.BlockSpec(memory_space=pl.ANY) for _ in earlier],
        out_specs=pl.BlockSpec(memory_space=pltpu.VMEM),
        out_shape=jax.ShapeDtypeStruct((rows, width), arrays[0].dtype),
        compiler_params=params(60),
        cost_estimate=LIGHT,
        name="hold",
    )(*arrays, *earlier)


def mark_kernel(tokens, meta, out):
    width = tokens.shape[1]
    out[:, :width] = tokens[...]
    left = meta[...]
    total = None
    for turn in range(3):
        part = left.astype(jnp.bfloat16).astype(jnp.float32)
        left = left - part
        part = pltpu.roll(part, 16 * turn, 1) if turn else part
        total = part if total is None else total + part
    out[:, width:] = total.astype(jnp.bfloat16)


def mark(tokens, meta):
    rows, width = tokens.shape
    return pl.pallas_call(
        mark_kernel,
        in_specs=[pl.BlockSpec(memory_space=pltpu.VMEM)] * 2,
        out_specs=pl.BlockSpec(memory_space=pltpu.VMEM),
        out_shape=jax.ShapeDtypeStruct((rows, width + 128), jnp.bfloat16),
        compiler_params=params(60),
        cost_estimate=LIGHT,
        name="mark",
    )(tokens, meta)


def choose_kernel(wanted, other, own, *refs):
    @pl.when(wanted[0] == 1)
    def _():
        refs[-1][...] = other[...]

    @pl.when(wanted[0] != 1)
    def _():
        refs[-1][...] = own[...]


def choose(wanted, other, own, *earlier):
    return pl.pallas_call(
        choose_kernel,
        in_specs=[pl.BlockSpec(memory_space=pltpu.SMEM)]
        + [pl.BlockSpec(memory_space=pltpu.VMEM) for _ in range(2)]
        + [pl.BlockSpec(memory_space=pl.ANY) for _ in earlier],
        out_specs=pl.BlockSpec(memory_space=pltpu.VMEM),
        out_shape=jax.ShapeDtypeStruct(own.shape, own.dtype),
        compiler_params=params(60),
        cost_estimate=LIGHT,
        name="choose",
    )(wanted, other, own, *earlier)


def sum_kernel(a, b, c, d, *refs):
    total = a[...].astype(jnp.float32) + b[...].astype(jnp.float32)
    total = total + c[...].astype(jnp.float32) + d[...].astype(jnp.float32)
    refs[-1][...] = total.astype(jnp.bfloat16)


def sum_blocks(blocks, *earlier):
    return pl.pallas_call(
        sum_kernel,
        in_specs=[pl.BlockSpec(memory_space=pltpu.VMEM) for _ in blocks]
        + [pl.BlockSpec(memory_space=pl.ANY) for _ in earlier],
        out_specs=pl.BlockSpec(memory_space=pltpu.VMEM),
        out_shape=jax.ShapeDtypeStruct(blocks[0].shape, jnp.bfloat16),
        compiler_params=params(60),
        cost_estimate=LIGHT,
        name="sum",
    )(*blocks, *earlier)


def plan_kernel(cap, top, ids_here, m0, m1, m2, m3, *refs):
    slot_ref, weight_ref = refs[-2:]
    rows = m0.shape[0]
    before = lax.broadcasted_iota(jnp.int32, (rows, rows), 0)
    after = lax.broadcasted_iota(jnp.int32, (rows, rows), 1)
    earlier = (before < after).astype(jnp.float32).astype(jnp.bfloat16)
    wanted = ids_here[...]
    for s, block in enumerate((m0, m1, m2, m3)):
        meta = block[...].astype(jnp.float32).T
        scale = meta[8:16, :] + meta[24:32, :] + meta[40:48, :]
        named = jnp.zeros(wanted.shape, jnp.float32)
        weight = jnp.zeros(wanted.shape, jnp.float32)
        for k in range(top):
            same = (meta[k : k + 1, :] == wanted).astype(jnp.float32)
            named = named + same
            weight = weight + same * scale[k : k + 1, :]
        rank = jnp.dot(named.astype(jnp.bfloat16), earlier, preferred_element_type=jnp.float32)
        slot = jnp.where(named > 0.5, rank + float(s * cap), -1.0)
        slot_ref[:, s * rows : (s + 1) * rows] = slot
        weight_ref[:, s * rows : (s + 1) * rows] = weight


def make_plan(cap, top, ids_here, parts, *earlier):
    rows, width = parts[0].shape
    last = width // 128 - 1
    out = jax.ShapeDtypeStruct((ids_here.shape[0], 4 * rows), jnp.float32)
    whole = pl.BlockSpec(out.shape, lambda i: (0, 0))
    return pl.pallas_call(
        lambda *refs: plan_kernel(cap, top, *refs),
        grid=(1,),
        in_specs=[pl.BlockSpec(ids_here.shape, lambda i: (0, 0))]
        + [pl.BlockSpec((rows, 128), lambda i: (0, last)) for _ in parts]
        + [pl.BlockSpec(memory_space=pl.ANY) for _ in earlier],
        out_specs=(whole, whole),
        out_shape=(out, out),
        compiler_params=params(60, "arbitrary"),
        cost_estimate=LIGHT,
        name="plan",
    )(ids_here, *parts, *earlier)


def select_kernel(scaled, slots, weights, t0, t1, t2, t3, *refs):
    *outs, pick, scale = refs
    tokens = slots.shape[1]
    block = pick.shape[0] // 8
    base = 8 if scaled else 0

    @pl.when(pl.program_id(0) == 0)
    def _():
        place = lax.broadcasted_iota(jnp.int32, (block, tokens), 0).astype(jnp.float32)
        for d in range(8):
            hit = (slots[base + d : base + d + 1, :] == place).astype(jnp.float32)
            pick[d * block : (d + 1) * block, :] = hit.astype(jnp.bfloat16)
            if scaled:
                row = jnp.sum(hit * weights[base + d : base + d + 1, :], axis=1, keepdims=True)
                scale[d * block : (d + 1) * block, :] = jnp.broadcast_to(row, (block, 128))

    source = jnp.concatenate([t0[...], t1[...], t2[...], t3[...]], axis=0)
    rows = jnp.dot(pick[...], source, preferred_element_type=jnp.float32)
    if scaled:
        rows = (rows * scale[:, 0:1]).astype(jnp.bfloat16)
        for k, out in enumerate(outs[-4:]):
            out[...] = rows[2 * k * block : 2 * (k + 1) * block, :]
    else:
        outs[-1][...] = rows.astype(jnp.bfloat16).reshape(8, block, -1)


def select_rows(scaled, cap, plan, parts, first, width, *earlier):
    slots, weights = plan
    rows = parts[0].shape[0]
    block = 4 * cap
    tile = 256 if width % 512 else 512
    offset = first // tile
    whole = pl.BlockSpec(slots.shape, lambda j: (0, 0))
    if scaled:
        out_spec = (pl.BlockSpec((2 * block, tile), lambda j: (0, j)),) * 4
        out_shape = (jax.ShapeDtypeStruct((2 * block, width), jnp.bfloat16),) * 4
    else:
        out_spec = pl.BlockSpec((8, block, tile), lambda j: (0, 0, j))
        out_shape = jax.ShapeDtypeStruct((8, block, width), jnp.bfloat16)
    return pl.pallas_call(
        lambda *refs: select_kernel(scaled, *refs),
        grid=(width // tile,),
        in_specs=[whole, whole]
        + [pl.BlockSpec((rows, tile), lambda j: (0, j + offset)) for _ in range(4)]
        + [pl.BlockSpec(memory_space=pl.ANY) for _ in earlier],
        out_specs=out_spec,
        out_shape=out_shape,
        scratch_shapes=[
            pltpu.VMEM((8 * block, 4 * rows), jnp.bfloat16),
            pltpu.VMEM((8 * block, 128), jnp.float32),
        ],
        compiler_params=params(60, "arbitrary"),
        cost_estimate=LIGHT,
        name="select_scaled" if scaled else "select",
    )(slots, weights, *parts, *earlier)


def hidden_kernel(count, where, *refs):
    xs, (gate_w, up_w), (out, held) = refs[:count], refs[count : count + 2], refs[-2:]
    step, tile = pl.program_id(0), gate_w.shape[1]
    steps, features = held.shape[0], out.shape[1]
    gate, up, first = None, None, 0
    for x in xs:
        rows = x[...].reshape(-1, x.shape[2])
        part = slice(first, first + x.shape[2])
        first += x.shape[2]
        g = jnp.dot(rows, gate_w[part, :], preferred_element_type=jnp.float32)
        u = jnp.dot(rows, up_w[part, :], preferred_element_type=jnp.float32)
        gate, up = (g, u) if gate is None else (gate + g, up + u)
    held[step] = (gate / (1.0 + jnp.exp(-gate)) * up).astype(jnp.bfloat16)

    @pl.when(step == steps - 1)
    def _():
        shard = features // (N_Y * N_ZH)
        column = lax.broadcasted_iota(jnp.int32, (tile, features), 1)
        row = lax.broadcasted_iota(jnp.int32, (tile, features), 0)
        number = column // shard
        zh = (where[1] + number % 2) % N_ZH
        y = (where[0] + number // 2) % N_Y
        origin = (y * N_ZH + zh) * shard + (column - number * shard)
        total = None
        for s in range(steps):
            move = (row + s * tile == origin).astype(jnp.float32).astype(jnp.bfloat16)
            part = jnp.dot(held[s], move, preferred_element_type=jnp.float32)
            total = part if total is None else total + part
        out[...] = total.astype(jnp.bfloat16)


def hidden_rows(where, xs, gate_weight, up_weight, earlier):
    depth, features = gate_weight.shape
    count = xs[0].shape[0] * xs[0].shape[1]
    tile = 256
    steps = features // tile
    return pl.pallas_call(
        lambda *refs: hidden_kernel(len(xs), *refs),
        grid=(steps,),
        in_specs=[pl.BlockSpec(memory_space=pltpu.SMEM)]
        + [pl.BlockSpec(x.shape, lambda j: (0, 0, 0)) for x in xs]
        + [pl.BlockSpec((depth, tile), lambda j: (0, j)) for _ in range(2)]
        + [pl.BlockSpec(memory_space=pl.ANY) for _ in earlier],
        out_specs=pl.BlockSpec((count, features), lambda j: (0, 0)),
        out_shape=jax.ShapeDtypeStruct((count, features), jnp.bfloat16),
        scratch_shapes=[pltpu.VMEM((steps, count, tile), jnp.bfloat16)],
        compiler_params=params(60, "arbitrary"),
        name="hidden",
    )(where, *xs, gate_weight, up_weight, *earlier)


def down_kernel(hidden, d0, d1, d2, d3, out):
    weight = jnp.concatenate([d0[...], d1[...], d2[...], d3[...]], axis=0)
    rows = jnp.dot(hidden[...], weight, preferred_element_type=jnp.float32)
    out[...] = rows.astype(jnp.bfloat16).reshape(out.shape)


def down_rows(hidden, downs, cap, first, width):
    tile = 256 if width % 512 else 512
    offset = first // tile
    block = 4 * cap
    return pl.pallas_call(
        down_kernel,
        grid=(width // tile,),
        in_specs=[pl.BlockSpec(hidden.shape, lambda j: (0, 0))]
        + [pl.BlockSpec((d.shape[0], tile), lambda j: (0, j + offset)) for d in downs],
        out_specs=pl.BlockSpec((8, block, tile), lambda j: (0, 0, j)),
        out_shape=jax.ShapeDtypeStruct((8, block, width), jnp.bfloat16),
        compiler_params=params(60, "arbitrary"),
        name="down",
    )(hidden, *downs)


def grad_kernel(where, hidden, *refs):
    rows, outs, turned = refs[:5], refs[-5:-1], refs[-1]
    block = rows[0].shape[0]

    @pl.when(pl.program_id(0) == 0)
    def _():
        parts = []
        for k in range(8):
            source = (where[2] + N_X - k % 4) % N_X * 2 + (where[3] + k // 4) % 2
            parts.append(hidden[pl.ds(pl.multiple_of(source * block, 16), block), :])
        turned[...] = jnp.concatenate(parts, axis=0).T

    value = jnp.concatenate([r[...] for r in rows], axis=0)
    grad = jnp.dot(turned[...], value, preferred_element_type=jnp.float32).astype(jnp.bfloat16)
    quarter = outs[0].shape[0]
    for k, out in enumerate(outs):
        out[...] = grad[k * quarter : (k + 1) * quarter, :]


def grad_blocks(where, hidden, rows, first, width, *earlier):
    block = rows[0].shape[0] // 2
    tile = 256 if width % 512 else 512
    offset = first // tile
    quarter = hidden.shape[1] // N_Y
    spec = pl.BlockSpec((quarter, tile), lambda j: (0, j))
    out = jax.ShapeDtypeStruct((quarter, width), jnp.bfloat16)
    return pl.pallas_call(
        grad_kernel,
        grid=(width // tile,),
        in_specs=[
            pl.BlockSpec(memory_space=pltpu.SMEM),
            pl.BlockSpec(hidden.shape, lambda j: (0, 0)),
        ]
        + [pl.BlockSpec((block, tile), lambda j: (0, j + offset)) for _ in range(4)]
        + [pl.BlockSpec((4 * block, tile), lambda j: (0, j + offset))]
        + [pl.BlockSpec(memory_space=pl.ANY) for _ in earlier],
        out_specs=(spec,) * 4,
        out_shape=(out,) * 4,
        scratch_shapes=[pltpu.VMEM(hidden.shape[::-1], jnp.bfloat16)],
        compiler_params=params(60, "arbitrary"),
        name="grad",
    )(where, hidden, *rows, *earlier)


def combine_kernel(slots, weights, rows, o0, o1, o2, o3, high, low):
    dests, block, width = rows.shape
    tokens = slots.shape[1]

    @pl.when(pl.program_id(0) == 0)
    def _():
        place = lax.broadcasted_iota(jnp.int32, (block, tokens), 0).astype(jnp.float32)
        picked = []
        for d in range(dests):
            hit = (slots[d : d + 1, :] == place).astype(jnp.float32)
            picked.append(hit * weights[d : d + 1, :])
        pick = jnp.concatenate(picked, axis=0).T
        coarse = pick.astype(jnp.bfloat16)
        high[...] = coarse
        low[...] = (pick - coarse.astype(jnp.float32)).astype(jnp.bfloat16)

    value = rows[...].reshape(-1, width)
    total = jnp.dot(high[...], value, preferred_element_type=jnp.float32)
    total = total + jnp.dot(low[...], value, preferred_element_type=jnp.float32)
    count = o0.shape[0]
    for s, out in enumerate((o0, o1, o2, o3)):
        out[...] = total[s * count : (s + 1) * count, :].astype(out.dtype)


def combine_rows(plan, rows):
    slots, weights = plan
    width = rows.shape[2]
    tile = 256 if width % 512 else 512
    count = slots.shape[1] // 4
    whole = pl.BlockSpec((8, slots.shape[1]), lambda j: (0, 0))
    spec = pl.BlockSpec((count, tile), lambda j: (0, j))
    return pl.pallas_call(
        combine_kernel,
        grid=(width // tile,),
        in_specs=[whole, whole, pl.BlockSpec((*rows.shape[:2], tile), lambda j: (0, 0, j))],
        out_specs=(spec,) * 4,
        out_shape=tuple(
            jax.ShapeDtypeStruct((count, width), t)
            for t in (jnp.float32, jnp.bfloat16, jnp.bfloat16, jnp.bfloat16)
        ),
        scratch_shapes=[
            pltpu.VMEM((slots.shape[1], rows.shape[0] * rows.shape[1]), jnp.bfloat16)
            for _ in range(2)
        ],
        compiler_params=params(60, "arbitrary"),
        name="combine",
    )(slots, weights, rows)


def plane_permute(blocks):
    out = [blocks[0]]
    for k in range(1, N_X):
        out.append(permute(blocks[k], lambda y, z, x, c, k=k: (y, z, x + k, c)))
    return out


def core_permute(blocks, *earlier):
    passed = hold(blocks, *earlier, start=blocks[0].shape[0] // 2)
    return permute(passed, lambda y, z, x, c: (y, z, x, c + 1))


def plane_exchange(rows):
    return lax.all_to_all(rows, ("x", "c"), split_axis=0, concat_axis=0, tiled=True)


def z_return(own, near, other, far):
    step = z_down(far).astype(jnp.float32) + near.astype(jnp.float32)
    from_near = z_down(step.astype(jnp.bfloat16))
    from_other = z_up(other)
    total = own + from_near.astype(jnp.float32) + from_other.astype(jnp.float32)
    return total.astype(jnp.bfloat16)


def y_move(array, k):
    return permute(array, lambda y, z, x, c: (y + k, z, x, c))


def adam(grad, weight, first, second):
    weight_old = weight.astype(jnp.float32)
    moment_one = first_decay_rate * first.astype(jnp.float32) + (1.0 - first_decay_rate) * grad
    moment_two = beta_two * second.astype(jnp.float32) + (1.0 - beta_two) * grad * grad
    updated = weight_old - learn_rate * moment_one / (jnp.sqrt(moment_two) + adam_eps)
    return tuple(v.astype(jnp.bfloat16)[None] for v in (updated, moment_one, moment_two))


def local(
    tokens,
    expert_ids,
    route_weight,
    placement,
    swap_mask,
    gate_weight,
    up_weight,
    down_weight,
    first_moment,
    second_moment,
    out_grad,
):
    tok_rows, top = expert_ids.shape
    width = tokens.shape[1]
    experts = placement.shape[0]
    cap = tok_rows * top * 7 // (6 * experts)
    jumps = range(2 ** (SWAP_BITS - 1))
    jump = jnp.clip(swap_mask[0] // 2, 0, len(jumps) - 1)
    bits = [swap_mask // 2**bit % 2 for bit in range(SWAP_BITS)]

    where = [lax.axis_index(a) for a in ("y", "zh", "x", "c")]
    where = jnp.stack(where).astype(jnp.int32)

    dest = jnp.arange(8, dtype=jnp.int32)
    ring = (where[2] + dest // 2) % N_X * 2 + (where[3] + dest) % 2
    dest = jnp.concatenate([dest, ring])
    held_at = (dest // 2) * 8 + lax.axis_index("zl") * 2 + dest % 2
    ids = jnp.arange(experts, dtype=jnp.int32)
    here = jnp.sum(jnp.where(placement[None, :] == held_at[:, None], ids[None, :], 0), axis=1)
    here = jnp.broadcast_to(here.astype(jnp.float32)[:, None], (16, tok_rows))
    numbers = jnp.pad(expert_ids.astype(jnp.float32), ((0, 0), (0, 128 - top)))
    meta = numbers + jnp.pad(route_weight, ((0, 0), (8, 120 - top)))

    x_parts = z_gather(mark(tokens, meta))
    state = hold((down_weight[0], first_moment[0], second_moment[0]))
    far_state = swap(state, x=1)
    plan = make_plan(cap, top, here, x_parts, far_state)
    x_send = select_rows(False, cap, plan, x_parts, 0, width)
    x_rows = plane_exchange(x_send)
    g_parts = z_gather(hold((out_grad,), plan[0]))
    state = choose(bits[3], far_state, state, x_send)
    state_cores = choose(bits[0], swap(state, c=1), state, *g_parts[2:])
    state_far = swap(state_cores, zl=2)

    g_send = select_rows(True, cap, plan, g_parts, 0, width, x_rows, state_cores)
    g_rows = plane_permute(g_send)

    down = hold((down_weight[0],), plan[0])
    partner = permute(down, lambda y, z, x, c: (y, z + 4, x, c))
    pair = jnp.concatenate([down, partner], axis=0)
    downs = (pair, y_move(pair, -1), y_move(pair, -2), y_move(pair, 1))

    hidden = hidden_rows(where, [x_rows], gate_weight[0], up_weight[0], g_send[3:])
    r_send = down_rows(hidden, downs, cap, 0, width)
    returned = plane_exchange(r_send)
    state_far = choose(bits[2], state_far, state_cores, r_send)
    state = choose(bits[1], swap(state_far, zl=1), state_far)

    g_rows = (*g_rows, core_permute(g_rows, state_far))
    chunk = width // G_CHUNKS
    partials = [
        grad_blocks(where, hidden, g_rows, i * chunk, chunk, r_send) for i in range(G_CHUNKS)
    ]
    grads = []
    for i, blocks in enumerate(partials):
        moved = [blocks[0]] + [y_move(blocks[k], k) for k in (1, 2, 3)]
        earlier = (grads[-1], returned) if grads else (partials[-1][0],)
        total = sum_blocks(moved, state, *earlier)
        total = choose(bits[0], swap(total, c=1), total)
        rows = total.shape[0] // 2
        mine, theirs = lax.switch(
            jump,
            [lambda a, b, m=m: (relocate(a, m), relocate(b, m, True)) for m in jumps],
            total[:rows],
            total[rows:],
        )
        grads.append(mine.astype(jnp.float32) + theirs.astype(jnp.float32))
    new_state = adam(jnp.concatenate(grads, axis=1), *jnp.split(state, 3, axis=0))

    layer_out = z_return(*combine_rows(plan, returned))
    return (layer_out, *new_state)


def solution(mesh):
    fine = Mesh(mesh.devices.reshape(N_Y, N_ZH, N_X, N_ZL, N_C), AXES)
    dp, expert = ("y", "zh"), ("x", "zl", "c")
    batch, weight, state = P(dp + expert, None), P(expert, None, None), P(expert, dp, None)
    return jax.shard_map(
        local,
        mesh=fine,
        in_specs=(batch,) * 3 + (P(), P()) + (weight,) * 2 + (state,) * 3 + (batch,),
        out_specs=(batch, state, state, state),
        check_vma=False,
    )
```

```python
import jax
import jax.numpy as jnp
from jax import lax
from jax.experimental import pallas as pl
from jax.experimental.pallas import tpu as pltpu
from jax.sharding import Mesh, PartitionSpec as P

SWAP_BITS = 4
N_Y, N_ZH, N_X, N_ZL, N_C = 4, 2, 4, 4, 2
AXES = ("y", "zh", "x", "zl", "c")
MIB = 1024 * 1024

first_decay_rate = 0.9
beta_two = 0.95
learn_rate = 0.003
adam_eps = 1e-08

G_CHUNKS = 2


def flat_index(y, z, x, c):
    z = z % 8
    return ((((y % 4) * N_ZH + z // N_ZL) * N_X + x % 4) * N_ZL + z % N_ZL) * N_C + c % 2


def permute(array, move):
    pairs = []
    for y in range(N_Y):
        for z in range(8):
            for x in range(N_X):
                for c in range(N_C):
                    pairs.append((flat_index(y, z, x, c), flat_index(*move(y, z, x, c))))
    return lax.ppermute(array, AXES, pairs)


def along(c):
    return 1 if c == 0 else -1


def z_up(array):
    return permute(array, lambda y, z, x, c: (y, z + along(c), x, c))


def z_down(array):
    return permute(array, lambda y, z, x, c: (y, z - along(c), x, c))


def z_gather(array):
    near = z_up(array)
    other = z_down(array)
    far = z_up(near)
    return array, near, other, far


def swap(array, zl=0, x=0, c=0):
    return permute(array, lambda y, z, i, j: (y, z ^ zl, i ^ x, j ^ c))


def relocate(array, jump, flip_zh=False):
    if jump == 0 and not flip_zh:
        return array

    def move(y, z, x, c):
        zl = (z % 4) ^ (jump & 3)
        zh = z // 4 ^ (1 if flip_zh else 0)
        return y, zh * 4 + zl, x ^ (jump >> 2), c

    return permute(array, move)


LIGHT = pl.CostEstimate(flops=1, bytes_accessed=1, transcendentals=0)


def params(mib, *semantics):
    return pltpu.CompilerParams(
        dimension_semantics=semantics or None, vmem_limit_bytes=mib * MIB
    )


def hold_kernel(count, start, *refs):
    out, first = refs[-1], 0
    for array in refs[:count]:
        rows = array.shape[0] - start
        out[first : first + rows, :] = array[start:, :]
        first += rows


def hold(arrays, *earlier, start=0):
    rows, width = sum(a.shape[0] - start for a in arrays), arrays[0].shape[1]
    return pl.pallas_call(
        lambda *refs: hold_kernel(len(arrays), start, *refs),
        in_specs=[pl.BlockSpec(memory_space=pltpu.VMEM) for _ in arrays]
        + [pl.BlockSpec(memory_space=pl.ANY) for _ in earlier],
        out_specs=pl.BlockSpec(memory_space=pltpu.VMEM),
        out_shape=jax.ShapeDtypeStruct((rows, width), arrays[0].dtype),
        compiler_params=params(60),
        cost_estimate=LIGHT,
        name="hold",
    )(*arrays, *earlier)


def mark_kernel(tokens, meta, out):
    width = tokens.shape[1]
    out[:, :width] = tokens[...]
    left = meta[...]
    total = None
    for turn in range(3):
        part = left.astype(jnp.bfloat16).astype(jnp.float32)
        left = left - part
        part = pltpu.roll(part, 16 * turn, 1) if turn else part
        total = part if total is None else total + part
    out[:, width:] = total.astype(jnp.bfloat16)


def mark(tokens, meta):
    rows, width = tokens.shape
    return pl.pallas_call(
        mark_kernel,
        in_specs=[pl.BlockSpec(memory_space=pltpu.VMEM)] * 2,
        out_specs=pl.BlockSpec(memory_space=pltpu.VMEM),
        out_shape=jax.ShapeDtypeStruct((rows, width + 128), jnp.bfloat16),
        compiler_params=params(60),
        cost_estimate=LIGHT,
        name="mark",
    )(tokens, meta)


def choose_kernel(wanted, other, own, *refs):
    @pl.when(wanted[0] == 1)
    def _():
        refs[-1][...] = other[...]

    @pl.when(wanted[0] != 1)
    def _():
        refs[-1][...] = own[...]


def choose(wanted, other, own, *earlier):
    return pl.pallas_call(
        choose_kernel,
        in_specs=[pl.BlockSpec(memory_space=pltpu.SMEM)]
        + [pl.BlockSpec(memory_space=pltpu.VMEM) for _ in range(2)]
        + [pl.BlockSpec(memory_space=pl.ANY) for _ in earlier],
        out_specs=pl.BlockSpec(memory_space=pltpu.VMEM),
        out_shape=jax.ShapeDtypeStruct(own.shape, own.dtype),
        compiler_params=params(60),
        cost_estimate=LIGHT,
        name="choose",
    )(wanted, other, own, *earlier)


def sum_kernel(a, b, c, d, *refs):
    total = a[...].astype(jnp.float32) + b[...].astype(jnp.float32)
    total = total + c[...].astype(jnp.float32) + d[...].astype(jnp.float32)
    refs[-1][...] = total.astype(jnp.bfloat16)


def sum_blocks(blocks, *earlier):
    return pl.pallas_call(
        sum_kernel,
        in_specs=[pl.BlockSpec(memory_space=pltpu.VMEM) for _ in blocks]
        + [pl.BlockSpec(memory_space=pl.ANY) for _ in earlier],
        out_specs=pl.BlockSpec(memory_space=pltpu.VMEM),
        out_shape=jax.ShapeDtypeStruct(blocks[0].shape, jnp.bfloat16),
        compiler_params=params(60),
        cost_estimate=LIGHT,
        name="sum",
    )(*blocks, *earlier)


def plan_kernel(cap, top, ids_here, m0, m1, m2, m3, *refs):
    slot_ref, weight_ref = refs[-2:]
    rows = m0.shape[0]
    before = lax.broadcasted_iota(jnp.int32, (rows, rows), 0)
    after = lax.broadcasted_iota(jnp.int32, (rows, rows), 1)
    earlier = (before < after).astype(jnp.float32).astype(jnp.bfloat16)
    wanted = ids_here[...]
    for s, block in enumerate((m0, m1, m2, m3)):
        meta = block[...].astype(jnp.float32).T
        scale = meta[8:16, :] + meta[24:32, :] + meta[40:48, :]
        named = jnp.zeros(wanted.shape, jnp.float32)
        weight = jnp.zeros(wanted.shape, jnp.float32)
        for k in range(top):
            same = (meta[k : k + 1, :] == wanted).astype(jnp.float32)
            named = named + same
            weight = weight + same * scale[k : k + 1, :]
        rank = jnp.dot(named.astype(jnp.bfloat16), earlier, preferred_element_type=jnp.float32)
        slot = jnp.where(named > 0.5, rank + float(s * cap), -1.0)
        slot_ref[:, s * rows : (s + 1) * rows] = slot
        weight_ref[:, s * rows : (s + 1) * rows] = weight


def make_plan(cap, top, ids_here, parts, *earlier):
    rows, width = parts[0].shape
    last = width // 128 - 1
    out = jax.ShapeDtypeStruct((ids_here.shape[0], 4 * rows), jnp.float32)
    whole = pl.BlockSpec(out.shape, lambda i: (0, 0))
    return pl.pallas_call(
        lambda *refs: plan_kernel(cap, top, *refs),
        grid=(1,),
        in_specs=[pl.BlockSpec(ids_here.shape, lambda i: (0, 0))]
        + [pl.BlockSpec((rows, 128), lambda i: (0, last)) for _ in parts]
        + [pl.BlockSpec(memory_space=pl.ANY) for _ in earlier],
        out_specs=(whole, whole),
        out_shape=(out, out),
        compiler_params=params(60, "arbitrary"),
        cost_estimate=LIGHT,
        name="plan",
    )(ids_here, *parts, *earlier)


def select_kernel(scaled, slots, weights, t0, t1, t2, t3, *refs):
    *outs, pick, scale = refs
    tokens = slots.shape[1]
    block = pick.shape[0] // 8
    base = 8 if scaled else 0

    @pl.when(pl.program_id(0) == 0)
    def _():
        place = lax.broadcasted_iota(jnp.int32, (block, tokens), 0).astype(jnp.float32)
        for d in range(8):
            hit = (slots[base + d : base + d + 1, :] == place).astype(jnp.float32)
            pick[d * block : (d + 1) * block, :] = hit.astype(jnp.bfloat16)
            if scaled:
                row = jnp.sum(hit * weights[base + d : base + d + 1, :], axis=1, keepdims=True)
                scale[d * block : (d + 1) * block, :] = jnp.broadcast_to(row, (block, 128))

    source = jnp.concatenate([t0[...], t1[...], t2[...], t3[...]], axis=0)
    rows = jnp.dot(pick[...], source, preferred_element_type=jnp.float32)
    if scaled:
        rows = (rows * scale[:, 0:1]).astype(jnp.bfloat16)
        for k, out in enumerate(outs[-4:]):
            out[...] = rows[2 * k * block : 2 * (k + 1) * block, :]
    else:
        outs[-1][...] = rows.astype(jnp.bfloat16).reshape(8, block, -1)


def select_rows(scaled, cap, plan, parts, first, width, *earlier):
    slots, weights = plan
    rows = parts[0].shape[0]
    block = 4 * cap
    tile = 256 if width % 512 else 512
    offset = first // tile
    whole = pl.BlockSpec(slots.shape, lambda j: (0, 0))
    if scaled:
        out_spec = (pl.BlockSpec((2 * block, tile), lambda j: (0, j)),) * 4
        out_shape = (jax.ShapeDtypeStruct((2 * block, width), jnp.bfloat16),) * 4
    else:
        out_spec = pl.BlockSpec((8, block, tile), lambda j: (0, 0, j))
        out_shape = jax.ShapeDtypeStruct((8, block, width), jnp.bfloat16)
    return pl.pallas_call(
        lambda *refs: select_kernel(scaled, *refs),
        grid=(width // tile,),
        in_specs=[whole, whole]
        + [pl.BlockSpec((rows, tile), lambda j: (0, j + offset)) for _ in range(4)]
        + [pl.BlockSpec(memory_space=pl.ANY) for _ in earlier],
        out_specs=out_spec,
        out_shape=out_shape,
        scratch_shapes=[
            pltpu.VMEM((8 * block, 4 * rows), jnp.bfloat16),
            pltpu.VMEM((8 * block, 128), jnp.float32),
        ],
        compiler_params=params(60, "arbitrary"),
        cost_estimate=LIGHT,
        name="select_scaled" if scaled else "select",
    )(slots, weights, *parts, *earlier)


def hidden_kernel(count, where, *refs):
    xs, (gate_w, up_w), (out, held) = refs[:count], refs[count : count + 2], refs[-2:]
    step, tile = pl.program_id(0), gate_w.shape[1]
    steps, features = held.shape[0], out.shape[1]
    gate, up, first = None, None, 0
    for x in xs:
        rows = x[...].reshape(-1, x.shape[2])
        part = slice(first, first + x.shape[2])
        first += x.shape[2]
        g = jnp.dot(rows, gate_w[part, :], preferred_element_type=jnp.float32)
        u = jnp.dot(rows, up_w[part, :], preferred_element_type=jnp.float32)
        gate, up = (g, u) if gate is None else (gate + g, up + u)
    held[step] = (gate / (1.0 + jnp.exp(-gate)) * up).astype(jnp.bfloat16)

    @pl.when(step == steps - 1)
    def _():
        shard = features // (N_Y * N_ZH)
        column = lax.broadcasted_iota(jnp.int32, (tile, features), 1)
        row = lax.broadcasted_iota(jnp.int32, (tile, features), 0)
        number = column // shard
        zh = (where[1] + number % 2) % N_ZH
        y = (where[0] + number // 2) % N_Y
        origin = (y * N_ZH + zh) * shard + (column - number * shard)
        total = None
        for s in range(steps):
            move = (row + s * tile == origin).astype(jnp.float32).astype(jnp.bfloat16)
            part = jnp.dot(held[s], move, preferred_element_type=jnp.float32)
            total = part if total is None else total + part
        out[...] = total.astype(jnp.bfloat16)


def hidden_rows(where, xs, gate_weight, up_weight, earlier):
    depth, features = gate_weight.shape
    count = xs[0].shape[0] * xs[0].shape[1]
    tile = 256
    steps = features // tile
    return pl.pallas_call(
        lambda *refs: hidden_kernel(len(xs), *refs),
        grid=(steps,),
        in_specs=[pl.BlockSpec(memory_space=pltpu.SMEM)]
        + [pl.BlockSpec(x.shape, lambda j: (0, 0, 0)) for x in xs]
        + [pl.BlockSpec((depth, tile), lambda j: (0, j)) for _ in range(2)]
        + [pl.BlockSpec(memory_space=pl.ANY) for _ in earlier],
        out_specs=pl.BlockSpec((count, features), lambda j: (0, 0)),
        out_shape=jax.ShapeDtypeStruct((count, features), jnp.bfloat16),
        scratch_shapes=[pltpu.VMEM((steps, count, tile), jnp.bfloat16)],
        compiler_params=params(60, "arbitrary"),
        name="hidden",
    )(where, *xs, gate_weight, up_weight, *earlier)


def down_kernel(hidden, d0, d1, d2, d3, out):
    weight = jnp.concatenate([d0[...], d1[...], d2[...], d3[...]], axis=0)
    rows = jnp.dot(hidden[...], weight, preferred_element_type=jnp.float32)
    out[...] = rows.astype(jnp.bfloat16).reshape(out.shape)


def down_rows(hidden, downs, cap, first, width):
    tile = 256 if width % 512 else 512
    offset = first // tile
    block = 4 * cap
    return pl.pallas_call(
        down_kernel,
        grid=(width // tile,),
        in_specs=[pl.BlockSpec(hidden.shape, lambda j: (0, 0))]
        + [pl.BlockSpec((d.shape[0], tile), lambda j: (0, j + offset)) for d in downs],
        out_specs=pl.BlockSpec((8, block, tile), lambda j: (0, 0, j)),
        out_shape=jax.ShapeDtypeStruct((8, block, width), jnp.bfloat16),
        compiler_params=params(60, "arbitrary"),
        name="down",
    )(hidden, *downs)


def grad_kernel(where, hidden, *refs):
    rows, outs, turned = refs[:5], refs[-5:-1], refs[-1]
    block = rows[0].shape[0]

    @pl.when(pl.program_id(0) == 0)
    def _():
        parts = []
        for k in range(8):
            source = (where[2] + N_X - k % 4) % N_X * 2 + (where[3] + k // 4) % 2
            parts.append(hidden[pl.ds(pl.multiple_of(source * block, 16), block), :])
        turned[...] = jnp.concatenate(parts, axis=0).T

    value = jnp.concatenate([r[...] for r in rows], axis=0)
    grad = jnp.dot(turned[...], value, preferred_element_type=jnp.float32).astype(jnp.bfloat16)
    quarter = outs[0].shape[0]
    for k, out in enumerate(outs):
        out[...] = grad[k * quarter : (k + 1) * quarter, :]


def grad_blocks(where, hidden, rows, first, width, *earlier):
    block = rows[0].shape[0] // 2
    tile = 256 if width % 512 else 512
    offset = first // tile
    quarter = hidden.shape[1] // N_Y
    spec = pl.BlockSpec((quarter, tile), lambda j: (0, j))
    out = jax.ShapeDtypeStruct((quarter, width), jnp.bfloat16)
    return pl.pallas_call(
        grad_kernel,
        grid=(width // tile,),
        in_specs=[
            pl.BlockSpec(memory_space=pltpu.SMEM),
            pl.BlockSpec(hidden.shape, lambda j: (0, 0)),
        ]
        + [pl.BlockSpec((block, tile), lambda j: (0, j + offset)) for _ in range(4)]
        + [pl.BlockSpec((4 * block, tile), lambda j: (0, j + offset))]
        + [pl.BlockSpec(memory_space=pl.ANY) for _ in earlier],
        out_specs=(spec,) * 4,
        out_shape=(out,) * 4,
        scratch_shapes=[pltpu.VMEM(hidden.shape[::-1], jnp.bfloat16)],
        compiler_params=params(60, "arbitrary"),
        name="grad",
    )(where, hidden, *rows, *earlier)


def combine_kernel(slots, weights, rows, *refs):
    *outs, high, low = refs[-6:]
    dests, block, width = rows.shape
    tokens = slots.shape[1]

    @pl.when(pl.program_id(0) == 0)
    def _():
        place = lax.broadcasted_iota(jnp.int32, (block, tokens), 0).astype(jnp.float32)
        picked = []
        for d in range(dests):
            hit = (slots[d : d + 1, :] == place).astype(jnp.float32)
            picked.append(hit * weights[d : d + 1, :])
        pick = jnp.concatenate(picked, axis=0).T
        coarse = pick.astype(jnp.bfloat16)
        high[...] = coarse
        low[...] = (pick - coarse.astype(jnp.float32)).astype(jnp.bfloat16)

    value = rows[...].reshape(-1, width)
    total = jnp.dot(high[...], value, preferred_element_type=jnp.float32)
    total = total + jnp.dot(low[...], value, preferred_element_type=jnp.float32)
    count = outs[0].shape[0]
    for s, out in enumerate(outs):
        out[...] = total[s * count : (s + 1) * count, :].astype(out.dtype)


def combine_rows(plan, rows, *earlier):
    slots, weights = plan
    width = rows.shape[2]
    tile = 256 if width % 512 else 512
    count = slots.shape[1] // 4
    whole = pl.BlockSpec((8, slots.shape[1]), lambda j: (0, 0))
    spec = pl.BlockSpec((count, tile), lambda j: (0, j))
    return pl.pallas_call(
        combine_kernel,
        grid=(width // tile,),
        in_specs=[whole, whole, pl.BlockSpec((*rows.shape[:2], tile), lambda j: (0, 0, j))]
        + [pl.BlockSpec(memory_space=pl.ANY) for _ in earlier],
        out_specs=(spec,) * 4,
        out_shape=tuple(
            jax.ShapeDtypeStruct((count, width), t)
            for t in (jnp.float32, jnp.bfloat16, jnp.bfloat16, jnp.bfloat16)
        ),
        scratch_shapes=[
            pltpu.VMEM((slots.shape[1], rows.shape[0] * rows.shape[1]), jnp.bfloat16)
            for _ in range(2)
        ],
        compiler_params=params(60, "arbitrary"),
        name="combine",
    )(slots, weights, rows, *earlier)


def plane_permute(blocks):
    out = [blocks[0]]
    for k in range(1, N_X):
        out.append(permute(blocks[k], lambda y, z, x, c, k=k: (y, z, x + k, c)))
    return out


def core_permute(blocks, *earlier):
    passed = hold(blocks, *earlier, start=blocks[0].shape[0] // 2)
    return permute(passed, lambda y, z, x, c: (y, z, x, c + 1))


def plane_exchange(rows):
    return lax.all_to_all(rows, ("x", "c"), split_axis=0, concat_axis=0, tiled=True)


def z_return(own, near, other, far):
    step = z_down(far).astype(jnp.float32) + near.astype(jnp.float32)
    from_near = z_down(step.astype(jnp.bfloat16))
    from_other = z_up(other)
    total = own + from_near.astype(jnp.float32) + from_other.astype(jnp.float32)
    return total.astype(jnp.bfloat16)


def y_move(array, k):
    return permute(array, lambda y, z, x, c: (y + k, z, x, c))


def adam(grad, weight, first, second):
    weight_old = weight.astype(jnp.float32)
    moment_one = first_decay_rate * first.astype(jnp.float32) + (1.0 - first_decay_rate) * grad
    moment_two = beta_two * second.astype(jnp.float32) + (1.0 - beta_two) * grad * grad
    updated = weight_old - learn_rate * moment_one / (jnp.sqrt(moment_two) + adam_eps)
    return tuple(v.astype(jnp.bfloat16)[None] for v in (updated, moment_one, moment_two))


def local(
    tokens,
    expert_ids,
    route_weight,
    placement,
    swap_mask,
    gate_weight,
    up_weight,
    down_weight,
    first_moment,
    second_moment,
    out_grad,
):
    tok_rows, top = expert_ids.shape
    width = tokens.shape[1]
    experts = placement.shape[0]
    cap = tok_rows * top * 7 // (6 * experts)
    jumps = range(2 ** (SWAP_BITS - 1))
    jump = jnp.clip(swap_mask[0] // 2, 0, len(jumps) - 1)
    bits = [swap_mask // 2**bit % 2 for bit in range(SWAP_BITS)]

    where = [lax.axis_index(a) for a in ("y", "zh", "x", "c")]
    where = jnp.stack(where).astype(jnp.int32)

    dest = jnp.arange(8, dtype=jnp.int32)
    ring = (where[2] + dest // 2) % N_X * 2 + (where[3] + dest) % 2
    dest = jnp.concatenate([dest, ring])
    held_at = (dest // 2) * 8 + lax.axis_index("zl") * 2 + dest % 2
    ids = jnp.arange(experts, dtype=jnp.int32)
    here = jnp.sum(jnp.where(placement[None, :] == held_at[:, None], ids[None, :], 0), axis=1)
    here = jnp.broadcast_to(here.astype(jnp.float32)[:, None], (16, tok_rows))
    numbers = jnp.pad(expert_ids.astype(jnp.float32), ((0, 0), (0, 128 - top)))
    meta = numbers + jnp.pad(route_weight, ((0, 0), (8, 120 - top)))

    x_parts = z_gather(mark(tokens, meta))
    state = hold((down_weight[0], first_moment[0], second_moment[0]))
    far_state = swap(state, x=1)
    plan = make_plan(cap, top, here, x_parts, far_state)
    x_send = select_rows(False, cap, plan, x_parts, 0, width)
    x_rows = plane_exchange(x_send)
    down = hold((down_weight[0],), x_parts[1])
    partner = permute(down, lambda y, z, x, c: (y, z + 4, x, c))
    g_parts = z_gather(hold((out_grad,), plan[0], partner))
    state = choose(bits[3], far_state, state, x_send)
    state_cores = choose(bits[0], swap(state, c=1), state, *g_parts[2:])
    state_far = swap(state_cores, zl=2)

    g_send = select_rows(True, cap, plan, g_parts, 0, width, x_rows, state_cores)
    g_rows = plane_permute(g_send)

    pair = hold((down, partner), x_send)
    downs = (pair, y_move(pair, -1), y_move(pair, -2), y_move(pair, 1))

    hidden = hidden_rows(where, [x_rows], gate_weight[0], up_weight[0], g_send[3:])
    r_send = down_rows(hidden, downs, cap, 0, width)
    returned = plane_exchange(r_send)
    state_far = choose(bits[2], state_far, state_cores, r_send)
    state = choose(bits[1], swap(state_far, zl=1), state_far)

    g_rows = (*g_rows, core_permute(g_rows, state_far))
    chunk = width // G_CHUNKS
    partials = [
        grad_blocks(where, hidden, g_rows, i * chunk, chunk, r_send) for i in range(G_CHUNKS)
    ]
    grads = []
    for i, blocks in enumerate(partials):
        moved = [blocks[0]] + [y_move(blocks[k], k) for k in (1, 2, 3)]
        earlier = (grads[-1], returned) if grads else (partials[-1][0],)
        total = sum_blocks(moved, state, *earlier)
        total = choose(bits[0], swap(total, c=1), total)
        rows = total.shape[0] // 2
        mine, theirs = lax.switch(
            jump,
            [lambda a, b, m=m: (relocate(a, m), relocate(b, m, True)) for m in jumps],
            total[:rows],
            total[rows:],
        )
        grads.append(mine.astype(jnp.float32) + theirs.astype(jnp.float32))
    new_state = adam(jnp.concatenate(grads, axis=1), *jnp.split(state, 3, axis=0))

    layer_out = z_return(*combine_rows(plan, returned, grads[0]))
    return (layer_out, *new_state)


def solution(mesh):
    fine = Mesh(mesh.devices.reshape(N_Y, N_ZH, N_X, N_ZL, N_C), AXES)
    dp, expert = ("y", "zh"), ("x", "zl", "c")
    batch, weight, state = P(dp + expert, None), P(expert, None, None), P(expert, dp, None)
    return jax.shard_map(
        local,
        mesh=fine,
        in_specs=(batch,) * 3 + (P(), P()) + (weight,) * 2 + (state,) * 3 + (batch,),
        out_specs=(batch, state, state, state),
        check_vma=False,
    )
```

```python
import jax
import jax.numpy as jnp
from jax import lax
from jax.experimental import pallas as pl
from jax.experimental.pallas import tpu as pltpu
from jax.sharding import Mesh, PartitionSpec as P

SWAP_BITS = 4
N_Y, N_ZH, N_X, N_ZL, N_C = 4, 2, 4, 4, 2
AXES = ("y", "zh", "x", "zl", "c")
MIB = 1024 * 1024

first_decay_rate = 0.9
beta_two = 0.95
learn_rate = 0.003
adam_eps = 1e-08


def flat_index(y, z, x, c):
    z = z % 8
    return ((((y % 4) * N_ZH + z // N_ZL) * N_X + x % 4) * N_ZL + z % N_ZL) * N_C + c % 2


def permute(array, move):
    pairs = []
    for y in range(N_Y):
        for z in range(8):
            for x in range(N_X):
                for c in range(N_C):
                    pairs.append((flat_index(y, z, x, c), flat_index(*move(y, z, x, c))))
    return lax.ppermute(array, AXES, pairs)


def along(c):
    return 1 if c == 0 else -1


def z_up(array):
    return permute(array, lambda y, z, x, c: (y, z + along(c), x, c))


def z_down(array):
    return permute(array, lambda y, z, x, c: (y, z - along(c), x, c))


def z_gather(array):
    near = z_up(array)
    other = z_down(array)
    far = z_up(near)
    return array, near, other, far


def swap(array, zl=0, x=0, c=0):
    return permute(array, lambda y, z, i, j: (y, z ^ zl, i ^ x, j ^ c))


def relocate(array, jump, flip_zh=False):
    if jump == 0 and not flip_zh:
        return array

    def move(y, z, x, c):
        zl = (z % 4) ^ (jump & 3)
        zh = z // 4 ^ (1 if flip_zh else 0)
        return y, zh * 4 + zl, x ^ (jump >> 2), c

    return permute(array, move)


LIGHT = pl.CostEstimate(flops=1, bytes_accessed=1, transcendentals=0)


def params(mib, *semantics):
    return pltpu.CompilerParams(
        dimension_semantics=semantics or None, vmem_limit_bytes=mib * MIB
    )


def hold_kernel(count, start, *refs):
    out, first = refs[-1], 0
    for array in refs[:count]:
        rows = array.shape[0] - start
        out[first : first + rows, :] = array[start:, :]
        first += rows


def hold(arrays, *earlier, start=0):
    rows, width = sum(a.shape[0] - start for a in arrays), arrays[0].shape[1]
    return pl.pallas_call(
        lambda *refs: hold_kernel(len(arrays), start, *refs),
        in_specs=[pl.BlockSpec(memory_space=pltpu.VMEM) for _ in arrays]
        + [pl.BlockSpec(memory_space=pl.ANY) for _ in earlier],
        out_specs=pl.BlockSpec(memory_space=pltpu.VMEM),
        out_shape=jax.ShapeDtypeStruct((rows, width), arrays[0].dtype),
        compiler_params=params(60),
        cost_estimate=LIGHT,
        name="hold",
    )(*arrays, *earlier)


def mark_kernel(tokens, meta, out):
    width = tokens.shape[1]
    out[:, :width] = tokens[...]
    left = meta[...]
    total = None
    for turn in range(3):
        part = left.astype(jnp.bfloat16).astype(jnp.float32)
        left = left - part
        part = pltpu.roll(part, 16 * turn, 1) if turn else part
        total = part if total is None else total + part
    out[:, width:] = total.astype(jnp.bfloat16)


def mark(tokens, meta):
    rows, width = tokens.shape
    return pl.pallas_call(
        mark_kernel,
        in_specs=[pl.BlockSpec(memory_space=pltpu.VMEM)] * 2,
        out_specs=pl.BlockSpec(memory_space=pltpu.VMEM),
        out_shape=jax.ShapeDtypeStruct((rows, width + 128), jnp.bfloat16),
        compiler_params=params(60),
        cost_estimate=LIGHT,
        name="mark",
    )(tokens, meta)


def choose_kernel(wanted, other, own, *refs):
    @pl.when(wanted[0] == 1)
    def _():
        refs[-1][...] = other[...]

    @pl.when(wanted[0] != 1)
    def _():
        refs[-1][...] = own[...]


def choose(wanted, other, own, *earlier):
    return pl.pallas_call(
        choose_kernel,
        in_specs=[pl.BlockSpec(memory_space=pltpu.SMEM)]
        + [pl.BlockSpec(memory_space=pltpu.VMEM) for _ in range(2)]
        + [pl.BlockSpec(memory_space=pl.ANY) for _ in earlier],
        out_specs=pl.BlockSpec(memory_space=pltpu.VMEM),
        out_shape=jax.ShapeDtypeStruct(own.shape, own.dtype),
        compiler_params=params(60),
        cost_estimate=LIGHT,
        name="choose",
    )(wanted, other, own, *earlier)


def sum_kernel(a, b, c, d, *refs):
    total = a[...].astype(jnp.float32) + b[...].astype(jnp.float32)
    total = total + c[...].astype(jnp.float32) + d[...].astype(jnp.float32)
    refs[-1][...] = total.astype(jnp.bfloat16)


def sum_blocks(blocks, *earlier):
    return pl.pallas_call(
        sum_kernel,
        in_specs=[pl.BlockSpec(memory_space=pltpu.VMEM) for _ in blocks]
        + [pl.BlockSpec(memory_space=pl.ANY) for _ in earlier],
        out_specs=pl.BlockSpec(memory_space=pltpu.VMEM),
        out_shape=jax.ShapeDtypeStruct(blocks[0].shape, jnp.bfloat16),
        compiler_params=params(60),
        cost_estimate=LIGHT,
        name="sum",
    )(*blocks, *earlier)


def plan_kernel(cap, top, ids_here, m0, m1, m2, m3, *refs):
    slot_ref, weight_ref = refs[-2:]
    rows = m0.shape[0]
    before = lax.broadcasted_iota(jnp.int32, (rows, rows), 0)
    after = lax.broadcasted_iota(jnp.int32, (rows, rows), 1)
    earlier = (before < after).astype(jnp.float32).astype(jnp.bfloat16)
    wanted = ids_here[...]
    for s, block in enumerate((m0, m1, m2, m3)):
        meta = block[...].astype(jnp.float32).T
        scale = meta[8:16, :] + meta[24:32, :] + meta[40:48, :]
        named = jnp.zeros(wanted.shape, jnp.float32)
        weight = jnp.zeros(wanted.shape, jnp.float32)
        for k in range(top):
            same = (meta[k : k + 1, :] == wanted).astype(jnp.float32)
            named = named + same
            weight = weight + same * scale[k : k + 1, :]
        rank = jnp.dot(named.astype(jnp.bfloat16), earlier, preferred_element_type=jnp.float32)
        slot = jnp.where(named > 0.5, rank + float(s * cap), -1.0)
        slot_ref[:, s * rows : (s + 1) * rows] = slot
        weight_ref[:, s * rows : (s + 1) * rows] = weight


def make_plan(cap, top, ids_here, parts, *earlier):
    rows, width = parts[0].shape
    last = width // 128 - 1
    out = jax.ShapeDtypeStruct((ids_here.shape[0], 4 * rows), jnp.float32)
    whole = pl.BlockSpec(out.shape, lambda i: (0, 0))
    return pl.pallas_call(
        lambda *refs: plan_kernel(cap, top, *refs),
        grid=(1,),
        in_specs=[pl.BlockSpec(ids_here.shape, lambda i: (0, 0))]
        + [pl.BlockSpec((rows, 128), lambda i: (0, last)) for _ in parts]
        + [pl.BlockSpec(memory_space=pl.ANY) for _ in earlier],
        out_specs=(whole, whole),
        out_shape=(out, out),
        compiler_params=params(60, "arbitrary"),
        cost_estimate=LIGHT,
        name="plan",
    )(ids_here, *parts, *earlier)


def select_kernel(scaled, slots, weights, t0, t1, t2, t3, *refs):
    *outs, pick, scale = refs
    tokens = slots.shape[1]
    block = pick.shape[0] // 8
    base = 8 if scaled else 0

    @pl.when(pl.program_id(0) == 0)
    def _():
        place = lax.broadcasted_iota(jnp.int32, (block, tokens), 0).astype(jnp.float32)
        for d in range(8):
            hit = (slots[base + d : base + d + 1, :] == place).astype(jnp.float32)
            pick[d * block : (d + 1) * block, :] = hit.astype(jnp.bfloat16)
            if scaled:
                row = jnp.sum(hit * weights[base + d : base + d + 1, :], axis=1, keepdims=True)
                scale[d * block : (d + 1) * block, :] = jnp.broadcast_to(row, (block, 128))

    source = jnp.concatenate([t0[...], t1[...], t2[...], t3[...]], axis=0)
    rows = jnp.dot(pick[...], source, preferred_element_type=jnp.float32)
    if scaled:
        rows = (rows * scale[:, 0:1]).astype(jnp.bfloat16)
        for k, out in enumerate(outs[-4:]):
            out[...] = rows[2 * k * block : 2 * (k + 1) * block, :]
    else:
        outs[-1][...] = rows.astype(jnp.bfloat16).reshape(8, block, -1)


def select_rows(scaled, cap, plan, parts, first, width, *earlier):
    slots, weights = plan
    rows = parts[0].shape[0]
    block = 4 * cap
    tile = 256 if width % 512 else 512
    offset = first // tile
    whole = pl.BlockSpec(slots.shape, lambda j: (0, 0))
    if scaled:
        out_spec = (pl.BlockSpec((2 * block, tile), lambda j: (0, j)),) * 4
        out_shape = (jax.ShapeDtypeStruct((2 * block, width), jnp.bfloat16),) * 4
    else:
        out_spec = pl.BlockSpec((8, block, tile), lambda j: (0, 0, j))
        out_shape = jax.ShapeDtypeStruct((8, block, width), jnp.bfloat16)
    return pl.pallas_call(
        lambda *refs: select_kernel(scaled, *refs),
        grid=(width // tile,),
        in_specs=[whole, whole]
        + [pl.BlockSpec((rows, tile), lambda j: (0, j + offset)) for _ in range(4)]
        + [pl.BlockSpec(memory_space=pl.ANY) for _ in earlier],
        out_specs=out_spec,
        out_shape=out_shape,
        scratch_shapes=[
            pltpu.VMEM((8 * block, 4 * rows), jnp.bfloat16),
            pltpu.VMEM((8 * block, 128), jnp.float32),
        ],
        compiler_params=params(60, "arbitrary"),
        cost_estimate=LIGHT,
        name="select_scaled" if scaled else "select",
    )(slots, weights, *parts, *earlier)


def hidden_kernel(count, where, *refs):
    xs, (gate_w, up_w), (out, held) = refs[:count], refs[count : count + 2], refs[-2:]
    step, tile = pl.program_id(0), gate_w.shape[1]
    steps, features = held.shape[0], out.shape[1]
    gate, up, first = None, None, 0
    for x in xs:
        rows = x[...].reshape(-1, x.shape[2])
        part = slice(first, first + x.shape[2])
        first += x.shape[2]
        g = jnp.dot(rows, gate_w[part, :], preferred_element_type=jnp.float32)
        u = jnp.dot(rows, up_w[part, :], preferred_element_type=jnp.float32)
        gate, up = (g, u) if gate is None else (gate + g, up + u)
    held[step] = (gate / (1.0 + jnp.exp(-gate)) * up).astype(jnp.bfloat16)

    @pl.when(step == steps - 1)
    def _():
        shard = features // (N_Y * N_ZH)
        column = lax.broadcasted_iota(jnp.int32, (tile, features), 1)
        row = lax.broadcasted_iota(jnp.int32, (tile, features), 0)
        number = column // shard
        zh = (where[1] + number % 2) % N_ZH
        y = (where[0] + number // 2) % N_Y
        origin = (y * N_ZH + zh) * shard + (column - number * shard)
        total = None
        for s in range(steps):
            move = (row + s * tile == origin).astype(jnp.float32).astype(jnp.bfloat16)
            part = jnp.dot(held[s], move, preferred_element_type=jnp.float32)
            total = part if total is None else total + part
        out[...] = total.astype(jnp.bfloat16)


def hidden_rows(where, xs, gate_weight, up_weight, earlier):
    depth, features = gate_weight.shape
    count = xs[0].shape[0] * xs[0].shape[1]
    tile = 256
    steps = features // tile
    return pl.pallas_call(
        lambda *refs: hidden_kernel(len(xs), *refs),
        grid=(steps,),
        in_specs=[pl.BlockSpec(memory_space=pltpu.SMEM)]
        + [pl.BlockSpec(x.shape, lambda j: (0, 0, 0)) for x in xs]
        + [pl.BlockSpec((depth, tile), lambda j: (0, j)) for _ in range(2)]
        + [pl.BlockSpec(memory_space=pl.ANY) for _ in earlier],
        out_specs=pl.BlockSpec((count, features), lambda j: (0, 0)),
        out_shape=jax.ShapeDtypeStruct((count, features), jnp.bfloat16),
        scratch_shapes=[pltpu.VMEM((steps, count, tile), jnp.bfloat16)],
        compiler_params=params(60, "arbitrary"),
        name="hidden",
    )(where, *xs, gate_weight, up_weight, *earlier)


def down_kernel(hidden, d0, d1, d2, d3, out):
    weight = jnp.concatenate([d0[...], d1[...], d2[...], d3[...]], axis=0)
    rows = jnp.dot(hidden[...], weight, preferred_element_type=jnp.float32)
    out[...] = rows.astype(jnp.bfloat16).reshape(out.shape)


def down_rows(hidden, downs, cap, first, width):
    tile = 256 if width % 512 else 512
    offset = first // tile
    block = 4 * cap
    return pl.pallas_call(
        down_kernel,
        grid=(width // tile,),
        in_specs=[pl.BlockSpec(hidden.shape, lambda j: (0, 0))]
        + [pl.BlockSpec((d.shape[0], tile), lambda j: (0, j + offset)) for d in downs],
        out_specs=pl.BlockSpec((8, block, tile), lambda j: (0, 0, j)),
        out_shape=jax.ShapeDtypeStruct((8, block, width), jnp.bfloat16),
        compiler_params=params(60, "arbitrary"),
        name="down",
    )(hidden, *downs)


def grad_kernel(where, hidden, *refs):
    rows, outs, turned = refs[:5], refs[-5:-1], refs[-1]
    block = rows[0].shape[0]

    @pl.when(pl.program_id(0) == 0)
    def _():
        parts = []
        for k in range(8):
            source = (where[2] + N_X - k % 4) % N_X * 2 + (where[3] + k // 4) % 2
            parts.append(hidden[pl.ds(pl.multiple_of(source * block, 16), block), :])
        turned[...] = jnp.concatenate(parts, axis=0).T

    value = jnp.concatenate([r[...] for r in rows], axis=0)
    grad = jnp.dot(turned[...], value, preferred_element_type=jnp.float32).astype(jnp.bfloat16)
    quarter = outs[0].shape[0]
    for k, out in enumerate(outs):
        out[...] = grad[k * quarter : (k + 1) * quarter, :]


def grad_blocks(where, hidden, rows, *earlier):
    width = rows[0].shape[1]
    block = rows[0].shape[0] // 2
    tile = 256 if width % 512 else 512
    quarter = hidden.shape[1] // N_Y
    spec = pl.BlockSpec((quarter, tile), lambda j: (0, j))
    out = jax.ShapeDtypeStruct((quarter, width), jnp.bfloat16)
    return pl.pallas_call(
        grad_kernel,
        grid=(width // tile,),
        in_specs=[
            pl.BlockSpec(memory_space=pltpu.SMEM),
            pl.BlockSpec(hidden.shape, lambda j: (0, 0)),
        ]
        + [pl.BlockSpec((block, tile), lambda j: (0, j)) for _ in range(4)]
        + [pl.BlockSpec((4 * block, tile), lambda j: (0, j))]
        + [pl.BlockSpec(memory_space=pl.ANY) for _ in earlier],
        out_specs=(spec,) * 4,
        out_shape=(out,) * 4,
        scratch_shapes=[pltpu.VMEM(hidden.shape[::-1], jnp.bfloat16)],
        compiler_params=params(60, "arbitrary"),
        name="grad",
    )(where, hidden, *rows, *earlier)


def combine_kernel(slots, weights, rows, *refs):
    *outs, high, low = refs[-6:]
    dests, block, width = rows.shape
    tokens = slots.shape[1]

    @pl.when(pl.program_id(0) == 0)
    def _():
        place = lax.broadcasted_iota(jnp.int32, (block, tokens), 0).astype(jnp.float32)
        picked = []
        for d in range(dests):
            hit = (slots[d : d + 1, :] == place).astype(jnp.float32)
            picked.append(hit * weights[d : d + 1, :])
        pick = jnp.concatenate(picked, axis=0).T
        coarse = pick.astype(jnp.bfloat16)
        high[...] = coarse
        low[...] = (pick - coarse.astype(jnp.float32)).astype(jnp.bfloat16)

    value = rows[...].reshape(-1, width)
    total = jnp.dot(high[...], value, preferred_element_type=jnp.float32)
    total = total + jnp.dot(low[...], value, preferred_element_type=jnp.float32)
    count = outs[0].shape[0]
    for s, out in enumerate(outs):
        out[...] = total[s * count : (s + 1) * count, :].astype(out.dtype)


def combine_rows(plan, rows, *earlier):
    slots, weights = plan
    width = rows.shape[2]
    tile = 256 if width % 512 else 512
    count = slots.shape[1] // 4
    whole = pl.BlockSpec((8, slots.shape[1]), lambda j: (0, 0))
    spec = pl.BlockSpec((count, tile), lambda j: (0, j))
    return pl.pallas_call(
        combine_kernel,
        grid=(width // tile,),
        in_specs=[whole, whole, pl.BlockSpec((*rows.shape[:2], tile), lambda j: (0, 0, j))]
        + [pl.BlockSpec(memory_space=pl.ANY) for _ in earlier],
        out_specs=(spec,) * 4,
        out_shape=tuple(
            jax.ShapeDtypeStruct((count, width), t)
            for t in (jnp.float32, jnp.bfloat16, jnp.bfloat16, jnp.bfloat16)
        ),
        scratch_shapes=[
            pltpu.VMEM((slots.shape[1], rows.shape[0] * rows.shape[1]), jnp.bfloat16)
            for _ in range(2)
        ],
        compiler_params=params(60, "arbitrary"),
        name="combine",
    )(slots, weights, rows, *earlier)


def plane_permute(blocks):
    out = [blocks[0]]
    for k in range(1, N_X):
        out.append(permute(blocks[k], lambda y, z, x, c, k=k: (y, z, x + k, c)))
    return out


def core_permute(blocks, *earlier):
    passed = hold(blocks, *earlier, start=blocks[0].shape[0] // 2)
    return permute(passed, lambda y, z, x, c: (y, z, x, c + 1))


def plane_exchange(rows):
    return lax.all_to_all(rows, ("x", "c"), split_axis=0, concat_axis=0, tiled=True)


def z_return(own, near, other, far):
    step = z_down(far).astype(jnp.float32) + near.astype(jnp.float32)
    from_near = z_down(step.astype(jnp.bfloat16))
    from_other = z_up(other)
    total = own + from_near.astype(jnp.float32) + from_other.astype(jnp.float32)
    return total.astype(jnp.bfloat16)


def y_move(array, k):
    return permute(array, lambda y, z, x, c: (y + k, z, x, c))


def adam(grad, weight, first, second):
    weight_old = weight.astype(jnp.float32)
    moment_one = first_decay_rate * first.astype(jnp.float32) + (1.0 - first_decay_rate) * grad
    moment_two = beta_two * second.astype(jnp.float32) + (1.0 - beta_two) * grad * grad
    updated = weight_old - learn_rate * moment_one / (jnp.sqrt(moment_two) + adam_eps)
    return tuple(v.astype(jnp.bfloat16)[None] for v in (updated, moment_one, moment_two))


def local(
    tokens,
    expert_ids,
    route_weight,
    placement,
    swap_mask,
    gate_weight,
    up_weight,
    down_weight,
    first_moment,
    second_moment,
    out_grad,
):
    tok_rows, top = expert_ids.shape
    width = tokens.shape[1]
    experts = placement.shape[0]
    cap = tok_rows * top * 7 // (6 * experts)
    jumps = range(2 ** (SWAP_BITS - 1))
    jump = jnp.clip(swap_mask[0] // 2, 0, len(jumps) - 1)
    bits = [swap_mask // 2**bit % 2 for bit in range(SWAP_BITS)]

    where = [lax.axis_index(a) for a in ("y", "zh", "x", "c")]
    where = jnp.stack(where).astype(jnp.int32)

    dest = jnp.arange(8, dtype=jnp.int32)
    ring = (where[2] + dest // 2) % N_X * 2 + (where[3] + dest) % 2
    dest = jnp.concatenate([dest, ring])
    held_at = (dest // 2) * 8 + lax.axis_index("zl") * 2 + dest % 2
    ids = jnp.arange(experts, dtype=jnp.int32)
    here = jnp.sum(jnp.where(placement[None, :] == held_at[:, None], ids[None, :], 0), axis=1)
    here = jnp.broadcast_to(here.astype(jnp.float32)[:, None], (16, tok_rows))
    numbers = jnp.pad(expert_ids.astype(jnp.float32), ((0, 0), (0, 128 - top)))
    meta = numbers + jnp.pad(route_weight, ((0, 0), (8, 120 - top)))

    x_parts = z_gather(mark(tokens, meta))
    state = hold((down_weight[0], first_moment[0], second_moment[0]))
    far_state = swap(state, x=1)
    plan = make_plan(cap, top, here, x_parts, far_state)
    x_send = select_rows(False, cap, plan, x_parts, 0, width)
    x_rows = plane_exchange(x_send)
    g_parts = z_gather(hold((out_grad,), plan[0]))
    state = choose(bits[3], far_state, state, x_send)
    state_cores = choose(bits[0], swap(state, c=1), state, *g_parts[2:])
    state_far = swap(state_cores, zl=2)

    g_send = select_rows(True, cap, plan, g_parts, 0, width, x_rows, state_cores)
    g_rows = plane_permute(g_send)

    down = hold((down_weight[0],), plan[0])
    partner = permute(down, lambda y, z, x, c: (y, z + 4, x, c))
    pair = jnp.concatenate([down, partner], axis=0)
    downs = (pair, y_move(pair, -1), y_move(pair, -2), y_move(pair, 1))

    hidden = hidden_rows(where, [x_rows], gate_weight[0], up_weight[0], g_send[3:])
    r_send = down_rows(hidden, downs, cap, 0, width)
    returned = plane_exchange(r_send)
    state_far = choose(bits[2], state_far, state_cores, r_send)
    state = choose(bits[1], swap(state_far, zl=1), state_far)

    g_rows = (*g_rows, core_permute(g_rows, state_far))
    blocks = grad_blocks(where, hidden, g_rows)
    blocks = [blocks[0]] + [y_move(blocks[k], k) for k in (1, 2, 3)]
    total = sum_blocks(blocks)
    total = choose(bits[0], swap(total, c=1), total)
    rows = total.shape[0] // 2
    mine, theirs = lax.switch(
        jump,
        [lambda a, b, m=m: (relocate(a, m), relocate(b, m, True)) for m in jumps],
        total[:rows],
        total[rows:],
    )
    grad = mine.astype(jnp.float32) + theirs.astype(jnp.float32)
    new_state = adam(grad, *jnp.split(state, 3, axis=0))

    layer_out = z_return(*combine_rows(plan, returned, blocks[1]))
    return (layer_out, *new_state)


def solution(mesh):
    fine = Mesh(mesh.devices.reshape(N_Y, N_ZH, N_X, N_ZL, N_C), AXES)
    dp, expert = ("y", "zh"), ("x", "zl", "c")
    batch, weight, state = P(dp + expert, None), P(expert, None, None), P(expert, dp, None)
    return jax.shard_map(
        local,
        mesh=fine,
        in_specs=(batch,) * 3 + (P(), P()) + (weight,) * 2 + (state,) * 3 + (batch,),
        out_specs=(batch, state, state, state),
        check_vma=False,
    )
```

```python
import jax
import jax.numpy as jnp
from jax import lax
from jax.experimental import pallas as pl
from jax.experimental.pallas import tpu as pltpu
from jax.sharding import Mesh, PartitionSpec as P

SWAP_BITS = 4
N_Y, N_ZH, N_X, N_ZL, N_C = 4, 2, 4, 4, 2
AXES = ("y", "zh", "x", "zl", "c")
MIB = 1024 * 1024

first_decay_rate = 0.9
beta_two = 0.95
learn_rate = 0.003
adam_eps = 1e-08


def flat_index(y, z, x, c):
    z = z % 8
    return ((((y % 4) * N_ZH + z // N_ZL) * N_X + x % 4) * N_ZL + z % N_ZL) * N_C + c % 2


def permute(array, move):
    pairs = []
    for y in range(N_Y):
        for z in range(8):
            for x in range(N_X):
                for c in range(N_C):
                    pairs.append((flat_index(y, z, x, c), flat_index(*move(y, z, x, c))))
    return lax.ppermute(array, AXES, pairs)


def along(c):
    return 1 if c == 0 else -1


def z_up(array):
    return permute(array, lambda y, z, x, c: (y, z + along(c), x, c))


def z_down(array):
    return permute(array, lambda y, z, x, c: (y, z - along(c), x, c))


def z_gather(array):
    near = z_up(array)
    other = z_down(array)
    far = z_up(near)
    return array, near, other, far


def swap(array, zl=0, x=0, c=0):
    return permute(array, lambda y, z, i, j: (y, z ^ zl, i ^ x, j ^ c))


def relocate(array, jump, flip_zh=False):
    if jump == 0 and not flip_zh:
        return array

    def move(y, z, x, c):
        zl = (z % 4) ^ (jump & 3)
        zh = z // 4 ^ (1 if flip_zh else 0)
        return y, zh * 4 + zl, x ^ (jump >> 2), c

    return permute(array, move)


LIGHT = pl.CostEstimate(flops=1, bytes_accessed=1, transcendentals=0)


def params(mib, *semantics):
    return pltpu.CompilerParams(
        dimension_semantics=semantics or None, vmem_limit_bytes=mib * MIB
    )


def hold_kernel(count, start, *refs):
    out, first = refs[-1], 0
    for array in refs[:count]:
        rows = array.shape[0] - start
        out[first : first + rows, :] = array[start:, :]
        first += rows


def hold(arrays, *earlier, start=0):
    rows, width = sum(a.shape[0] - start for a in arrays), arrays[0].shape[1]
    return pl.pallas_call(
        lambda *refs: hold_kernel(len(arrays), start, *refs),
        in_specs=[pl.BlockSpec(memory_space=pltpu.VMEM) for _ in arrays]
        + [pl.BlockSpec(memory_space=pl.ANY) for _ in earlier],
        out_specs=pl.BlockSpec(memory_space=pltpu.VMEM),
        out_shape=jax.ShapeDtypeStruct((rows, width), arrays[0].dtype),
        compiler_params=params(60),
        cost_estimate=LIGHT,
        name="hold",
    )(*arrays, *earlier)


def mark_kernel(tokens, meta, out):
    width = tokens.shape[1]
    out[:, :width] = tokens[...]
    left = meta[...]
    total = None
    for turn in range(3):
        part = left.astype(jnp.bfloat16).astype(jnp.float32)
        left = left - part
        part = pltpu.roll(part, 16 * turn, 1) if turn else part
        total = part if total is None else total + part
    out[:, width:] = total.astype(jnp.bfloat16)


def mark(tokens, meta):
    rows, width = tokens.shape
    return pl.pallas_call(
        mark_kernel,
        in_specs=[pl.BlockSpec(memory_space=pltpu.VMEM)] * 2,
        out_specs=pl.BlockSpec(memory_space=pltpu.VMEM),
        out_shape=jax.ShapeDtypeStruct((rows, width + 128), jnp.bfloat16),
        compiler_params=params(60),
        cost_estimate=LIGHT,
        name="mark",
    )(tokens, meta)


def choose_kernel(wanted, other, own, *refs):
    @pl.when(wanted[0] == 1)
    def _():
        refs[-1][...] = other[...]

    @pl.when(wanted[0] != 1)
    def _():
        refs[-1][...] = own[...]


def choose(wanted, other, own, *earlier):
    return pl.pallas_call(
        choose_kernel,
        in_specs=[pl.BlockSpec(memory_space=pltpu.SMEM)]
        + [pl.BlockSpec(memory_space=pltpu.VMEM) for _ in range(2)]
        + [pl.BlockSpec(memory_space=pl.ANY) for _ in earlier],
        out_specs=pl.BlockSpec(memory_space=pltpu.VMEM),
        out_shape=jax.ShapeDtypeStruct(own.shape, own.dtype),
        compiler_params=params(60),
        cost_estimate=LIGHT,
        name="choose",
    )(wanted, other, own, *earlier)


def sum_kernel(a, b, c, d, *refs):
    total = a[...].astype(jnp.float32) + b[...].astype(jnp.float32)
    total = total + c[...].astype(jnp.float32) + d[...].astype(jnp.float32)
    refs[-1][...] = total.astype(jnp.bfloat16)


def sum_blocks(blocks, *earlier):
    return pl.pallas_call(
        sum_kernel,
        in_specs=[pl.BlockSpec(memory_space=pltpu.VMEM) for _ in blocks]
        + [pl.BlockSpec(memory_space=pl.ANY) for _ in earlier],
        out_specs=pl.BlockSpec(memory_space=pltpu.VMEM),
        out_shape=jax.ShapeDtypeStruct(blocks[0].shape, jnp.bfloat16),
        compiler_params=params(60),
        cost_estimate=LIGHT,
        name="sum",
    )(*blocks, *earlier)


def plan_kernel(cap, top, ids_here, m0, m1, m2, m3, *refs):
    slot_ref, weight_ref = refs[-2:]
    rows = m0.shape[0]
    before = lax.broadcasted_iota(jnp.int32, (rows, rows), 0)
    after = lax.broadcasted_iota(jnp.int32, (rows, rows), 1)
    earlier = (before < after).astype(jnp.float32).astype(jnp.bfloat16)
    wanted = ids_here[...]
    for s, block in enumerate((m0, m1, m2, m3)):
        meta = block[...].astype(jnp.float32).T
        scale = meta[8:16, :] + meta[24:32, :] + meta[40:48, :]
        named = jnp.zeros(wanted.shape, jnp.float32)
        weight = jnp.zeros(wanted.shape, jnp.float32)
        for k in range(top):
            same = (meta[k : k + 1, :] == wanted).astype(jnp.float32)
            named = named + same
            weight = weight + same * scale[k : k + 1, :]
        rank = jnp.dot(named.astype(jnp.bfloat16), earlier, preferred_element_type=jnp.float32)
        slot = jnp.where(named > 0.5, rank + float(s * cap), -1.0)
        slot_ref[:, s * rows : (s + 1) * rows] = slot
        weight_ref[:, s * rows : (s + 1) * rows] = weight


def make_plan(cap, top, ids_here, parts, *earlier):
    rows, width = parts[0].shape
    last = width // 128 - 1
    out = jax.ShapeDtypeStruct((ids_here.shape[0], 4 * rows), jnp.float32)
    whole = pl.BlockSpec(out.shape, lambda i: (0, 0))
    return pl.pallas_call(
        lambda *refs: plan_kernel(cap, top, *refs),
        grid=(1,),
        in_specs=[pl.BlockSpec(ids_here.shape, lambda i: (0, 0))]
        + [pl.BlockSpec((rows, 128), lambda i: (0, last)) for _ in parts]
        + [pl.BlockSpec(memory_space=pl.ANY) for _ in earlier],
        out_specs=(whole, whole),
        out_shape=(out, out),
        compiler_params=params(60, "arbitrary"),
        cost_estimate=LIGHT,
        name="plan",
    )(ids_here, *parts, *earlier)


def select_kernel(scaled, slots, weights, t0, t1, t2, t3, *refs):
    *outs, pick, scale = refs
    tokens = slots.shape[1]
    block = pick.shape[0] // 8
    base = 8 if scaled else 0

    @pl.when(pl.program_id(0) == 0)
    def _():
        place = lax.broadcasted_iota(jnp.int32, (block, tokens), 0).astype(jnp.float32)
        for d in range(8):
            hit = (slots[base + d : base + d + 1, :] == place).astype(jnp.float32)
            pick[d * block : (d + 1) * block, :] = hit.astype(jnp.bfloat16)
            if scaled:
                row = jnp.sum(hit * weights[base + d : base + d + 1, :], axis=1, keepdims=True)
                scale[d * block : (d + 1) * block, :] = jnp.broadcast_to(row, (block, 128))

    source = jnp.concatenate([t0[...], t1[...], t2[...], t3[...]], axis=0)
    rows = jnp.dot(pick[...], source, preferred_element_type=jnp.float32)
    if scaled:
        rows = (rows * scale[:, 0:1]).astype(jnp.bfloat16)
        for k, out in enumerate(outs[-4:]):
            out[...] = rows[2 * k * block : 2 * (k + 1) * block, :]
    else:
        outs[-1][...] = rows.astype(jnp.bfloat16).reshape(8, block, -1)


def select_rows(scaled, cap, plan, parts, first, width, *earlier):
    slots, weights = plan
    rows = parts[0].shape[0]
    block = 4 * cap
    tile = 256 if width % 512 else 512
    offset = first // tile
    whole = pl.BlockSpec(slots.shape, lambda j: (0, 0))
    if scaled:
        out_spec = (pl.BlockSpec((2 * block, tile), lambda j: (0, j)),) * 4
        out_shape = (jax.ShapeDtypeStruct((2 * block, width), jnp.bfloat16),) * 4
    else:
        out_spec = pl.BlockSpec((8, block, tile), lambda j: (0, 0, j))
        out_shape = jax.ShapeDtypeStruct((8, block, width), jnp.bfloat16)
    return pl.pallas_call(
        lambda *refs: select_kernel(scaled, *refs),
        grid=(width // tile,),
        in_specs=[whole, whole]
        + [pl.BlockSpec((rows, tile), lambda j: (0, j + offset)) for _ in range(4)]
        + [pl.BlockSpec(memory_space=pl.ANY) for _ in earlier],
        out_specs=out_spec,
        out_shape=out_shape,
        scratch_shapes=[
            pltpu.VMEM((8 * block, 4 * rows), jnp.bfloat16),
            pltpu.VMEM((8 * block, 128), jnp.float32),
        ],
        compiler_params=params(60, "arbitrary"),
        cost_estimate=LIGHT,
        name="select_scaled" if scaled else "select",
    )(slots, weights, *parts, *earlier)


def hidden_kernel(count, where, *refs):
    xs, (gate_w, up_w), (out, held) = refs[:count], refs[count : count + 2], refs[-2:]
    step, tile = pl.program_id(0), gate_w.shape[1]
    steps, features = held.shape[0], out.shape[1]
    gate, up, first = None, None, 0
    for x in xs:
        rows = x[...].reshape(-1, x.shape[2])
        part = slice(first, first + x.shape[2])
        first += x.shape[2]
        g = jnp.dot(rows, gate_w[part, :], preferred_element_type=jnp.float32)
        u = jnp.dot(rows, up_w[part, :], preferred_element_type=jnp.float32)
        gate, up = (g, u) if gate is None else (gate + g, up + u)
    held[step] = (gate / (1.0 + jnp.exp(-gate)) * up).astype(jnp.bfloat16)

    @pl.when(step == steps - 1)
    def _():
        shard = features // (N_Y * N_ZH)
        column = lax.broadcasted_iota(jnp.int32, (tile, features), 1)
        row = lax.broadcasted_iota(jnp.int32, (tile, features), 0)
        number = column // shard
        zh = (where[1] + number % 2) % N_ZH
        y = (where[0] + number // 2) % N_Y
        origin = (y * N_ZH + zh) * shard + (column - number * shard)
        total = None
        for s in range(steps):
            move = (row + s * tile == origin).astype(jnp.float32).astype(jnp.bfloat16)
            part = jnp.dot(held[s], move, preferred_element_type=jnp.float32)
            total = part if total is None else total + part
        out[...] = total.astype(jnp.bfloat16)


def hidden_rows(where, xs, gate_weight, up_weight, earlier):
    depth, features = gate_weight.shape
    count = xs[0].shape[0] * xs[0].shape[1]
    tile = 256
    steps = features // tile
    return pl.pallas_call(
        lambda *refs: hidden_kernel(len(xs), *refs),
        grid=(steps,),
        in_specs=[pl.BlockSpec(memory_space=pltpu.SMEM)]
        + [pl.BlockSpec(x.shape, lambda j: (0, 0, 0)) for x in xs]
        + [pl.BlockSpec((depth, tile), lambda j: (0, j)) for _ in range(2)]
        + [pl.BlockSpec(memory_space=pl.ANY) for _ in earlier],
        out_specs=pl.BlockSpec((count, features), lambda j: (0, 0)),
        out_shape=jax.ShapeDtypeStruct((count, features), jnp.bfloat16),
        scratch_shapes=[pltpu.VMEM((steps, count, tile), jnp.bfloat16)],
        compiler_params=params(60, "arbitrary"),
        name="hidden",
    )(where, *xs, gate_weight, up_weight, *earlier)


def down_kernel(hidden, d0, d1, d2, d3, out):
    weight = jnp.concatenate([d0[...], d1[...], d2[...], d3[...]], axis=0)
    rows = jnp.dot(hidden[...], weight, preferred_element_type=jnp.float32)
    out[...] = rows.astype(jnp.bfloat16).reshape(out.shape)


def down_rows(hidden, downs, cap, first, width):
    tile = 256 if width % 512 else 512
    offset = first // tile
    block = 4 * cap
    return pl.pallas_call(
        down_kernel,
        grid=(width // tile,),
        in_specs=[pl.BlockSpec(hidden.shape, lambda j: (0, 0))]
        + [pl.BlockSpec((d.shape[0], tile), lambda j: (0, j + offset)) for d in downs],
        out_specs=pl.BlockSpec((8, block, tile), lambda j: (0, 0, j)),
        out_shape=jax.ShapeDtypeStruct((8, block, width), jnp.bfloat16),
        compiler_params=params(60, "arbitrary"),
        name="down",
    )(hidden, *downs)


def grad_kernel(where, hidden, *refs):
    rows, outs, turned = refs[:5], refs[-5:-1], refs[-1]
    block = rows[0].shape[0]

    @pl.when(pl.program_id(0) == 0)
    def _():
        parts = []
        for k in range(8):
            source = (where[2] + N_X - k % 4) % N_X * 2 + (where[3] + k // 4) % 2
            parts.append(hidden[pl.ds(pl.multiple_of(source * block, 16), block), :])
        turned[...] = jnp.concatenate(parts, axis=0).T

    value = jnp.concatenate([r[...] for r in rows], axis=0)
    grad = jnp.dot(turned[...], value, preferred_element_type=jnp.float32).astype(jnp.bfloat16)
    quarter = outs[0].shape[0]
    for k, out in enumerate(outs):
        out[...] = grad[k * quarter : (k + 1) * quarter, :]


def grad_blocks(where, hidden, rows, *earlier):
    width = rows[0].shape[1]
    block = rows[0].shape[0] // 2
    tile = 256 if width % 512 else 512
    quarter = hidden.shape[1] // N_Y
    spec = pl.BlockSpec((quarter, tile), lambda j: (0, j))
    out = jax.ShapeDtypeStruct((quarter, width), jnp.bfloat16)
    return pl.pallas_call(
        grad_kernel,
        grid=(width // tile,),
        in_specs=[
            pl.BlockSpec(memory_space=pltpu.SMEM),
            pl.BlockSpec(hidden.shape, lambda j: (0, 0)),
        ]
        + [pl.BlockSpec((block, tile), lambda j: (0, j)) for _ in range(4)]
        + [pl.BlockSpec((4 * block, tile), lambda j: (0, j))]
        + [pl.BlockSpec(memory_space=pl.ANY) for _ in earlier],
        out_specs=(spec,) * 4,
        out_shape=(out,) * 4,
        scratch_shapes=[pltpu.VMEM(hidden.shape[::-1], jnp.bfloat16)],
        compiler_params=params(60, "arbitrary"),
        name="grad",
    )(where, hidden, *rows, *earlier)


def combine_kernel(slots, weights, rows, *refs):
    *outs, high, low = refs[-6:]
    dests, block, width = rows.shape
    tokens = slots.shape[1]

    @pl.when(pl.program_id(0) == 0)
    def _():
        place = lax.broadcasted_iota(jnp.int32, (block, tokens), 0).astype(jnp.float32)
        picked = []
        for d in range(dests):
            hit = (slots[d : d + 1, :] == place).astype(jnp.float32)
            picked.append(hit * weights[d : d + 1, :])
        pick = jnp.concatenate(picked, axis=0).T
        coarse = pick.astype(jnp.bfloat16)
        high[...] = coarse
        low[...] = (pick - coarse.astype(jnp.float32)).astype(jnp.bfloat16)

    value = rows[...].reshape(-1, width)
    total = jnp.dot(high[...], value, preferred_element_type=jnp.float32)
    total = total + jnp.dot(low[...], value, preferred_element_type=jnp.float32)
    count = outs[0].shape[0]
    for s, out in enumerate(outs):
        out[...] = total[s * count : (s + 1) * count, :].astype(out.dtype)


def combine_rows(plan, rows, *earlier):
    slots, weights = plan
    width = rows.shape[2]
    tile = 256 if width % 512 else 512
    count = slots.shape[1] // 4
    whole = pl.BlockSpec((8, slots.shape[1]), lambda j: (0, 0))
    spec = pl.BlockSpec((count, tile), lambda j: (0, j))
    return pl.pallas_call(
        combine_kernel,
        grid=(width // tile,),
        in_specs=[whole, whole, pl.BlockSpec((*rows.shape[:2], tile), lambda j: (0, 0, j))]
        + [pl.BlockSpec(memory_space=pl.ANY) for _ in earlier],
        out_specs=(spec,) * 4,
        out_shape=tuple(
            jax.ShapeDtypeStruct((count, width), t)
            for t in (jnp.float32, jnp.bfloat16, jnp.bfloat16, jnp.bfloat16)
        ),
        scratch_shapes=[
            pltpu.VMEM((slots.shape[1], rows.shape[0] * rows.shape[1]), jnp.bfloat16)
            for _ in range(2)
        ],
        compiler_params=params(60, "arbitrary"),
        name="combine",
    )(slots, weights, rows, *earlier)


def plane_permute(blocks):
    out = [blocks[0]]
    for k in range(1, N_X):
        out.append(permute(blocks[k], lambda y, z, x, c, k=k: (y, z, x + k, c)))
    return out


def core_permute(blocks, *earlier):
    passed = hold(blocks, *earlier, start=blocks[0].shape[0] // 2)
    return permute(passed, lambda y, z, x, c: (y, z, x, c + 1))


def plane_exchange(rows):
    return lax.all_to_all(rows, ("x", "c"), split_axis=0, concat_axis=0, tiled=True)


def z_return(own, near, other, far):
    step = z_down(far).astype(jnp.float32) + near.astype(jnp.float32)
    from_near = z_down(step.astype(jnp.bfloat16))
    from_other = z_up(other)
    total = own + from_near.astype(jnp.float32) + from_other.astype(jnp.float32)
    return total.astype(jnp.bfloat16)


def y_move(array, k):
    return permute(array, lambda y, z, x, c: (y + k, z, x, c))


def adam(grad, weight, first, second):
    weight_old = weight.astype(jnp.float32)
    moment_one = first_decay_rate * first.astype(jnp.float32) + (1.0 - first_decay_rate) * grad
    moment_two = beta_two * second.astype(jnp.float32) + (1.0 - beta_two) * grad * grad
    updated = weight_old - learn_rate * moment_one / (jnp.sqrt(moment_two) + adam_eps)
    return tuple(v.astype(jnp.bfloat16)[None] for v in (updated, moment_one, moment_two))


def local(
    tokens,
    expert_ids,
    route_weight,
    placement,
    swap_mask,
    gate_weight,
    up_weight,
    down_weight,
    first_moment,
    second_moment,
    out_grad,
):
    tok_rows, top = expert_ids.shape
    width = tokens.shape[1]
    experts = placement.shape[0]
    cap = tok_rows * top * 7 // (6 * experts)
    jumps = range(2 ** (SWAP_BITS - 1))
    jump = jnp.clip(swap_mask[0] // 2, 0, len(jumps) - 1)
    bits = [swap_mask // 2**bit % 2 for bit in range(SWAP_BITS)]

    where = [lax.axis_index(a) for a in ("y", "zh", "x", "c")]
    where = jnp.stack(where).astype(jnp.int32)

    dest = jnp.arange(8, dtype=jnp.int32)
    ring = (where[2] + dest // 2) % N_X * 2 + (where[3] + dest) % 2
    dest = jnp.concatenate([dest, ring])
    held_at = (dest // 2) * 8 + lax.axis_index("zl") * 2 + dest % 2
    ids = jnp.arange(experts, dtype=jnp.int32)
    here = jnp.sum(jnp.where(placement[None, :] == held_at[:, None], ids[None, :], 0), axis=1)
    here = jnp.broadcast_to(here.astype(jnp.float32)[:, None], (16, tok_rows))
    numbers = jnp.pad(expert_ids.astype(jnp.float32), ((0, 0), (0, 128 - top)))
    meta = numbers + jnp.pad(route_weight, ((0, 0), (8, 120 - top)))

    x_parts = z_gather(mark(tokens, meta))
    state = hold((down_weight[0], first_moment[0], second_moment[0]))
    far_state = swap(state, x=1)
    plan = make_plan(cap, top, here, x_parts, far_state)
    x_send = select_rows(False, cap, plan, x_parts, 0, width)
    x_rows = plane_exchange(x_send)
    g_parts = z_gather(hold((out_grad,), plan[0]))
    state = choose(bits[3], far_state, state, x_send)
    state_cores = choose(bits[0], swap(state, c=1), state, *g_parts[2:])
    state_far = swap(state_cores, zl=2)

    g_send = select_rows(True, cap, plan, g_parts, 0, width, x_rows, state_cores)
    g_rows = plane_permute(g_send)

    down = hold((down_weight[0],), plan[0])
    partner = permute(down, lambda y, z, x, c: (y, z + 4, x, c))
    pair = jnp.concatenate([down, partner], axis=0)
    later = hold((pair,), g_send[3])
    downs = (pair, y_move(pair, -1), y_move(pair, -2), y_move(later, 1))

    hidden = hidden_rows(where, [x_rows], gate_weight[0], up_weight[0], g_send[3:])
    r_send = down_rows(hidden, downs, cap, 0, width)
    returned = plane_exchange(r_send)
    state_far = choose(bits[2], state_far, state_cores, r_send)
    state = choose(bits[1], swap(state_far, zl=1), state_far)

    g_rows = (*g_rows, core_permute(g_rows, state_far))
    blocks = grad_blocks(where, hidden, g_rows)
    blocks = [blocks[0]] + [y_move(blocks[k], k) for k in (1, 2, 3)]
    total = sum_blocks(blocks, returned)
    total = choose(bits[0], swap(total, c=1), total)
    rows = total.shape[0] // 2
    mine, theirs = lax.switch(
        jump,
        [lambda a, b, m=m: (relocate(a, m), relocate(b, m, True)) for m in jumps],
        total[:rows],
        total[rows:],
    )
    grad = mine.astype(jnp.float32) + theirs.astype(jnp.float32)
    new_state = adam(grad, *jnp.split(state, 3, axis=0))

    layer_out = z_return(*combine_rows(plan, returned, blocks[1]))
    return (layer_out, *new_state)


def solution(mesh):
    fine = Mesh(mesh.devices.reshape(N_Y, N_ZH, N_X, N_ZL, N_C), AXES)
    dp, expert = ("y", "zh"), ("x", "zl", "c")
    batch, weight, state = P(dp + expert, None), P(expert, None, None), P(expert, dp, None)
    return jax.shard_map(
        local,
        mesh=fine,
        in_specs=(batch,) * 3 + (P(), P()) + (weight,) * 2 + (state,) * 3 + (batch,),
        out_specs=(batch, state, state, state),
        check_vma=False,
    )
```

```python
import jax
import jax.numpy as jnp
from jax import lax
from jax.experimental import pallas as pl
from jax.experimental.pallas import tpu as pltpu
from jax.sharding import Mesh, PartitionSpec as P

SWAP_BITS = 4
N_Y, N_ZH, N_X, N_ZL, N_C = 4, 2, 4, 4, 2
AXES = ("y", "zh", "x", "zl", "c")
MIB = 1024 * 1024

first_decay_rate = 0.9
beta_two = 0.95
learn_rate = 0.003
adam_eps = 1e-08


def flat_index(y, z, x, c):
    z = z % 8
    return ((((y % 4) * N_ZH + z // N_ZL) * N_X + x % 4) * N_ZL + z % N_ZL) * N_C + c % 2


def permute(array, move):
    pairs = []
    for y in range(N_Y):
        for z in range(8):
            for x in range(N_X):
                for c in range(N_C):
                    pairs.append((flat_index(y, z, x, c), flat_index(*move(y, z, x, c))))
    return lax.ppermute(array, AXES, pairs)


def along(c):
    return 1 if c == 0 else -1


def z_up(array):
    return permute(array, lambda y, z, x, c: (y, z + along(c), x, c))


def z_down(array):
    return permute(array, lambda y, z, x, c: (y, z - along(c), x, c))


def z_gather(array):
    near = z_up(array)
    other = z_down(array)
    far = z_up(near)
    return array, near, other, far


def swap(array, zl=0, x=0, c=0):
    return permute(array, lambda y, z, i, j: (y, z ^ zl, i ^ x, j ^ c))


def relocate(array, jump, flip_zh=False):
    if jump == 0 and not flip_zh:
        return array

    def move(y, z, x, c):
        zl = (z % 4) ^ (jump & 3)
        zh = z // 4 ^ (1 if flip_zh else 0)
        return y, zh * 4 + zl, x ^ (jump >> 2), c

    return permute(array, move)


LIGHT = pl.CostEstimate(flops=1, bytes_accessed=1, transcendentals=0)


def params(mib, *semantics):
    return pltpu.CompilerParams(
        dimension_semantics=semantics or None, vmem_limit_bytes=mib * MIB
    )


def hold_kernel(count, start, *refs):
    out, first = refs[-1], 0
    for array in refs[:count]:
        rows = array.shape[0] - start
        out[first : first + rows, :] = array[start:, :]
        first += rows


def hold(arrays, *earlier, start=0):
    rows, width = sum(a.shape[0] - start for a in arrays), arrays[0].shape[1]
    return pl.pallas_call(
        lambda *refs: hold_kernel(len(arrays), start, *refs),
        in_specs=[pl.BlockSpec(memory_space=pltpu.VMEM) for _ in arrays]
        + [pl.BlockSpec(memory_space=pl.ANY) for _ in earlier],
        out_specs=pl.BlockSpec(memory_space=pltpu.VMEM),
        out_shape=jax.ShapeDtypeStruct((rows, width), arrays[0].dtype),
        compiler_params=params(60),
        cost_estimate=LIGHT,
        name="hold",
    )(*arrays, *earlier)


def mark_kernel(tokens, meta, out):
    width = tokens.shape[1]
    out[:, :width] = tokens[...]
    left = meta[...]
    total = None
    for turn in range(3):
        part = left.astype(jnp.bfloat16).astype(jnp.float32)
        left = left - part
        part = pltpu.roll(part, 16 * turn, 1) if turn else part
        total = part if total is None else total + part
    out[:, width:] = total.astype(jnp.bfloat16)


def mark(tokens, meta):
    rows, width = tokens.shape
    return pl.pallas_call(
        mark_kernel,
        in_specs=[pl.BlockSpec(memory_space=pltpu.VMEM)] * 2,
        out_specs=pl.BlockSpec(memory_space=pltpu.VMEM),
        out_shape=jax.ShapeDtypeStruct((rows, width + 128), jnp.bfloat16),
        compiler_params=params(60),
        cost_estimate=LIGHT,
        name="mark",
    )(tokens, meta)


def choose_kernel(wanted, other, own, *refs):
    @pl.when(wanted[0] == 1)
    def _():
        refs[-1][...] = other[...]

    @pl.when(wanted[0] != 1)
    def _():
        refs[-1][...] = own[...]


def choose(wanted, other, own, *earlier):
    return pl.pallas_call(
        choose_kernel,
        in_specs=[pl.BlockSpec(memory_space=pltpu.SMEM)]
        + [pl.BlockSpec(memory_space=pltpu.VMEM) for _ in range(2)]
        + [pl.BlockSpec(memory_space=pl.ANY) for _ in earlier],
        out_specs=pl.BlockSpec(memory_space=pltpu.VMEM),
        out_shape=jax.ShapeDtypeStruct(own.shape, own.dtype),
        compiler_params=params(60),
        cost_estimate=LIGHT,
        name="choose",
    )(wanted, other, own, *earlier)


def sum_kernel(a, b, c, d, *refs):
    total = a[...].astype(jnp.float32) + b[...].astype(jnp.float32)
    total = total + c[...].astype(jnp.float32) + d[...].astype(jnp.float32)
    refs[-1][...] = total.astype(jnp.bfloat16)


def sum_blocks(blocks, *earlier):
    return pl.pallas_call(
        sum_kernel,
        in_specs=[pl.BlockSpec(memory_space=pltpu.VMEM) for _ in blocks]
        + [pl.BlockSpec(memory_space=pl.ANY) for _ in earlier],
        out_specs=pl.BlockSpec(memory_space=pltpu.VMEM),
        out_shape=jax.ShapeDtypeStruct(blocks[0].shape, jnp.bfloat16),
        compiler_params=params(60),
        cost_estimate=LIGHT,
        name="sum",
    )(*blocks, *earlier)


def plan_kernel(cap, top, ids_here, m0, m1, m2, m3, *refs):
    slot_ref, weight_ref = refs[-2:]
    rows = m0.shape[0]
    before = lax.broadcasted_iota(jnp.int32, (rows, rows), 0)
    after = lax.broadcasted_iota(jnp.int32, (rows, rows), 1)
    earlier = (before < after).astype(jnp.float32).astype(jnp.bfloat16)
    wanted = ids_here[...]
    for s, block in enumerate((m0, m1, m2, m3)):
        meta = block[...].astype(jnp.float32).T
        scale = meta[8:16, :] + meta[24:32, :] + meta[40:48, :]
        named = jnp.zeros(wanted.shape, jnp.float32)
        weight = jnp.zeros(wanted.shape, jnp.float32)
        for k in range(top):
            same = (meta[k : k + 1, :] == wanted).astype(jnp.float32)
            named = named + same
            weight = weight + same * scale[k : k + 1, :]
        rank = jnp.dot(named.astype(jnp.bfloat16), earlier, preferred_element_type=jnp.float32)
        slot = jnp.where(named > 0.5, rank + float(s * cap), -1.0)
        slot_ref[:, s * rows : (s + 1) * rows] = slot
        weight_ref[:, s * rows : (s + 1) * rows] = weight


def make_plan(cap, top, ids_here, parts, *earlier):
    rows, width = parts[0].shape
    last = width // 128 - 1
    out = jax.ShapeDtypeStruct((ids_here.shape[0], 4 * rows), jnp.float32)
    whole = pl.BlockSpec(out.shape, lambda i: (0, 0))
    return pl.pallas_call(
        lambda *refs: plan_kernel(cap, top, *refs),
        grid=(1,),
        in_specs=[pl.BlockSpec(ids_here.shape, lambda i: (0, 0))]
        + [pl.BlockSpec((rows, 128), lambda i: (0, last)) for _ in parts]
        + [pl.BlockSpec(memory_space=pl.ANY) for _ in earlier],
        out_specs=(whole, whole),
        out_shape=(out, out),
        compiler_params=params(60, "arbitrary"),
        cost_estimate=LIGHT,
        name="plan",
    )(ids_here, *parts, *earlier)


def select_kernel(scaled, slots, weights, t0, t1, t2, t3, *refs):
    *outs, pick, scale = refs
    tokens = slots.shape[1]
    block = pick.shape[0] // 8
    base = 8 if scaled else 0

    @pl.when(pl.program_id(0) == 0)
    def _():
        place = lax.broadcasted_iota(jnp.int32, (block, tokens), 0).astype(jnp.float32)
        for d in range(8):
            hit = (slots[base + d : base + d + 1, :] == place).astype(jnp.float32)
            pick[d * block : (d + 1) * block, :] = hit.astype(jnp.bfloat16)
            if scaled:
                row = jnp.sum(hit * weights[base + d : base + d + 1, :], axis=1, keepdims=True)
                scale[d * block : (d + 1) * block, :] = jnp.broadcast_to(row, (block, 128))

    source = jnp.concatenate([t0[...], t1[...], t2[...], t3[...]], axis=0)
    rows = jnp.dot(pick[...], source, preferred_element_type=jnp.float32)
    if scaled:
        rows = (rows * scale[:, 0:1]).astype(jnp.bfloat16)
        for k, out in enumerate(outs[-4:]):
            out[...] = rows[2 * k * block : 2 * (k + 1) * block, :]
    else:
        outs[-1][...] = rows.astype(jnp.bfloat16).reshape(8, block, -1)


def select_rows(scaled, cap, plan, parts, first, width, *earlier):
    slots, weights = plan
    rows = parts[0].shape[0]
    block = 4 * cap
    tile = 256 if width % 512 else 512
    offset = first // tile
    whole = pl.BlockSpec(slots.shape, lambda j: (0, 0))
    if scaled:
        out_spec = (pl.BlockSpec((2 * block, tile), lambda j: (0, j)),) * 4
        out_shape = (jax.ShapeDtypeStruct((2 * block, width), jnp.bfloat16),) * 4
    else:
        out_spec = pl.BlockSpec((8, block, tile), lambda j: (0, 0, j))
        out_shape = jax.ShapeDtypeStruct((8, block, width), jnp.bfloat16)
    return pl.pallas_call(
        lambda *refs: select_kernel(scaled, *refs),
        grid=(width // tile,),
        in_specs=[whole, whole]
        + [pl.BlockSpec((rows, tile), lambda j: (0, j + offset)) for _ in range(4)]
        + [pl.BlockSpec(memory_space=pl.ANY) for _ in earlier],
        out_specs=out_spec,
        out_shape=out_shape,
        scratch_shapes=[
            pltpu.VMEM((8 * block, 4 * rows), jnp.bfloat16),
            pltpu.VMEM((8 * block, 128), jnp.float32),
        ],
        compiler_params=params(60, "arbitrary"),
        cost_estimate=LIGHT,
        name="select_scaled" if scaled else "select",
    )(slots, weights, *parts, *earlier)


def hidden_kernel(count, where, *refs):
    xs, (gate_w, up_w), (out, held) = refs[:count], refs[count : count + 2], refs[-2:]
    step, tile = pl.program_id(0), gate_w.shape[1]
    steps, features = held.shape[0], out.shape[1]
    gate, up, first = None, None, 0
    for x in xs:
        rows = x[...].reshape(-1, x.shape[2])
        part = slice(first, first + x.shape[2])
        first += x.shape[2]
        g = jnp.dot(rows, gate_w[part, :], preferred_element_type=jnp.float32)
        u = jnp.dot(rows, up_w[part, :], preferred_element_type=jnp.float32)
        gate, up = (g, u) if gate is None else (gate + g, up + u)
    held[step] = (gate / (1.0 + jnp.exp(-gate)) * up).astype(jnp.bfloat16)

    @pl.when(step == steps - 1)
    def _():
        shard = features // (N_Y * N_ZH)
        column = lax.broadcasted_iota(jnp.int32, (tile, features), 1)
        row = lax.broadcasted_iota(jnp.int32, (tile, features), 0)
        number = column // shard
        zh = (where[1] + number % 2) % N_ZH
        y = (where[0] + number // 2) % N_Y
        origin = (y * N_ZH + zh) * shard + (column - number * shard)
        total = None
        for s in range(steps):
            move = (row + s * tile == origin).astype(jnp.float32).astype(jnp.bfloat16)
            part = jnp.dot(held[s], move, preferred_element_type=jnp.float32)
            total = part if total is None else total + part
        out[...] = total.astype(jnp.bfloat16)


def hidden_rows(where, xs, gate_weight, up_weight, earlier):
    depth, features = gate_weight.shape
    count = xs[0].shape[0] * xs[0].shape[1]
    tile = 256
    steps = features // tile
    return pl.pallas_call(
        lambda *refs: hidden_kernel(len(xs), *refs),
        grid=(steps,),
        in_specs=[pl.BlockSpec(memory_space=pltpu.SMEM)]
        + [pl.BlockSpec(x.shape, lambda j: (0, 0, 0)) for x in xs]
        + [pl.BlockSpec((depth, tile), lambda j: (0, j)) for _ in range(2)]
        + [pl.BlockSpec(memory_space=pl.ANY) for _ in earlier],
        out_specs=pl.BlockSpec((count, features), lambda j: (0, 0)),
        out_shape=jax.ShapeDtypeStruct((count, features), jnp.bfloat16),
        scratch_shapes=[pltpu.VMEM((steps, count, tile), jnp.bfloat16)],
        compiler_params=params(60, "arbitrary"),
        name="hidden",
    )(where, *xs, gate_weight, up_weight, *earlier)


def down_kernel(hidden, d0, d1, d2, d3, out):
    weight = jnp.concatenate([d0[...], d1[...], d2[...], d3[...]], axis=0)
    rows = jnp.dot(hidden[...], weight, preferred_element_type=jnp.float32)
    out[...] = rows.astype(jnp.bfloat16).reshape(out.shape)


def down_rows(hidden, downs, cap, first, width):
    tile = 256 if width % 512 else 512
    offset = first // tile
    block = 4 * cap
    return pl.pallas_call(
        down_kernel,
        grid=(width // tile,),
        in_specs=[pl.BlockSpec(hidden.shape, lambda j: (0, 0))]
        + [pl.BlockSpec((d.shape[0], tile), lambda j: (0, j + offset)) for d in downs],
        out_specs=pl.BlockSpec((8, block, tile), lambda j: (0, 0, j)),
        out_shape=jax.ShapeDtypeStruct((8, block, width), jnp.bfloat16),
        compiler_params=params(60, "arbitrary"),
        name="down",
    )(hidden, *downs)


def grad_kernel(where, hidden, *refs):
    rows, outs, turned = refs[:5], refs[-5:-1], refs[-1]
    block = rows[0].shape[0]

    @pl.when(pl.program_id(0) == 0)
    def _():
        parts = []
        for k in range(8):
            source = (where[2] + N_X - k % 4) % N_X * 2 + (where[3] + k // 4) % 2
            parts.append(hidden[pl.ds(pl.multiple_of(source * block, 16), block), :])
        turned[...] = jnp.concatenate(parts, axis=0).T

    value = jnp.concatenate([r[...] for r in rows], axis=0)
    grad = jnp.dot(turned[...], value, preferred_element_type=jnp.float32).astype(jnp.bfloat16)
    quarter = outs[0].shape[0]
    for k, out in enumerate(outs):
        out[...] = grad[k * quarter : (k + 1) * quarter, :]


def grad_blocks(where, hidden, rows, *earlier):
    width = rows[0].shape[1]
    block = rows[0].shape[0] // 2
    tile = 256 if width % 512 else 512
    quarter = hidden.shape[1] // N_Y
    spec = pl.BlockSpec((quarter, tile), lambda j: (0, j))
    out = jax.ShapeDtypeStruct((quarter, width), jnp.bfloat16)
    return pl.pallas_call(
        grad_kernel,
        grid=(width // tile,),
        in_specs=[
            pl.BlockSpec(memory_space=pltpu.SMEM),
            pl.BlockSpec(hidden.shape, lambda j: (0, 0)),
        ]
        + [pl.BlockSpec((block, tile), lambda j: (0, j)) for _ in range(4)]
        + [pl.BlockSpec((4 * block, tile), lambda j: (0, j))]
        + [pl.BlockSpec(memory_space=pl.ANY) for _ in earlier],
        out_specs=(spec,) * 4,
        out_shape=(out,) * 4,
        scratch_shapes=[pltpu.VMEM(hidden.shape[::-1], jnp.bfloat16)],
        compiler_params=params(60, "arbitrary"),
        name="grad",
    )(where, hidden, *rows, *earlier)


def combine_kernel(slots, weights, rows, *refs):
    *outs, high, low = refs[-6:]
    dests, block, width = rows.shape
    tokens = slots.shape[1]

    @pl.when(pl.program_id(0) == 0)
    def _():
        place = lax.broadcasted_iota(jnp.int32, (block, tokens), 0).astype(jnp.float32)
        picked = []
        for d in range(dests):
            hit = (slots[d : d + 1, :] == place).astype(jnp.float32)
            picked.append(hit * weights[d : d + 1, :])
        pick = jnp.concatenate(picked, axis=0).T
        coarse = pick.astype(jnp.bfloat16)
        high[...] = coarse
        low[...] = (pick - coarse.astype(jnp.float32)).astype(jnp.bfloat16)

    value = rows[...].reshape(-1, width)
    total = jnp.dot(high[...], value, preferred_element_type=jnp.float32)
    total = total + jnp.dot(low[...], value, preferred_element_type=jnp.float32)
    count = outs[0].shape[0]
    for s, out in enumerate(outs):
        out[...] = total[s * count : (s + 1) * count, :].astype(out.dtype)


def combine_rows(plan, rows, *earlier):
    slots, weights = plan
    width = rows.shape[2]
    tile = 256 if width % 512 else 512
    count = slots.shape[1] // 4
    whole = pl.BlockSpec((8, slots.shape[1]), lambda j: (0, 0))
    spec = pl.BlockSpec((count, tile), lambda j: (0, j))
    return pl.pallas_call(
        combine_kernel,
        grid=(width // tile,),
        in_specs=[whole, whole, pl.BlockSpec((*rows.shape[:2], tile), lambda j: (0, 0, j))]
        + [pl.BlockSpec(memory_space=pl.ANY) for _ in earlier],
        out_specs=(spec,) * 4,
        out_shape=tuple(
            jax.ShapeDtypeStruct((count, width), t)
            for t in (jnp.float32, jnp.bfloat16, jnp.bfloat16, jnp.bfloat16)
        ),
        scratch_shapes=[
            pltpu.VMEM((slots.shape[1], rows.shape[0] * rows.shape[1]), jnp.bfloat16)
            for _ in range(2)
        ],
        compiler_params=params(60, "arbitrary"),
        name="combine",
    )(slots, weights, rows, *earlier)


def plane_permute(blocks):
    out = [blocks[0]]
    for k in range(1, N_X):
        out.append(permute(blocks[k], lambda y, z, x, c, k=k: (y, z, x + k, c)))
    return out


def core_permute(blocks, *earlier):
    passed = hold(blocks, *earlier, start=blocks[0].shape[0] // 2)
    return permute(passed, lambda y, z, x, c: (y, z, x, c + 1))


def plane_exchange(rows):
    return lax.all_to_all(rows, ("x", "c"), split_axis=0, concat_axis=0, tiled=True)


def total_kernel(own, near, other, *refs):
    total = own[...] + near[...].astype(jnp.float32) + other[...].astype(jnp.float32)
    refs[-1][...] = total.astype(jnp.bfloat16)


def z_return(own, near, other, far_back, *earlier):
    step = far_back.astype(jnp.float32) + near.astype(jnp.float32)
    from_near = z_down(step.astype(jnp.bfloat16))
    from_other = z_up(other)
    return pl.pallas_call(
        total_kernel,
        in_specs=[pl.BlockSpec(memory_space=pltpu.VMEM) for _ in range(3)]
        + [pl.BlockSpec(memory_space=pl.ANY) for _ in earlier],
        out_specs=pl.BlockSpec(memory_space=pltpu.VMEM),
        out_shape=jax.ShapeDtypeStruct(own.shape, jnp.bfloat16),
        compiler_params=params(60),
        cost_estimate=LIGHT,
        name="total",
    )(own, from_near, from_other, *earlier)


def y_move(array, k):
    return permute(array, lambda y, z, x, c: (y + k, z, x, c))


def adam(grad, weight, first, second):
    weight_old = weight.astype(jnp.float32)
    moment_one = first_decay_rate * first.astype(jnp.float32) + (1.0 - first_decay_rate) * grad
    moment_two = beta_two * second.astype(jnp.float32) + (1.0 - beta_two) * grad * grad
    updated = weight_old - learn_rate * moment_one / (jnp.sqrt(moment_two) + adam_eps)
    return tuple(v.astype(jnp.bfloat16)[None] for v in (updated, moment_one, moment_two))


def local(
    tokens,
    expert_ids,
    route_weight,
    placement,
    swap_mask,
    gate_weight,
    up_weight,
    down_weight,
    first_moment,
    second_moment,
    out_grad,
):
    tok_rows, top = expert_ids.shape
    width = tokens.shape[1]
    experts = placement.shape[0]
    cap = tok_rows * top * 7 // (6 * experts)
    jumps = range(2 ** (SWAP_BITS - 1))
    jump = jnp.clip(swap_mask[0] // 2, 0, len(jumps) - 1)
    bits = [swap_mask // 2**bit % 2 for bit in range(SWAP_BITS)]

    where = [lax.axis_index(a) for a in ("y", "zh", "x", "c")]
    where = jnp.stack(where).astype(jnp.int32)

    dest = jnp.arange(8, dtype=jnp.int32)
    ring = (where[2] + dest // 2) % N_X * 2 + (where[3] + dest) % 2
    dest = jnp.concatenate([dest, ring])
    held_at = (dest // 2) * 8 + lax.axis_index("zl") * 2 + dest % 2
    ids = jnp.arange(experts, dtype=jnp.int32)
    here = jnp.sum(jnp.where(placement[None, :] == held_at[:, None], ids[None, :], 0), axis=1)
    here = jnp.broadcast_to(here.astype(jnp.float32)[:, None], (16, tok_rows))
    numbers = jnp.pad(expert_ids.astype(jnp.float32), ((0, 0), (0, 128 - top)))
    meta = numbers + jnp.pad(route_weight, ((0, 0), (8, 120 - top)))

    x_parts = z_gather(mark(tokens, meta))
    state = hold((down_weight[0], first_moment[0], second_moment[0]))
    far_state = swap(state, x=1)
    plan = make_plan(cap, top, here, x_parts, far_state)
    x_send = select_rows(False, cap, plan, x_parts, 0, width)
    x_rows = plane_exchange(x_send)
    g_parts = z_gather(hold((out_grad,), plan[0]))
    state = choose(bits[3], far_state, state, x_send)
    state_cores = choose(bits[0], swap(state, c=1), state, *g_parts[2:])
    state_far = swap(state_cores, zl=2)

    g_send = select_rows(True, cap, plan, g_parts, 0, width, x_rows, state_cores)
    g_rows = plane_permute(g_send)

    down = hold((down_weight[0],), plan[0])
    partner = permute(down, lambda y, z, x, c: (y, z + 4, x, c))
    pair = jnp.concatenate([down, partner], axis=0)
    downs = (pair, y_move(pair, -1), y_move(pair, -2), y_move(pair, 1))

    hidden = hidden_rows(where, [x_rows], gate_weight[0], up_weight[0], g_send[3:])
    r_send = down_rows(hidden, downs, cap, 0, width)
    returned = plane_exchange(r_send)
    state_far = choose(bits[2], state_far, state_cores, r_send)
    state_near = swap(state_far, zl=1)

    g_rows = (*g_rows, core_permute(g_rows, state_far))
    blocks = grad_blocks(where, hidden, g_rows)
    blocks = [blocks[0]] + [y_move(blocks[k], k) for k in (1, 2, 3)]
    combined = combine_rows(plan, returned, blocks[1])
    far_back = z_down(combined[3])
    total = sum_blocks(blocks, far_back)
    other = swap(total, c=1)
    halves = [jnp.where(bits[0] == 1, o, t) for o, t in zip(jnp.split(other, 2), jnp.split(total, 2))]
    mine, theirs = lax.switch(
        jump,
        [lambda a, b, m=m: (relocate(a, m), relocate(b, m, True)) for m in jumps],
        *halves,
    )
    grad = mine.astype(jnp.float32) + theirs.astype(jnp.float32)
    state = jnp.where(bits[1] == 1, state_near, state_far)
    new_state = adam(grad, *jnp.split(state, 3, axis=0))

    layer_out = z_return(*combined[:3], far_back, theirs)
    return (layer_out, *new_state)


def solution(mesh):
    fine = Mesh(mesh.devices.reshape(N_Y, N_ZH, N_X, N_ZL, N_C), AXES)
    dp, expert = ("y", "zh"), ("x", "zl", "c")
    batch, weight, state = P(dp + expert, None), P(expert, None, None), P(expert, dp, None)
    return jax.shard_map(
        local,
        mesh=fine,
        in_specs=(batch,) * 3 + (P(), P()) + (weight,) * 2 + (state,) * 3 + (batch,),
        out_specs=(batch, state, state, state),
        check_vma=False,
    )
```
